32 devices in a mesh: img: 16 (over z, y, core), txt: 2 (over x).
Axes of the slice: x: 2, y: 2, z: 4, core: 2. Of those that a mesh axis runs over, the one named last changes fastest.
Arguments:
- tokens: bfloat16 [4096, 1536], P('img'), may hold values from -6 to 6
- cotangent: bfloat16 [4096, 1536], P('img'), may hold values from -6 to 6
- text_states: bfloat16 [256, 4096], P('img'), may hold values from -6 to 6
- conditions: bfloat16 [16, 1024], replicated, may hold values from -6 to 6
- image_sides: int32 [16, 2], replicated, may hold values from 16 to 32, as said below
- master: float32 [16, 2, 1572864], P('img', 'txt')
- moment_one: float32 [16, 2, 1572864], P('img', 'txt'), may hold values from -0.0008457003 to 0.0008457003
- moment_two: float32 [16, 2, 1572864], P('img', 'txt'), may hold values from 1.9866917e-08 to 7.946767e-08
- average: float32 [16, 2, 1572864], P('img', 'txt')
- small_master: float32 [3288], replicated
- small_one: float32 [3288], replicated, may hold values from -0.0033828013 to 0.0033828013
- small_two: float32 [3288], replicated, may hold values from 3.1787067e-07 to 1.2714827e-06
- small_average: float32 [3288], replicated
Outputs:
- block_out: float32 [4096, 1536], P('img')
- d_tokens: float32 [4096, 1536], P('img')
- grad_square: float32 [], replicated
- moment_one_new: float32 [16, 2, 1572864], P('img', 'txt')
- moment_two_new: float32 [16, 2, 1572864], P('img', 'txt')
- master_new: float32 [16, 2, 1572864], P('img', 'txt')
- average_new: float32 [16, 2, 1572864], P('img', 'txt')
- master_low: bfloat16 [16, 2, 1572864], P('img', 'txt')
- small_one_new: float32 [3288], replicated
- small_two_new: float32 [3288], replicated
- small_new: float32 [3288], replicated
- small_average_new: float32 [3288], replicated
The draws below stay inside these ranges and needn't reach their ends.
Inputs may be any that keep to these rules, and one draw needn't show every extreme that they name: `image_sides`: row s gives image s's height and width in patches; its h * (w + 1) tokens follow those of image s - 1 in the packed rows; one of the first two images is 32 by 32; the images together hold 4096 tokens or more, and the rows after the last token are unused.
All inputs are finite; a program needn't handle non-finite values.
Results may differ from the reference program's by a relative error of at most 0.008.
The reference program's roundings to bfloat16 on the way count: a program that leaves them out, or rounds other values in their place, can miss the bound.
Values may be sent and summed in bfloat16 or wider, within the bound.
No kernel may reach another device: no remote copies, remote signals or barrier semaphores. Data moves between devices by JAX's collectives and lax.ppermute only.
A program may use at most 448 MiB of HBM per device.

```python
import math
import jax
import jax.numpy as jnp
from jax import lax

D = 1536
HEADS = 24
HD = 64
FF = 4096
TXT_D = 4096
COND = 1024
TXT_LEN = 256
SIDE_MIN = 16
SIDE_MAX = 32
STEP = 10
TOKENS = 4096
SAMPLES = 16
SHARD = 1572864
SMALLP = 3288
PARAMS_ALL = 50334936
N_IMG = 16
N_TXT = 2


def segment_scales():
    half_d = D // N_TXT
    item_sizes = [D * 2 * (FF // N_TXT), FF // N_TXT * D, D * 3 * half_d, TXT_D * 2 * half_d, half_d * D, COND * 6 * half_d]
    fan_ins = [D * 1.0, FF * 1.0, D * 1.0, TXT_D * 1.0, D / 16.0, COND * 1.0]
    pieces = [jnp.full((item_count // N_IMG,), fan_in ** (-0.5), jnp.float32) for item_count, fan_in in zip(item_sizes, fan_ins)]
    return jnp.concatenate(pieces)


def flat_weights(key):
    scales = segment_scales()
    base = jnp.clip(jax.random.normal(key, (N_IMG, N_TXT, SHARD), jnp.float32), -4.0, 4.0)
    return base * scales[None, None, :]


def small_values(key):
    keys_split = jax.random.split(key, 4)
    ramp = 0.6 * 3.0 ** (jnp.arange(D, dtype=jnp.float32) / D)
    jitter = jax.random.uniform(keys_split[0], (2, D), jnp.float32, 0.8, 1.25)
    gains = (ramp[None, :] * jitter).reshape(2 * D)
    head_gains = jax.random.uniform(keys_split[1], (3 * HD,), jnp.float32, 0.7, 1.4)
    signs = jnp.where(jax.random.bernoulli(keys_split[3], 0.5, (HEADS,)), 1.0, -1.0)
    gates = jax.random.uniform(keys_split[2], (HEADS,), jnp.float32, 0.4, 1.4) * signs
    return jnp.concatenate([gains, head_gains, gates])


def draw_master(key, part):
    key = jax.random.fold_in(key, 11)
    return flat_weights(key)


def draw_average(key, part):
    key = jax.random.fold_in(key, 12)
    return flat_weights(key)


def draw_small_master(key, part):
    key = jax.random.fold_in(key, 21)
    return small_values(key)


def draw_small_average(key, part):
    key = jax.random.fold_in(key, 22)
    value_key, factor_key = jax.random.split(key)
    factors = jax.random.uniform(factor_key, (SMALLP,), jnp.float32, 0.4, 1.8)
    return small_values(value_key) * factors


def draw_image_sides(key, part):
    key = jax.random.fold_in(key, 31)
    first_key, second_key = jax.random.split(key)
    sides_drawn = jax.random.randint(first_key, (SAMPLES, 2), SIDE_MIN, SIDE_MAX + 1, dtype=jnp.int32)
    place = jax.random.randint(second_key, (), 0, 2, dtype=jnp.int32)
    row_index = jnp.arange(SAMPLES, dtype=jnp.int32)[:, None]
    return jnp.where(row_index == place, SIDE_MAX, sides_drawn).astype(jnp.int32)


def shard_levels(own_key, dims, cuts, least, high):
    def one(position, parts):
        steps = jax.random.uniform(jax.random.fold_in(jax.random.fold_in(own_key, 6), position), (parts,), jnp.float32, least / len(cuts), high / len(cuts))
        return jnp.repeat(jnp.exp(steps), dims[position] // parts).reshape((-1,) + (1,) * (len(dims) - position - 1))

    loudness = one(*cuts[0])
    for cut in cuts[1:]:
        loudness = loudness * one(*cut)
    return loudness


def noise(own_key, extent, deviation, bound, cuts=(), held_as=jnp.bfloat16):
    factor_of = shard_levels(own_key, extent, cuts, -0.22, 0.18) if cuts else 1.0
    entries = jax.random.normal(own_key, extent, jnp.float32) * deviation * factor_of
    return jnp.minimum(jnp.maximum(entries, -bound), bound).astype(held_as)


def setup_inputs(seed: int = 0) -> dict:
    key_list = jax.random.split(jax.random.key(seed), 14)
    return {
        "tokens": noise(key_list[0], (TOKENS, D), 1.0, 6.0, ((0, 16),)),
        "cotangent": noise(key_list[1], (TOKENS, D), 1.0, 6.0, ((0, 16),)),
        "text_states": noise(key_list[2], (TXT_LEN, TXT_D), 1.0, 6.0, ((0, 16),)),
        "conditions": noise(key_list[3], (SAMPLES, COND), 1.0, 6.0),
        "image_sides": draw_image_sides(jax.random.fold_in(key_list[13], 71), 0),
        "master": draw_master(jax.random.fold_in(key_list[13], 71), 0),
        "moment_one": noise(key_list[6], (N_IMG, N_TXT, SHARD), (1.0 / PARAMS_ALL ** 0.5), 0.0008457003, ((0, 16), (1, 2)), jnp.float32),
        "moment_two": jnp.clip(jnp.exp(math.log(7.946766800159821e-08) - 1.3862944 * jax.random.uniform(key_list[7], (N_IMG, N_TXT, SHARD), jnp.float32) ** shard_levels(key_list[7], (N_IMG, N_TXT, SHARD), ((0, 16), (1, 2)), -0.2, 0.2)), 1.9866917000399553e-08, 7.946766800159821e-08),
        "average": draw_average(jax.random.fold_in(key_list[13], 71), 0),
        "small_master": draw_small_master(jax.random.fold_in(key_list[13], 71), 0),
        "small_one": noise(key_list[10], (SMALLP,), (4.0 / PARAMS_ALL ** 0.5), 0.0033828013, (), jnp.float32),
        "small_two": jnp.clip(jnp.exp(jax.random.uniform(key_list[11], (SMALLP,), jnp.float32, math.log(3.1787067200639285e-07), math.log(1.2714826880255714e-06))), 3.1787067200639285e-07, 1.2714826880255714e-06),
        "small_average": draw_small_average(jax.random.fold_in(key_list[13], 71), 0),
    }


@jax.custom_vjp
def low(v):
    return lax.optimization_barrier(v.astype(jnp.bfloat16)).astype(jnp.float32)

@jax.custom_vjp
def low_back(v):
    return v

def low_keep(v):
    return (low(v), None)

def low_pass(kept, grad):
    return (grad,)

def back_keep(v):
    return (v, None)

def back_low(kept, grad):
    return (low(grad),)
low.defvjp(low_keep, low_pass)
low_back.defvjp(back_keep, back_low)
HIGH = lax.Precision.HIGHEST
EPS_NORM = 1e-06
MAX_NORM = 1.0
BETA_ONE = 0.5
BETA_TWO = 0.5
RATE_MATRIX = 0.01
RATE_SMALL = 0.1
DECAY_WEIGHT = 0.01
ADAM_EPS = 1e-08
EMA_DECAY = 0.8

def segment_table(n_txt):
    half_d = D // n_txt
    return [((D, 2, FF // n_txt), 2), ((FF // n_txt, D), 0), ((D, 3, half_d), 2), ((TXT_D, 2, half_d), 2), ((half_d, D), 0), ((COND, 6, half_d), 2)]

def token_places(row_index, image_sides):
    heights = image_sides[:, 0]
    widths = image_sides[:, 1]
    lengths = heights * (widths + 1)
    sample_ends = jnp.cumsum(lengths, dtype=jnp.int32)
    starts = sample_ends - lengths
    sample_ids = lax.optimization_barrier(jnp.sum((sample_ends[None, :] <= row_index[:, None]).astype(jnp.int32), axis=1, dtype=jnp.int32))
    matched = jnp.arange(image_sides.shape[0], dtype=jnp.int32)[None, :] == sample_ids[:, None]
    first_row = lax.optimization_barrier(jnp.sum(jnp.where(matched, starts[None, :], 0), axis=1, dtype=jnp.int32))
    row_width = lax.optimization_barrier(jnp.sum(jnp.where(matched, widths[None, :] + 1, 0), axis=1, dtype=jnp.int32))
    row_width = jnp.maximum(row_width, 1)
    offset = row_index - first_row
    return (sample_ids, offset // row_width, offset % row_width)

def rotate(tensor, row_pos, col_pos, direction):
    head_dim = tensor.shape[-1]
    quarter = head_dim // 4
    frequency = 10000.0 ** (-jnp.arange(quarter, dtype=jnp.float32) / quarter)
    angles = jnp.concatenate([row_pos.astype(jnp.float32)[:, None] * frequency[None, :], col_pos.astype(jnp.float32)[:, None] * frequency[None, :]], axis=1)
    cosine = jnp.cos(angles)[:, None, :]
    sine_part = direction * jnp.sin(angles)[:, None, :]
    first_part = tensor[..., :head_dim // 2]
    second_part = tensor[..., head_dim // 2:]
    return jnp.concatenate([first_part * cosine - second_part * sine_part, first_part * sine_part + second_part * cosine], axis=-1)

def rms_norm(values):
    return values * lax.rsqrt(lax.optimization_barrier(jnp.mean(values * values, axis=-1, keepdims=True)) + EPS_NORM)

def adam_update(gradient, first_moment, second_moment, weight, moving, rate, decay):
    first_new = BETA_ONE * first_moment + (1.0 - BETA_ONE) * gradient
    second_new = BETA_TWO * second_moment + (1.0 - BETA_TWO) * gradient * gradient
    corr_one = 1.0 - BETA_ONE ** STEP
    corr_two = 1.0 - BETA_TWO ** STEP
    step_dir = first_new / corr_one / (jnp.sqrt(second_new / corr_two) + ADAM_EPS)
    weight_new = weight - rate * (step_dir + decay * weight)
    moving_new = EMA_DECAY * moving + (1.0 - EMA_DECAY) * weight_new
    return (first_new, second_new, weight_new, moving_new)

def unpack_weights(master):
    layout_table = segment_table(N_TXT)
    offset = 0
    result = []
    for shape_dims, join_axis in layout_table:
        item_count = math.prod(shape_dims) // N_IMG
        halves = [master[:, txt_half, offset:offset + item_count].reshape(shape_dims) for txt_half in range(N_TXT)]
        result.append(jnp.concatenate(halves, axis=join_axis))
        offset += item_count
    return result

def pack_grads(gradients):
    layout_table = segment_table(N_TXT)
    pieces = []
    for (shape_dims, join_axis), gradient in zip(layout_table, gradients):
        halves = jnp.split(gradient, N_TXT, axis=join_axis)
        pieces.append(jnp.stack([piece_part.reshape(N_IMG, -1) for piece_part in halves], axis=1))
    return jnp.concatenate(pieces, axis=2)

def attention(queries, key_rows, value_rows, sample_ids, text_keys, text_values):
    reach_rows = SIDE_MAX * (SIDE_MAX + 1)
    block_rows = math.gcd(TOKENS, 512)
    padding = ((reach_rows, reach_rows), (0, 0), (0, 0))
    key_padded = jnp.pad(key_rows, padding)
    value_padded = jnp.pad(value_rows, padding)
    ids_padded = jnp.pad(sample_ids, (reach_rows, reach_rows), constant_values=-1)
    score_scale = HD ** (-0.5)
    window = block_rows + 2 * reach_rows

    def one_block(start):
        query_block = lax.dynamic_slice_in_dim(queries, start, block_rows, 0)
        query_ids = lax.dynamic_slice_in_dim(sample_ids, start, block_rows, 0)
        key_block = lax.dynamic_slice_in_dim(key_padded, start, window, 0)
        value_block = lax.dynamic_slice_in_dim(value_padded, start, window, 0)
        key_ids = lax.dynamic_slice_in_dim(ids_padded, start, window, 0)
        raw_scores = low_back(jnp.einsum('qhd,khd->hqk', query_block, key_block, precision=HIGH))
        same_sample = (query_ids[:, None] == key_ids[None, :])[None]
        scores = jnp.where(same_sample, raw_scores * score_scale, -1e+30)
        self_part = jnp.einsum('hqk,khd->qhd', low(jax.nn.softmax(scores, axis=-1)), value_block, precision=HIGH)
        cross_raw = low_back(jnp.einsum('qhd,khd->hqk', query_block, text_keys, precision=HIGH))
        cross_weights = low(jax.nn.softmax(cross_raw * score_scale, axis=-1))
        cross_part = jnp.einsum('hqk,khd->qhd', cross_weights, text_values, precision=HIGH)
        return (self_part, cross_part)
    starts = jnp.arange(TOKENS // block_rows, dtype=jnp.int32) * block_rows
    self_out, cross_out = lax.map(jax.checkpoint(one_block), starts)
    return (self_out.reshape(TOKENS, HEADS, HD), cross_out.reshape(TOKENS, HEADS, HD))

def forward(x_float, weight_list, small_params, text_float, cond_float, sample_ids, row_pos, col_pos):
    w_updown, w_down, w_project, w_text, w_output, w_modulate = weight_list
    gain_attn = small_params[:D]
    gain_ffn = small_params[D:2 * D]
    gain_query = small_params[2 * D:2 * D + HD]
    gain_key = small_params[2 * D + HD:2 * D + 2 * HD]
    gain_text = small_params[2 * D + 2 * HD:2 * D + 3 * HD]
    gate_heads = small_params[2 * D + 3 * HD:]
    modulation = low(jnp.dot(low(jax.nn.silu(cond_float)), w_modulate.reshape(COND, 6 * D), precision=HIGH))
    per_token = modulation.reshape(SAMPLES, 6, D)[sample_ids]
    shift_one = per_token[:, 0]
    scale_one = per_token[:, 1]
    gate_one = per_token[:, 2]
    shift_two = per_token[:, 3]
    scale_two = per_token[:, 4]
    gate_two = per_token[:, 5]
    attn_in = rms_norm(x_float) * gain_attn * (1.0 + scale_one) + shift_one
    projected = low_back(jnp.einsum('td,dcn->tcn', low(attn_in), w_project, precision=HIGH))
    heads_shape = (TOKENS, HEADS, HD)
    queries = low(rotate(rms_norm(projected[:, 0].reshape(heads_shape)) * gain_query, row_pos, col_pos, 1.0))
    key_rows = low(rotate(rms_norm(projected[:, 1].reshape(heads_shape)) * gain_key, row_pos, col_pos, 1.0))
    value_rows = low(projected[:, 2].reshape(heads_shape))
    text_proj = low_back(jnp.einsum('sd,dcn->scn', text_float, w_text, precision=HIGH))
    text_keys = low(rms_norm(text_proj[:, 0].reshape(TXT_LEN, HEADS, HD)) * gain_text)
    text_values = low(text_proj[:, 1].reshape(TXT_LEN, HEADS, HD))
    self_out, cross_out = attention(queries, key_rows, value_rows, sample_ids, text_keys, text_values)
    mixed = low_back(self_out) + jnp.tanh(gate_heads)[None, :, None] * low_back(cross_out)
    attn_out = low_back(jnp.dot(low(mixed.reshape(TOKENS, D)), w_output, precision=HIGH))
    hidden = x_float + gate_one * attn_out
    ffn_in = rms_norm(hidden) * gain_ffn * (1.0 + scale_two) + shift_two
    gate_up = low_back(jnp.einsum('td,dcf->tcf', low(ffn_in), w_updown, precision=HIGH))
    hidden_units = jax.nn.silu(gate_up[:, 0]) * gate_up[:, 1]
    branch = low_back(jnp.dot(low(hidden_units), w_down, precision=HIGH))
    return hidden + gate_two * branch

def reference(tokens, cotangent, text_states, conditions, image_sides, master, moment_one, moment_two, average, small_master, small_one, small_two, small_average):
    row_index = jnp.arange(TOKENS, dtype=jnp.int32)
    sample_ids, row_pos, col_pos = token_places(row_index, image_sides)
    weights_low = unpack_weights(low(master))
    text_float = text_states.astype(jnp.float32)
    cond_float = conditions.astype(jnp.float32)

    def block_fn(x_float, weight_list, small_params):
        return forward(x_float, weight_list, small_params, text_float, cond_float, sample_ids, row_pos, col_pos)
    block_out, pullback = jax.vjp(block_fn, tokens.astype(jnp.float32), weights_low, small_master)
    d_tokens, d_weights, d_small = pullback(cotangent.astype(jnp.float32))
    grads_big = pack_grads(d_weights)
    grad_square = jnp.sum(grads_big * grads_big) + jnp.sum(d_small * d_small)
    clip_factor = MAX_NORM / jnp.maximum(jnp.sqrt(grad_square), MAX_NORM)
    one_new, two_new, master_new, average_new = adam_update(grads_big * clip_factor, moment_one, moment_two, master, average, RATE_MATRIX, DECAY_WEIGHT)
    small_one_new, small_two_new, small_new, small_average_new = adam_update(d_small * clip_factor, small_one, small_two, small_master, small_average, RATE_SMALL, 0.0)
    return (block_out, d_tokens, grad_square, one_new, two_new, master_new, average_new, master_new.astype(jnp.bfloat16), small_one_new, small_two_new, small_new, small_average_new)
```

```python
import functools
import math

import jax
import jax.numpy as jnp
from jax import lax
from jax.experimental import pallas as pl
from jax.experimental.pallas import tpu as pltpu
from jax.sharding import PartitionSpec as P

D = 1536
HEADS = 24
HD = 64
FF = 4096
TXT_D = 4096
COND = 1024
SIDE_MAX = 32
STEP = 10

HIGH = lax.Precision.HIGHEST
EPS_NORM = 1e-06
MAX_NORM = 1.0
BETA_ONE = 0.5
BETA_TWO = 0.5
RATE_MATRIX = 0.01
RATE_SMALL = 0.1
DECAY_WEIGHT = 0.01
ADAM_EPS = 1e-08
EMA_DECAY = 0.8

LANES = 128
EDGE = 128
PACK = 16
PIECES = 14
MASKED = -1e30
VMEM = 48 * 1024 * 1024

bf16 = jnp.bfloat16
f32 = jnp.float32


def mm(a, b, on_a, on_b):
    return lax.dot_general(a, b, (((on_a,), (on_b,)), ((), ())), preferred_element_type=f32)


def lane_index(rows):
    return lax.broadcasted_iota(jnp.int32, (rows, LANES), 1)


def head_sum(values):
    low = lane_index(values.shape[0]) < HD
    first = jnp.sum(jnp.where(low, values, 0.0), axis=1, keepdims=True)
    second = jnp.sum(jnp.where(low, 0.0, values), axis=1, keepdims=True)
    return jnp.where(low, first, second)


def swap_halves(values):
    first = lane_index(values.shape[0]) % HD < HD // 2
    return jnp.where(
        first, pltpu.roll(values, LANES - HD // 2, 1), pltpu.roll(values, HD // 2, 1)
    )


def two_heads(pair):
    low = lane_index(pair.shape[0]) < HD
    zero = jnp.zeros_like(pair)
    return jnp.concatenate([jnp.where(low, pair, zero), jnp.where(low, zero, pair)], axis=0)


def one_pair(stacked):
    rows = stacked.shape[0] // 2
    low = lane_index(rows) < HD
    return jnp.where(low, stacked[:rows], stacked[rows:])


def columns_of(spread):
    return jnp.concatenate([spread[:, :1], spread[:, HD : HD + 1]], axis=0)


def norm_rope(raw, gain, cosine, sine):
    inverse = lax.rsqrt(head_sum(raw * raw) * (1.0 / HD) + EPS_NORM)
    scaled = raw * inverse * gain
    return scaled * cosine + swap_halves(scaled) * sine


def norm_rope_back(raw, gain, cosine, sine, d_out):
    inverse = lax.rsqrt(head_sum(raw * raw) * (1.0 / HD) + EPS_NORM)
    normed = raw * inverse
    d_scaled = d_out * cosine - swap_halves(d_out) * sine
    d_gain = jnp.sum(d_scaled * normed, axis=0, keepdims=True)
    d_normed = d_scaled * gain
    d_raw = inverse * (d_normed - normed * (head_sum(d_normed * normed) * (1.0 / HD)))
    return d_raw, d_gain


def split_three(values):
    high = values.astype(bf16)
    rest = values - high.astype(f32)
    middle = rest.astype(bf16)
    last = (rest - middle.astype(f32)).astype(bf16)
    return jnp.concatenate([high, middle, last], axis=1)


def joined(packed, rows):
    wide = packed.astype(f32)
    return wide[:, :rows] + wide[:, rows : 2 * rows] + wide[:, 2 * rows : 3 * rows]


def put_row(table, index, row):
    at = lax.broadcasted_iota(jnp.int32, table.shape, 0) == index
    return jnp.where(at, row, table)


def take_row(table, index):
    at = lax.broadcasted_iota(jnp.int32, table.shape, 0) == index
    return jnp.sum(jnp.where(at, table, 0.0), axis=0, keepdims=True)


def as_row(column):
    return jnp.broadcast_to(column, (column.shape[0], LANES)).T[:1]


def project_kernel(a_ref, wq_ref, wk_ref, wv_ref, gq_ref, gk_ref, cos_ref, sin_ref, q_ref, kv_ref, raw_ref):
    a = a_ref[...]
    cosine, sine = cos_ref[...], sin_ref[...]
    raw_q = mm(a, wq_ref[...], 1, 0)
    raw_k = mm(a, wk_ref[...], 1, 0)
    raw_ref[0] = raw_q
    raw_ref[1] = raw_k
    q_ref[...] = norm_rope(raw_q, gq_ref[...], cosine, sine).astype(bf16) * jnp.asarray(HD**-0.5, bf16)
    kv_ref[0] = norm_rope(raw_k, gk_ref[...], cosine, sine).astype(bf16)
    kv_ref[1] = mm(a, wv_ref[...], 1, 0).astype(bf16)


def piece_views(piece_refs, counts, per):
    views = []
    for ref, count in zip(piece_refs, counts):
        for at in range(count):
            views.append((ref, at * per))
    return views


def attend_kernel(counts, tok, flag_ref, q_ref, own_ids_ref, ids_ref, tk_ref, tv_ref, gate_ref, *rest):
    pieces = piece_views(rest[: len(counts)], counts, 2)
    mixed_ref, self_ref, cross_ref, lse_self_ref, lse_cross_ref, pack_ref = rest[len(counts) : len(counts) + 6]
    scores_ref, most_ref, total_ref, acc_ref, table_ref = rest[len(counts) + 6 :]
    step = pl.program_id(0)
    own_ids = own_ids_ref[...]
    q_pair = q_ref[...]
    q_two = two_heads(q_pair)
    own_two = jnp.concatenate([own_ids, own_ids], axis=0)
    most_ref[...] = jnp.full(most_ref.shape, MASKED, f32)
    total_ref[...] = jnp.zeros(total_ref.shape, f32)
    acc_ref[...] = jnp.zeros(acc_ref.shape, f32)
    for slot, (ref, at) in enumerate(pieces):
        rows = ref.shape[1]

        @pl.when(flag_ref[slot] > 0)
        def _(slot=slot, ref=ref, at=at, rows=rows):
            scores = mm(q_two, ref[at], 1, 1)
            scores = jnp.where(own_two == ids_ref[slot : slot + 1, :rows], scores, MASKED)
            scores_ref[slot, :, :rows] = scores
            most = most_ref[...]
            for part in range(rows // LANES):
                most = jnp.maximum(most, scores[:, part * LANES : (part + 1) * LANES])
            most_ref[...] = most

    row_most = jnp.max(most_ref[...], axis=1, keepdims=True)
    for slot, (ref, at) in enumerate(pieces):
        rows = ref.shape[1]

        @pl.when(flag_ref[slot] > 0)
        def _(slot=slot, ref=ref, at=at, rows=rows):
            weights = jnp.exp(scores_ref[slot, :, :rows] - row_most)
            total = total_ref[...]
            for part in range(rows // LANES):
                total = total + weights[:, part * LANES : (part + 1) * LANES]
            total_ref[...] = total
            acc_ref[...] += mm(weights.astype(bf16), ref[at + 1], 1, 0)

    row_total = jnp.sum(total_ref[...], axis=1, keepdims=True)
    self_out = one_pair(acc_ref[...] / row_total)
    lse_self = row_most + jnp.log(row_total)

    cross_scores = mm(q_two, tk_ref[...], 1, 1)
    cross_most = jnp.max(cross_scores, axis=1, keepdims=True)
    cross_weights = jnp.exp(cross_scores - cross_most)
    cross_total = jnp.sum(cross_weights, axis=1, keepdims=True)
    cross_out = one_pair(mm(cross_weights.astype(bf16), tv_ref[...], 1, 0) / cross_total)
    lse_cross = cross_most + jnp.log(cross_total)

    self_ref[...] = self_out
    cross_ref[...] = cross_out
    mixed_ref[...] = (self_out + gate_ref[...] * cross_out).astype(bf16)
    spread = (tok, LANES)
    low = lane_index(tok) < HD
    lse_self_ref[...] = jnp.where(
        low, jnp.broadcast_to(lse_self[:tok], spread), jnp.broadcast_to(lse_self[tok:], spread)
    )
    lse_cross_ref[...] = jnp.where(
        low, jnp.broadcast_to(lse_cross[:tok], spread), jnp.broadcast_to(lse_cross[tok:], spread)
    )

    @pl.when(step == 0)
    def _():
        table_ref[...] = jnp.zeros(table_ref.shape, f32)

    table = put_row(table_ref[...], 2 * step, as_row(lse_self[:tok]))
    table = put_row(table, 2 * step + 1, as_row(lse_self[tok:]))
    table_ref[...] = table
    pack_ref[0, :tok, pl.ds(pl.multiple_of(step * LANES, LANES), LANES)] = q_pair

    @pl.when(step == pl.num_programs(0) - 1)
    def _():
        pack_ref[0, tok:, :] = split_three(table_ref[...])


def mixed_back_kernel(tok, d_attn_ref, w_ref, self_ref, cross_ref, gate_ref, pack_ref, d_cross_ref, d_gate_ref, table_ref):
    step = pl.program_id(0)
    d_mixed = mm(d_attn_ref[...], w_ref[...], 1, 1)
    d_self = d_mixed.astype(bf16)
    d_cross_ref[...] = (gate_ref[...] * d_mixed).astype(bf16)
    d_gate_ref[...] = jnp.sum(d_mixed * cross_ref[...], axis=0, keepdims=True)
    delta = head_sum(d_self.astype(f32) * self_ref[...])

    @pl.when(step == 0)
    def _():
        table_ref[...] = jnp.zeros(table_ref.shape, f32)

    table = put_row(table_ref[...], 2 * step, as_row(delta[:, :1]))
    table = put_row(table, 2 * step + 1, as_row(delta[:, HD : HD + 1]))
    table_ref[...] = table
    pack_ref[0, :tok, pl.ds(pl.multiple_of(step * LANES, LANES), LANES)] = d_self

    @pl.when(step == pl.num_programs(0) - 1)
    def _():
        pack_ref[0, tok:, :] = split_three(table_ref[...])


def query_back_kernel(
    counts, tok, flag_ref, q_ref, own_ids_ref, ids_ref, tk_ref, tv_ref, d_self_ref, d_cross_ref,
    self_ref, cross_ref, lse_self_ref, lse_cross_ref, raw_ref, gain_ref, cos_ref, sin_ref, *rest
):
    pieces = piece_views(rest[: len(counts)], counts, 2)
    d_raw_ref, d_gain_ref, d_tk_ref, d_tv_ref, acc_ref = rest[len(counts) :]
    own_ids = own_ids_ref[...]
    own_two = jnp.concatenate([own_ids, own_ids], axis=0)
    q_two = two_heads(q_ref[...])
    d_self = d_self_ref[0]
    d_self_two = two_heads(d_self)
    delta = columns_of(head_sum(d_self.astype(f32) * self_ref[...]))
    lse = columns_of(lse_self_ref[...])

    d_cross = d_cross_ref[...]
    d_cross_two = two_heads(d_cross)
    delta_cross = columns_of(head_sum(d_cross.astype(f32) * cross_ref[...]))
    lse_cross = columns_of(lse_cross_ref[...])
    cross_p = jnp.exp(mm(q_two, tk_ref[...], 1, 1) - lse_cross)
    d_cross_p = mm(d_cross_two, tv_ref[...], 1, 1)
    d_cross_s = (cross_p * (d_cross_p - delta_cross)).astype(bf16)
    d_tv_ref[...] = mm(cross_p.astype(bf16), d_cross_two, 0, 0)
    d_tk_ref[...] = mm(d_cross_s, q_two, 0, 0)
    acc_ref[...] = mm(d_cross_s, tk_ref[...], 1, 0)
    for slot, (ref, at) in enumerate(pieces):
        rows = ref.shape[1]

        @pl.when(flag_ref[slot] > 0)
        def _(slot=slot, ref=ref, at=at, rows=rows):
            key = ref[at]
            scores = mm(q_two, key, 1, 1)
            scores = jnp.where(own_two == ids_ref[slot : slot + 1, :rows], scores, MASKED)
            weights = jnp.exp(scores - lse)
            d_weights = mm(d_self_two, ref[at + 1], 1, 1)
            d_scores = (weights * (d_weights - delta)).astype(bf16)
            acc_ref[...] += mm(d_scores, key, 1, 0)

    d_query = one_pair(acc_ref[...]) * (HD**-0.5)
    d_raw, d_gain = norm_rope_back(raw_ref[0], gain_ref[...], cos_ref[...], sin_ref[...], d_query)
    d_raw_ref[...] = d_raw.astype(bf16)
    d_gain_ref[...] = d_gain


def key_back_kernel(counts, tok, flag_ref, kv_ref, own_ids_ref, ids_ref, raw_ref, gain_ref, cos_ref, sin_ref, *rest):
    n = len(counts)
    q_views = piece_views(rest[:n], counts, 1)
    q_tables = piece_views(rest[n : 2 * n], counts, 1)
    g_views = piece_views(rest[2 * n : 3 * n], counts, 1)
    g_tables = piece_views(rest[3 * n : 4 * n], counts, 1)
    d_raw_ref, d_gain_ref, d_value_ref, acc_k_ref, acc_v_ref = rest[4 * n :]
    step = pl.program_id(0)
    own_ids = own_ids_ref[...]
    k_two = two_heads(kv_ref[0])
    v_two = two_heads(kv_ref[1])
    acc_k_ref[...] = jnp.zeros(acc_k_ref.shape, f32)
    acc_v_ref[...] = jnp.zeros(acc_v_ref.shape, f32)
    for slot in range(PIECES):
        q_ref, at = q_views[slot]
        rows = q_ref.shape[1]
        first = tok - EDGE if slot == PIECES - 2 else 0

        @pl.when(flag_ref[slot] > 0)
        def _(slot=slot, q_ref=q_ref, at=at, rows=rows, first=first):
            query = q_ref[at]
            d_self = g_views[slot][0][at]
            lse = joined(q_tables[slot][0][at], tok)[:, first : first + rows]
            delta = joined(g_tables[slot][0][at], tok)[:, first : first + rows]
            same = own_ids == ids_ref[slot : slot + 1, :rows]
            scores = mm(k_two, query, 1, 1)
            d_weights = mm(v_two, d_self, 1, 1)
            p_low, d_low = [], []
            for head in range(2):
                part = slice(head * tok, (head + 1) * tok)
                masked = jnp.where(same, scores[part], MASKED)
                weights = jnp.exp(masked - take_row(lse, 2 * step + head))
                p_low.append(weights.astype(bf16))
                d_low.append((weights * (d_weights[part] - take_row(delta, 2 * step + head))).astype(bf16))
            acc_v_ref[...] += mm(jnp.concatenate(p_low, axis=0), d_self, 1, 0)
            acc_k_ref[...] += mm(jnp.concatenate(d_low, axis=0), query, 1, 0)

    d_raw, d_gain = norm_rope_back(
        raw_ref[0], gain_ref[...], cos_ref[...], sin_ref[...], one_pair(acc_k_ref[...])
    )
    d_raw_ref[...] = d_raw.astype(bf16)
    d_gain_ref[...] = d_gain
    d_value_ref[...] = one_pair(acc_v_ref[...]).astype(bf16)


def update_kernel(clip_ref, g_ref, one_ref, two_ref, w_ref, avg_ref, one_out, two_out, w_out, avg_out, low_out):
    one, two, weight, moving = adam_update(
        g_ref[...] * clip_ref[0], one_ref[...], two_ref[...], w_ref[...], avg_ref[...], RATE_MATRIX, DECAY_WEIGHT
    )
    one_out[...] = one
    two_out[...] = two
    w_out[...] = weight
    avg_out[...] = moving
    low_out[...] = weight.astype(bf16)


def adam_update(gradient, first_moment, second_moment, weight, moving, rate, decay):
    first_new = BETA_ONE * first_moment + (1.0 - BETA_ONE) * gradient
    second_new = BETA_TWO * second_moment + (1.0 - BETA_TWO) * gradient * gradient
    corr_one = 1.0 - BETA_ONE**STEP
    corr_two = 1.0 - BETA_TWO**STEP
    step_dir = first_new / corr_one / (jnp.sqrt(second_new / corr_two) + ADAM_EPS)
    weight_new = weight - rate * (step_dir + decay * weight)
    moving_new = EMA_DECAY * moving + (1.0 - EMA_DECAY) * weight_new
    return (first_new, second_new, weight_new, moving_new)


def call(kernel, grid, in_specs, out_specs, out_shape, args, scratch=(), prefetch=0, flops=0, moved=0):
    return pl.pallas_call(
        kernel,
        grid_spec=pltpu.PrefetchScalarGridSpec(
            num_scalar_prefetch=prefetch, grid=grid, in_specs=in_specs, out_specs=out_specs, scratch_shapes=scratch
        ),
        out_shape=out_shape,
        compiler_params=pltpu.CompilerParams(dimension_semantics=("arbitrary",) * len(grid), vmem_limit_bytes=VMEM),
        cost_estimate=pl.CostEstimate(flops=flops, bytes_accessed=moved, transcendentals=0),
    )(*args)


def whole(shape):
    return pl.BlockSpec(shape, lambda *_: (0,) * len(shape))


def pair(rows, first=0):
    return pl.BlockSpec((rows, LANES), lambda j, *_: (0, first + j))


def pairs(count, rows, at=0):
    return pl.BlockSpec((count, rows, LANES), lambda j, *_: (at, 0, j))


def shape_of(shape, dtype):
    return jax.ShapeDtypeStruct(shape, dtype)


def shifted(x, by):
    count = lax.axis_size("img")
    return lax.ppermute(x, "img", [(i + by, i) for i in range(count) if 0 <= i + by < count])


def crossed(x, bit):
    count = lax.axis_size("img")
    return lax.ppermute(x, "img", [(i, i ^ bit) for i in range(count)])


def other_txt(x):
    return lax.ppermute(x, "txt", [(0, 1), (1, 0)])


def neighbourhood(x, low_edge, high_edge):
    beside = crossed(x, 1)
    across = crossed(x, 2)
    above, below = shifted(x, 4), shifted(x, -4)
    low, high = shifted(low_edge, -5), shifted(high_edge, 5)
    above_across, below_across = shifted(across, 4), shifted(across, -4)
    three = crossed(jnp.concatenate([across, above, below], axis=0), 1)
    two = crossed(jnp.concatenate([above_across, below_across], axis=0), 1)
    return [x, beside, across, above, below, three, above_across, below_across, two, low, high]


PIECE_COUNTS = (1, 1, 1, 1, 1, 3, 1, 1, 2, 1, 1)


def neighbour_indices(i):
    b = i ^ 1
    return [
        i, b, i ^ 2, i + 4, i - 4, b ^ 2, b + 4, b - 4, (i ^ 2) + 4, (i ^ 2) - 4, (b ^ 2) + 4, (b ^ 2) - 4, i - 5, i + 5
    ]


def token_places(row_index, image_sides):
    heights = image_sides[:, 0]
    widths = image_sides[:, 1]
    lengths = heights * (widths + 1)
    sample_ends = jnp.cumsum(lengths, dtype=jnp.int32)
    starts = sample_ends - lengths
    sample_ids = ids_of(row_index, sample_ends)
    matched = jnp.arange(image_sides.shape[0], dtype=jnp.int32)[None, :] == sample_ids[:, None]
    first_row = jnp.sum(jnp.where(matched, starts[None, :], 0), axis=1, dtype=jnp.int32)
    row_width = jnp.sum(jnp.where(matched, widths[None, :] + 1, 0), axis=1, dtype=jnp.int32)
    row_width = jnp.maximum(row_width, 1)
    offset = row_index - first_row
    return (sample_ids, offset // row_width, offset % row_width, sample_ends)


def ids_of(rows, sample_ends):
    return jnp.sum((sample_ends <= rows[..., None]).astype(jnp.int32), axis=-1, dtype=jnp.int32)


def turn_tables(row_pos, col_pos):
    quarter = HD // 4
    frequency = 10000.0 ** (-jnp.arange(quarter, dtype=f32) / quarter)
    angles = jnp.concatenate(
        [row_pos.astype(f32)[:, None] * frequency[None, :], col_pos.astype(f32)[:, None] * frequency[None, :]], axis=1
    )
    cosine, sine = jnp.cos(angles), jnp.sin(angles)
    return jnp.concatenate([cosine] * 4, axis=1), jnp.concatenate([-sine, sine, -sine, sine], axis=1)


def rms_norm(values):
    return values * lax.rsqrt(jnp.mean(values * values, axis=-1, keepdims=True) + EPS_NORM)


def rms_back(values, d_normed):
    inverse = lax.rsqrt(jnp.mean(values * values, axis=-1, keepdims=True) + EPS_NORM)
    normed = values * inverse
    return inverse * (d_normed - normed * jnp.mean(d_normed * normed, axis=-1, keepdims=True))


def on_device(
    tokens, cotangent, text_states, conditions, image_sides, master, moment_one, moment_two, average,
    small_master, small_one, small_two, small_average,
):
    n_img = lax.axis_size("img")
    n_txt = lax.axis_size("txt")
    img_index = lax.axis_index("img")
    txt_index = lax.axis_index("txt")
    tok = tokens.shape[0]
    samples = image_sides.shape[0]
    half_d = D // n_txt
    half_ff = FF // n_txt
    local_heads = half_d // HD
    n_pairs = half_d // LANES

    tables = [
        (D // n_img, 2 * half_ff),
        (half_ff // n_img, D),
        (D // n_img, 3 * half_d),
        (TXT_D // n_img, 2 * half_d),
        (half_d // n_img, D),
        (COND // n_img, 6 * half_d),
    ]
    flat = master.reshape(-1)
    own_rows = []
    offset = 0
    for rows, columns in tables:
        own_rows.append(flat[offset : offset + rows * columns].reshape(rows, columns).astype(bf16))
        offset += rows * columns
    own_updown, own_down, own_project, own_text, own_output, own_modulate = own_rows

    def gather(rows):
        return lax.all_gather(rows, "img", axis=0, tiled=True)

    def scatter(terms):
        return lax.psum_scatter(terms, "img", scatter_dimension=0, tiled=True)

    w_project = gather(own_project)

    gain_attn = small_master[:D]
    gain_ffn = small_master[D : 2 * D]
    gain_query = small_master[2 * D : 2 * D + HD]
    gain_key = small_master[2 * D + HD : 2 * D + 2 * HD]
    gain_text = small_master[2 * D + 2 * HD : 2 * D + 3 * HD]
    gate_heads = small_master[2 * D + 3 * HD :]
    gate_local = lax.dynamic_slice_in_dim(gate_heads, txt_index * local_heads, local_heads)
    tanh_gate = jnp.tanh(gate_local)
    gate_lanes = jnp.repeat(tanh_gate, HD)[None, :]
    gain_query_pair = jnp.tile(gain_query, 2)[None, :]
    gain_key_pair = jnp.tile(gain_key, 2)[None, :]

    cond_rows = COND // n_img
    cond_own = lax.dynamic_slice_in_dim(conditions, img_index * cond_rows, cond_rows, 1)
    silu_own = jax.nn.silu(cond_own.astype(f32)).astype(bf16)
    mod_half = lax.psum(jnp.dot(silu_own, own_modulate, preferred_element_type=f32), "img").astype(bf16)
    mods = lax.all_gather(mod_half.reshape(samples, 6, half_d), "txt", axis=2, tiled=True)

    row_index = img_index * tok + jnp.arange(tok, dtype=jnp.int32)
    sample_ids, row_pos, col_pos, sample_ends = token_places(row_index, image_sides)
    cosine, sine = turn_tables(row_pos, col_pos)
    one_hot = sample_ids[:, None] == jnp.arange(samples, dtype=jnp.int32)[None, :]
    per_token = jnp.dot(one_hot.astype(bf16), mods.reshape(samples, 6 * D), preferred_element_type=f32).astype(bf16)
    shift_one, scale_one, gate_one, shift_two, scale_two, gate_two = (
        per_token[:, c * D : (c + 1) * D].astype(f32) for c in range(6)
    )

    pieces = jnp.stack([jnp.asarray(p, jnp.int32) for p in neighbour_indices(img_index)])
    place = img_index % 4
    inside = (pieces >= 0) & (pieces < n_img)
    slots = jnp.arange(PIECES)
    inside &= (slots != PIECES - 2) | (place == 0)
    inside &= (slots != PIECES - 1) | (place == 3)
    column = jnp.arange(tok, dtype=jnp.int32)[None, :]
    piece_rows = pieces[:, None] * tok + column + jnp.where(slots == PIECES - 2, tok - EDGE, 0)[:, None]
    there = inside[:, None] & ((slots[:, None] < PIECES - 2) | (column < EDGE))
    piece_ids = jnp.where(there, ids_of(piece_rows, sample_ends), -1)
    flags = jnp.any((piece_ids >= sample_ids[0]) & (piece_ids <= sample_ids[-1]), axis=1).astype(jnp.int32)
    piece_ids = jnp.concatenate([piece_ids, jnp.full((16 - PIECES, tok), -1, jnp.int32)], axis=0)
    own_ids = sample_ids[:, None]

    text_rows = text_states.shape[0]
    text_len = text_rows * n_img
    text_columns = lax.all_to_all(text_states, "img", split_axis=1, concat_axis=0, tiled=True)
    text_proj = scatter(jnp.dot(text_columns, own_text, preferred_element_type=f32))
    text_shape = (text_rows, local_heads, HD)
    text_raw = text_proj[:, :half_d].reshape(text_shape)
    text_normed = rms_norm(text_raw)
    text_key_low = (text_normed * gain_text).reshape(text_rows, half_d).astype(bf16)
    text_low = jnp.concatenate([text_key_low, text_proj[:, half_d:].astype(bf16)], axis=1)
    all_text = gather(text_low)

    x_float = tokens.astype(f32)
    x_normed = rms_norm(x_float)
    normed_one = x_normed * gain_attn
    attn_in = (normed_one * (1.0 + scale_one) + shift_one).astype(bf16)
    queries, own_kv, raw_qk = call(
        project_kernel,
        (n_pairs,),
        [whole((tok, D)), pair(D), pair(D, n_pairs), pair(D, 2 * n_pairs)]
        + [whole((1, LANES))] * 2
        + [whole((tok, LANES))] * 2,
        [pair(tok), pairs(2, tok), pairs(2, tok)],
        [
            shape_of((tok, half_d), bf16),
            shape_of((2, tok, half_d), bf16),
            shape_of((2, tok, half_d), f32),
        ],
        (attn_in, w_project, w_project, w_project, gain_query_pair, gain_key_pair, cosine, sine),
        flops=2 * tok * D * 3 * half_d,
        moved=2 * D * 3 * half_d,
    )
    kv_pieces = neighbourhood(own_kv, own_kv[:, tok - EDGE :], own_kv[:, :EDGE])

    w_output = gather(own_output)
    w_updown = gather(own_updown)
    w_down = gather(own_down)
    w_output_other = other_txt(w_output)

    kv_specs = [pairs(2 * c, a.shape[1]) for c, a in zip(PIECE_COUNTS, kv_pieces)]
    id_specs = [whole((tok, 1)), whole((16, tok))]
    text_specs = [pair(text_len), pair(text_len, n_pairs)]
    attention_flops = 2 * 2 * tok * 12 * tok * half_d
    mixed_low, self_out, cross_out, lse_self, lse_cross, query_pack = call(
        functools.partial(attend_kernel, PIECE_COUNTS, tok),
        (n_pairs,),
        [pair(tok)] + id_specs + text_specs + [pair(1)] + kv_specs,
        [pair(tok)] * 5 + [whole((1, tok + PACK, half_d))],
        [shape_of((tok, half_d), bf16)]
        + [shape_of((tok, half_d), f32)] * 4
        + [shape_of((1, tok + PACK, half_d), bf16)],
        (flags, queries, own_ids, piece_ids, all_text, all_text, gate_lanes, *kv_pieces),
        scratch=[
            pltpu.VMEM((PIECES, 2 * tok, tok), f32),
            pltpu.VMEM((2 * tok, LANES), f32),
            pltpu.VMEM((2 * tok, LANES), f32),
            pltpu.VMEM((2 * tok, LANES), f32),
            pltpu.VMEM((PACK, tok), f32),
        ],
        prefetch=1,
        flops=attention_flops,
        moved=13 * 4 * tok * half_d,
    )

    def pack_edges(pack):
        table = pack[:, tok:]
        return (
            jnp.concatenate([pack[:, tok - EDGE : tok], table], axis=1),
            jnp.concatenate([pack[:, :EDGE], table], axis=1),
        )

    query_pieces = neighbourhood(query_pack, *pack_edges(query_pack))

    mixed_other = other_txt(mixed_low)
    attn_out = jnp.dot(mixed_low, w_output, preferred_element_type=f32) + jnp.dot(
        mixed_other, w_output_other, preferred_element_type=f32
    )
    hidden = x_float + gate_one * attn_out
    h_normed = rms_norm(hidden)
    normed_two = h_normed * gain_ffn
    ffn_in = (normed_two * (1.0 + scale_two) + shift_two).astype(bf16)
    gate_up = jnp.dot(ffn_in, w_updown, preferred_element_type=f32)
    gate, up = gate_up[:, :half_ff], gate_up[:, half_ff:]
    sigmoid = jax.nn.sigmoid(gate)
    activated = gate * sigmoid
    hidden_units = (activated * up).astype(bf16)
    branch_part = jnp.dot(hidden_units, w_down, preferred_element_type=f32)
    branch = branch_part + other_txt(branch_part)
    block_out = hidden + gate_two * branch

    d_out = cotangent.astype(f32)
    d_gate_two = d_out * branch
    d_branch = (d_out * gate_two).astype(bf16)
    d_units = mm(d_branch, w_down, 1, 1)
    d_gate = d_units * up * sigmoid * (1.0 + gate * (1.0 - sigmoid))
    d_up = d_units * activated
    d_gate_up = jnp.concatenate([d_gate.astype(bf16), d_up.astype(bf16)], axis=1)
    d_ffn_part = mm(d_gate_up, w_updown, 1, 1).astype(bf16)
    d_ffn_in = d_ffn_part.astype(f32) + other_txt(d_ffn_part).astype(f32)
    grad_down = scatter(mm(hidden_units, d_branch, 0, 0).astype(bf16)).astype(f32)
    grad_updown = scatter(mm(ffn_in, d_gate_up, 0, 0).astype(bf16)).astype(f32)

    d_scale_two = d_ffn_in * normed_two
    d_normed_two = d_ffn_in * (1.0 + scale_two)
    d_gain_ffn = jnp.sum(d_normed_two * h_normed, axis=0)
    d_hidden = d_out + rms_back(hidden, d_normed_two * gain_ffn)
    d_gate_one = d_hidden * attn_out
    d_attn = (d_hidden * gate_one).astype(bf16)
    grad_pack, d_cross_low, d_gate_lanes = call(
        functools.partial(mixed_back_kernel, tok),
        (n_pairs,),
        [whole((tok, D)), pl.BlockSpec((LANES, D), lambda j: (j, 0)), pair(tok), pair(tok), pair(1)],
        [whole((1, tok + PACK, half_d)), pair(tok), pair(1)],
        [
            shape_of((1, tok + PACK, half_d), bf16),
            shape_of((tok, half_d), bf16),
            shape_of((1, half_d), f32),
        ],
        (d_attn, w_output, self_out, cross_out, gate_lanes),
        scratch=[pltpu.VMEM((PACK, tok), f32)],
        flops=2 * tok * D * half_d,
        moved=4 * D * half_d,
    )
    grad_pieces = neighbourhood(grad_pack, *pack_edges(grad_pack))
    grad_output = scatter(mm(mixed_low, d_attn, 0, 0).astype(bf16)).astype(f32)

    turn_specs = [whole((1, LANES)), whole((tok, LANES)), whole((tok, LANES))]
    d_query_raw, d_gain_query, d_text_key, d_text_value = call(
        functools.partial(query_back_kernel, PIECE_COUNTS, tok),
        (n_pairs,),
        [pair(tok)]
        + id_specs
        + text_specs
        + [pairs(1, tok), pair(tok)]
        + [pair(tok)] * 4
        + [pairs(1, tok)]
        + turn_specs
        + kv_specs,
        [pair(tok), pair(1), pair(text_len), pair(text_len)],
        [
            shape_of((tok, half_d), bf16),
            shape_of((1, half_d), f32),
            shape_of((text_len, half_d), f32),
            shape_of((text_len, half_d), f32),
        ],
        (
            flags, queries, own_ids, piece_ids, all_text, all_text, grad_pack, d_cross_low,
            self_out, cross_out, lse_self, lse_cross, raw_qk, gain_query_pair, cosine, sine, *kv_pieces,
        ),
        scratch=[pltpu.VMEM((2 * tok, LANES), f32)],
        prefetch=1,
        flops=attention_flops * 3 // 2,
        moved=13 * 4 * tok * half_d,
    )

    def pack_specs(arrays):
        views = [pairs(c, a.shape[1] - PACK) for c, a in zip(PIECE_COUNTS, arrays)]
        rows = [
            pl.BlockSpec((c, PACK, half_d), lambda j, *_, at=(a.shape[1] - PACK) // PACK: (0, at, 0))
            for c, a in zip(PIECE_COUNTS, arrays)
        ]
        return views + rows

    d_key_raw, d_gain_key, d_value = call(
        functools.partial(key_back_kernel, PIECE_COUNTS, tok),
        (n_pairs,),
        [pairs(2, tok)]
        + id_specs
        + [pairs(1, tok, 1)]
        + turn_specs
        + pack_specs(query_pieces)
        + pack_specs(grad_pieces),
        [pair(tok), pair(1), pair(tok)],
        [
            shape_of((tok, half_d), bf16),
            shape_of((1, half_d), f32),
            shape_of((tok, half_d), bf16),
        ],
        (
            flags, own_kv, own_ids, piece_ids, raw_qk, gain_key_pair, cosine, sine,
            *query_pieces, *query_pieces, *grad_pieces, *grad_pieces,
        ),
        scratch=[pltpu.VMEM((2 * tok, LANES), f32)] * 2,
        prefetch=1,
        flops=attention_flops * 2,
        moved=13 * 4 * tok * half_d,
    )
    d_projected = jnp.concatenate([d_query_raw, d_key_raw, d_value], axis=1)
    grad_project = scatter(mm(attn_in, d_projected, 0, 0).astype(bf16)).astype(f32)
    d_attn_part = mm(d_projected, w_project, 1, 1)
    d_attn_in = d_attn_part + other_txt(d_attn_part)

    text_own = scatter(jnp.concatenate([d_text_key, d_text_value], axis=1))
    d_text_scaled = text_own[:, :half_d].reshape(text_shape)
    d_gain_text = jnp.sum(d_text_scaled * text_normed, axis=(0, 1))
    d_text_raw = rms_back(text_raw, d_text_scaled * gain_text).reshape(text_rows, half_d)
    d_text_proj = gather(jnp.concatenate([d_text_raw, text_own[:, half_d:]], axis=1).astype(bf16))
    grad_text = mm(text_columns, d_text_proj, 0, 0)

    d_scale_one = d_attn_in * normed_one
    d_normed_one = d_attn_in * (1.0 + scale_one)
    d_gain_attn = jnp.sum(d_normed_one * x_normed, axis=0)
    d_tokens = d_hidden + rms_back(x_float, d_normed_one * gain_attn)

    one_hot_wide = one_hot.astype(f32)

    def by_sample(values):
        summed = lax.dot_general(one_hot_wide, values, (((0,), (0,)), ((), ())), precision=HIGH)
        return lax.dynamic_slice_in_dim(summed, txt_index * half_d, half_d, 1)

    d_mod = lax.psum(
        jnp.concatenate(
            [by_sample(v) for v in (d_attn_in, d_scale_one, d_gate_one, d_ffn_in, d_scale_two, d_gate_two)], axis=1
        ),
        "img",
    )
    grad_modulate = lax.dot_general(silu_own.astype(f32), d_mod, (((0,), (0,)), ((), ())), precision=HIGH)

    grads = [grad_updown, grad_down, grad_project, grad_text, grad_output, grad_modulate]
    reduced = jnp.concatenate([g.reshape(-1, LANES) for g in grads], axis=0)

    replica = (txt_index == 0).astype(f32)
    d_gate_local = jnp.sum(d_gate_lanes.reshape(local_heads, HD), axis=1) * (1.0 - tanh_gate**2)
    gate_full = lax.dynamic_update_slice(jnp.zeros((HEADS,), f32), d_gate_local, (txt_index * local_heads,))
    small_terms = jnp.concatenate(
        [
            d_gain_attn * replica,
            d_gain_ffn * replica,
            jnp.sum(d_gain_query.reshape(local_heads, HD), axis=0),
            jnp.sum(d_gain_key.reshape(local_heads, HD), axis=0),
            d_gain_text,
            gate_full,
        ]
    )
    local_square = jnp.sum(reduced * reduced)
    small_grad, square_big = lax.psum((small_terms, local_square), ("img", "txt"))
    grad_square = square_big + jnp.sum(small_grad * small_grad)
    clip_factor = MAX_NORM / jnp.maximum(jnp.sqrt(grad_square), MAX_NORM)

    lines = reduced.shape[0]
    block = math.gcd(lines, 512)
    line_spec = pl.BlockSpec((block, LANES), lambda i: (i, 0))
    as_lines = (lines, LANES)
    updated = call(
        update_kernel,
        (lines // block,),
        [pl.BlockSpec(memory_space=pltpu.SMEM)] + [line_spec] * 5,
        [line_spec] * 5,
        [shape_of(as_lines, f32)] * 4 + [shape_of(as_lines, bf16)],
        (clip_factor.reshape(1), reduced, *(a.reshape(as_lines) for a in (moment_one, moment_two, master, average))),
        flops=20 * lines * LANES,
        moved=38 * lines * LANES,
    )
    one_new, two_new, master_new, average_new, master_low = (a.reshape(master.shape) for a in updated)
    small_one_new, small_two_new, small_new, small_average_new = adam_update(
        small_grad * clip_factor, small_one, small_two, small_master, small_average, RATE_SMALL, 0.0
    )
    return (
        block_out,
        d_tokens,
        grad_square,
        one_new,
        two_new,
        master_new,
        average_new,
        master_low,
        small_one_new,
        small_two_new,
        small_new,
        small_average_new,
    )


def solution(mesh):
    rows = P("img", None)
    shards = P("img", "txt", None)
    in_specs = (rows, rows, rows, P(), P(), shards, shards, shards, shards, P(), P(), P(), P())
    out_specs = (rows, rows, P(), shards, shards, shards, shards, shards, P(), P(), P(), P())
    return jax.shard_map(on_device, mesh=mesh, in_specs=in_specs, out_specs=out_specs, check_vma=False)
```

```python
import functools
import math

import jax
import jax.numpy as jnp
from jax import lax
from jax.experimental import pallas as pl
from jax.experimental.pallas import tpu as pltpu
from jax.sharding import PartitionSpec as P

D = 1536
HEADS = 24
HD = 64
FF = 4096
TXT_D = 4096
COND = 1024
SIDE_MAX = 32
STEP = 10

HIGH = lax.Precision.HIGHEST
EPS_NORM = 1e-06
MAX_NORM = 1.0
BETA_ONE = 0.5
BETA_TWO = 0.5
RATE_MATRIX = 0.01
RATE_SMALL = 0.1
DECAY_WEIGHT = 0.01
ADAM_EPS = 1e-08
EMA_DECAY = 0.8

LANES = 128
EDGE = 128
PACK = 16
PIECES = 14
MASKED = -1e30
VMEM = 48 * 1024 * 1024

bf16 = jnp.bfloat16
f32 = jnp.float32


def mm(a, b, on_a, on_b):
    return lax.dot_general(a, b, (((on_a,), (on_b,)), ((), ())), preferred_element_type=f32)


def lane_index(rows):
    return lax.broadcasted_iota(jnp.int32, (rows, LANES), 1)


def head_sum(values):
    low = lane_index(values.shape[0]) < HD
    first = jnp.sum(jnp.where(low, values, 0.0), axis=1, keepdims=True)
    second = jnp.sum(jnp.where(low, 0.0, values), axis=1, keepdims=True)
    return jnp.where(low, first, second)


def swap_halves(values):
    first = lane_index(values.shape[0]) % HD < HD // 2
    return jnp.where(
        first, pltpu.roll(values, LANES - HD // 2, 1), pltpu.roll(values, HD // 2, 1)
    )


def two_heads(pair):
    low = lane_index(pair.shape[0]) < HD
    zero = jnp.zeros_like(pair)
    return jnp.concatenate([jnp.where(low, pair, zero), jnp.where(low, zero, pair)], axis=0)


def one_pair(stacked):
    rows = stacked.shape[0] // 2
    low = lane_index(rows) < HD
    return jnp.where(low, stacked[:rows], stacked[rows:])


def columns_of(spread):
    return jnp.concatenate([spread[:, :1], spread[:, HD : HD + 1]], axis=0)


def norm_rope(raw, gain, cosine, sine):
    inverse = lax.rsqrt(head_sum(raw * raw) * (1.0 / HD) + EPS_NORM)
    scaled = raw * inverse * gain
    return scaled * cosine + swap_halves(scaled) * sine


def norm_rope_back(raw, gain, cosine, sine, d_out):
    inverse = lax.rsqrt(head_sum(raw * raw) * (1.0 / HD) + EPS_NORM)
    normed = raw * inverse
    d_scaled = d_out * cosine - swap_halves(d_out) * sine
    d_gain = jnp.sum(d_scaled * normed, axis=0, keepdims=True)
    d_normed = d_scaled * gain
    d_raw = inverse * (d_normed - normed * (head_sum(d_normed * normed) * (1.0 / HD)))
    return d_raw, d_gain


def split_three(values):
    high = values.astype(bf16)
    rest = values - high.astype(f32)
    middle = rest.astype(bf16)
    last = (rest - middle.astype(f32)).astype(bf16)
    return jnp.concatenate([high, middle, last], axis=1)


def joined(packed, rows):
    wide = packed.astype(f32)
    return wide[:, :rows] + wide[:, rows : 2 * rows] + wide[:, 2 * rows : 3 * rows]


def put_row(table, index, row):
    at = lax.broadcasted_iota(jnp.int32, table.shape, 0) == index
    return jnp.where(at, row, table)


def take_row(table, index):
    at = lax.broadcasted_iota(jnp.int32, table.shape, 0) == index
    return jnp.sum(jnp.where(at, table, 0.0), axis=0, keepdims=True)


def as_row(column):
    return jnp.broadcast_to(column, (column.shape[0], LANES)).T[:1]


def project_kernel(a_ref, wq_ref, wk_ref, wv_ref, gq_ref, gk_ref, cos_ref, sin_ref, q_ref, kv_ref, raw_ref):
    a = a_ref[...]
    cosine, sine = cos_ref[...], sin_ref[...]
    raw_q = mm(a, wq_ref[...], 1, 0)
    raw_k = mm(a, wk_ref[...], 1, 0)
    raw_ref[0] = raw_q
    raw_ref[1] = raw_k
    q_ref[...] = norm_rope(raw_q, gq_ref[...], cosine, sine).astype(bf16) * jnp.asarray(HD**-0.5, bf16)
    kv_ref[0] = norm_rope(raw_k, gk_ref[...], cosine, sine).astype(bf16)
    kv_ref[1] = mm(a, wv_ref[...], 1, 0).astype(bf16)


def piece_views(piece_refs, counts, per):
    views = []
    for ref, count in zip(piece_refs, counts):
        for at in range(count):
            views.append((ref, at * per))
    return views


def attend_kernel(counts, tok, flag_ref, q_ref, own_ids_ref, ids_ref, tk_ref, tv_ref, gate_ref, *rest):
    pieces = piece_views(rest[: len(counts)], counts, 2)
    mixed_ref, self_ref, cross_ref, lse_self_ref, lse_cross_ref, pack_ref = rest[len(counts) : len(counts) + 6]
    scores_ref, most_ref, total_ref, acc_ref, table_ref = rest[len(counts) + 6 :]
    step = pl.program_id(0)
    own_ids = own_ids_ref[...]
    q_pair = q_ref[...]
    q_two = two_heads(q_pair)
    own_two = jnp.concatenate([own_ids, own_ids], axis=0)
    most_ref[...] = jnp.full(most_ref.shape, MASKED, f32)
    total_ref[...] = jnp.zeros(total_ref.shape, f32)
    acc_ref[...] = jnp.zeros(acc_ref.shape, f32)
    for slot, (ref, at) in enumerate(pieces):
        rows = ref.shape[1]

        @pl.when(flag_ref[slot] > 0)
        def _(slot=slot, ref=ref, at=at, rows=rows):
            scores = mm(q_two, ref[at], 1, 1)
            scores = jnp.where(own_two == ids_ref[slot : slot + 1, :rows], scores, MASKED)
            scores_ref[slot, :, :rows] = scores
            most = most_ref[...]
            for part in range(rows // LANES):
                most = jnp.maximum(most, scores[:, part * LANES : (part + 1) * LANES])
            most_ref[...] = most

    row_most = jnp.max(most_ref[...], axis=1, keepdims=True)
    for slot, (ref, at) in enumerate(pieces):
        rows = ref.shape[1]

        @pl.when(flag_ref[slot] > 0)
        def _(slot=slot, ref=ref, at=at, rows=rows):
            weights = jnp.exp(scores_ref[slot, :, :rows] - row_most)
            total = total_ref[...]
            for part in range(rows // LANES):
                total = total + weights[:, part * LANES : (part + 1) * LANES]
            total_ref[...] = total
            acc_ref[...] += mm(weights.astype(bf16), ref[at + 1], 1, 0)

    row_total = jnp.sum(total_ref[...], axis=1, keepdims=True)
    self_out = one_pair(acc_ref[...] / row_total)
    lse_self = row_most + jnp.log(row_total)

    cross_scores = mm(q_two, tk_ref[...], 1, 1)
    cross_most = jnp.max(cross_scores, axis=1, keepdims=True)
    cross_weights = jnp.exp(cross_scores - cross_most)
    cross_total = jnp.sum(cross_weights, axis=1, keepdims=True)
    cross_out = one_pair(mm(cross_weights.astype(bf16), tv_ref[...], 1, 0) / cross_total)
    lse_cross = cross_most + jnp.log(cross_total)

    self_ref[...] = self_out
    cross_ref[...] = cross_out
    mixed_ref[...] = (self_out + gate_ref[...] * cross_out).astype(bf16)
    spread = (tok, LANES)
    low = lane_index(tok) < HD
    lse_self_ref[...] = jnp.where(
        low, jnp.broadcast_to(lse_self[:tok], spread), jnp.broadcast_to(lse_self[tok:], spread)
    )
    lse_cross_ref[...] = jnp.where(
        low, jnp.broadcast_to(lse_cross[:tok], spread), jnp.broadcast_to(lse_cross[tok:], spread)
    )

    @pl.when(step == 0)
    def _():
        table_ref[...] = jnp.zeros(table_ref.shape, f32)

    table = put_row(table_ref[...], 2 * step, as_row(lse_self[:tok]))
    table = put_row(table, 2 * step + 1, as_row(lse_self[tok:]))
    table_ref[...] = table
    pack_ref[0, :tok, pl.ds(pl.multiple_of(step * LANES, LANES), LANES)] = q_pair

    @pl.when(step == pl.num_programs(0) - 1)
    def _():
        pack_ref[0, tok:, :] = split_three(table_ref[...])


def mixed_back_kernel(tok, d_attn_ref, w_ref, self_ref, cross_ref, gate_ref, pack_ref, d_cross_ref, d_gate_ref, table_ref):
    step = pl.program_id(0)
    d_mixed = mm(d_attn_ref[...], w_ref[...], 1, 1)
    d_self = d_mixed.astype(bf16)
    d_cross_ref[...] = (gate_ref[...] * d_mixed).astype(bf16)
    d_gate_ref[...] = jnp.sum(d_mixed * cross_ref[...], axis=0, keepdims=True)
    delta = head_sum(d_self.astype(f32) * self_ref[...])

    @pl.when(step == 0)
    def _():
        table_ref[...] = jnp.zeros(table_ref.shape, f32)

    table = put_row(table_ref[...], 2 * step, as_row(delta[:, :1]))
    table = put_row(table, 2 * step + 1, as_row(delta[:, HD : HD + 1]))
    table_ref[...] = table
    pack_ref[0, :tok, pl.ds(pl.multiple_of(step * LANES, LANES), LANES)] = d_self

    @pl.when(step == pl.num_programs(0) - 1)
    def _():
        pack_ref[0, tok:, :] = split_three(table_ref[...])


def query_back_kernel(
    counts, tok, flag_ref, q_ref, own_ids_ref, ids_ref, tk_ref, tv_ref, d_self_ref, d_cross_ref,
    self_ref, cross_ref, lse_self_ref, lse_cross_ref, raw_ref, gain_ref, cos_ref, sin_ref, *rest
):
    pieces = piece_views(rest[: len(counts)], counts, 2)
    d_raw_ref, d_gain_ref, d_tk_ref, d_tv_ref, acc_ref = rest[len(counts) :]
    own_ids = own_ids_ref[...]
    own_two = jnp.concatenate([own_ids, own_ids], axis=0)
    q_two = two_heads(q_ref[...])
    d_self = d_self_ref[0]
    d_self_two = two_heads(d_self)
    delta = columns_of(head_sum(d_self.astype(f32) * self_ref[...]))
    lse = columns_of(lse_self_ref[...])

    d_cross = d_cross_ref[...]
    d_cross_two = two_heads(d_cross)
    delta_cross = columns_of(head_sum(d_cross.astype(f32) * cross_ref[...]))
    lse_cross = columns_of(lse_cross_ref[...])
    cross_p = jnp.exp(mm(q_two, tk_ref[...], 1, 1) - lse_cross)
    d_cross_p = mm(d_cross_two, tv_ref[...], 1, 1)
    d_cross_s = (cross_p * (d_cross_p - delta_cross)).astype(bf16)
    d_tv_ref[...] = mm(cross_p.astype(bf16), d_cross_two, 0, 0)
    d_tk_ref[...] = mm(d_cross_s, q_two, 0, 0)
    acc_ref[...] = mm(d_cross_s, tk_ref[...], 1, 0)
    for slot, (ref, at) in enumerate(pieces):
        rows = ref.shape[1]

        @pl.when(flag_ref[slot] > 0)
        def _(slot=slot, ref=ref, at=at, rows=rows):
            key = ref[at]
            scores = mm(q_two, key, 1, 1)
            scores = jnp.where(own_two == ids_ref[slot : slot + 1, :rows], scores, MASKED)
            weights = jnp.exp(scores - lse)
            d_weights = mm(d_self_two, ref[at + 1], 1, 1)
            d_scores = (weights * (d_weights - delta)).astype(bf16)
            acc_ref[...] += mm(d_scores, key, 1, 0)

    d_query = one_pair(acc_ref[...]) * (HD**-0.5)
    d_raw, d_gain = norm_rope_back(raw_ref[0], gain_ref[...], cos_ref[...], sin_ref[...], d_query)
    d_raw_ref[...] = d_raw.astype(bf16)
    d_gain_ref[...] = d_gain


def key_back_kernel(counts, tok, flag_ref, kv_ref, own_ids_ref, ids_ref, raw_ref, gain_ref, cos_ref, sin_ref, *rest):
    n = len(counts)
    q_views = piece_views(rest[:n], counts, 1)
    q_tables = piece_views(rest[n : 2 * n], counts, 1)
    g_views = piece_views(rest[2 * n : 3 * n], counts, 1)
    g_tables = piece_views(rest[3 * n : 4 * n], counts, 1)
    d_raw_ref, d_gain_ref, d_value_ref, acc_k_ref, acc_v_ref = rest[4 * n :]
    step = pl.program_id(0)
    own_ids = own_ids_ref[...]
    k_two = two_heads(kv_ref[0])
    v_two = two_heads(kv_ref[1])
    acc_k_ref[...] = jnp.zeros(acc_k_ref.shape, f32)
    acc_v_ref[...] = jnp.zeros(acc_v_ref.shape, f32)
    for slot in range(PIECES):
        q_ref, at = q_views[slot]
        rows = q_ref.shape[1]
        first = tok - EDGE if slot == PIECES - 2 else 0

        @pl.when(flag_ref[slot] > 0)
        def _(slot=slot, q_ref=q_ref, at=at, rows=rows, first=first):
            query = q_ref[at]
            d_self = g_views[slot][0][at]
            lse = joined(q_tables[slot][0][at], tok)[:, first : first + rows]
            delta = joined(g_tables[slot][0][at], tok)[:, first : first + rows]
            same = own_ids == ids_ref[slot : slot + 1, :rows]
            scores = mm(k_two, query, 1, 1)
            d_weights = mm(v_two, d_self, 1, 1)
            p_low, d_low = [], []
            for head in range(2):
                part = slice(head * tok, (head + 1) * tok)
                masked = jnp.where(same, scores[part], MASKED)
                weights = jnp.exp(masked - take_row(lse, 2 * step + head))
                p_low.append(weights.astype(bf16))
                d_low.append((weights * (d_weights[part] - take_row(delta, 2 * step + head))).astype(bf16))
            acc_v_ref[...] += mm(jnp.concatenate(p_low, axis=0), d_self, 1, 0)
            acc_k_ref[...] += mm(jnp.concatenate(d_low, axis=0), query, 1, 0)

    d_raw, d_gain = norm_rope_back(
        raw_ref[0], gain_ref[...], cos_ref[...], sin_ref[...], one_pair(acc_k_ref[...])
    )
    d_raw_ref[...] = d_raw.astype(bf16)
    d_gain_ref[...] = d_gain
    d_value_ref[...] = one_pair(acc_v_ref[...]).astype(bf16)


def unflatten_kernel(tables, *refs):
    for (rows, columns), lines_ref, out_ref in zip(tables, refs, refs[len(tables) :]):
        per_row = columns // LANES
        for at in range(per_row):
            out_ref[:, at * LANES : (at + 1) * LANES] = lines_ref[pl.ds(at, rows, stride=per_row), :].astype(bf16)


def flatten_kernel(*refs):
    *grad_refs, lines_ref, square_ref = refs
    offset = 0
    square = jnp.zeros((1, LANES), f32)
    for ref in grad_refs:
        rows, columns = ref.shape
        per_row = columns // LANES
        for at in range(per_row):
            part = ref[:, at * LANES : (at + 1) * LANES]
            lines_ref[pl.ds(offset + at, rows, stride=per_row), :] = part
            square = square + jnp.sum(part * part, axis=0, keepdims=True)
        offset += rows * per_row
    square_ref[...] = square


def update_kernel(clip_ref, g_ref, one_ref, two_ref, w_ref, avg_ref, one_out, two_out, w_out, avg_out, low_out):
    one, two, weight, moving = adam_update(
        g_ref[...] * clip_ref[0], one_ref[...], two_ref[...], w_ref[...], avg_ref[...], RATE_MATRIX, DECAY_WEIGHT
    )
    one_out[...] = one
    two_out[...] = two
    w_out[...] = weight
    avg_out[...] = moving
    low_out[...] = weight.astype(bf16)


def adam_update(gradient, first_moment, second_moment, weight, moving, rate, decay):
    first_new = BETA_ONE * first_moment + (1.0 - BETA_ONE) * gradient
    second_new = BETA_TWO * second_moment + (1.0 - BETA_TWO) * gradient * gradient
    corr_one = 1.0 - BETA_ONE**STEP
    corr_two = 1.0 - BETA_TWO**STEP
    step_dir = first_new / corr_one / (jnp.sqrt(second_new / corr_two) + ADAM_EPS)
    weight_new = weight - rate * (step_dir + decay * weight)
    moving_new = EMA_DECAY * moving + (1.0 - EMA_DECAY) * weight_new
    return (first_new, second_new, weight_new, moving_new)


def call(kernel, grid, in_specs, out_specs, out_shape, args, scratch=(), prefetch=0, flops=0, moved=0):
    return pl.pallas_call(
        kernel,
        grid_spec=pltpu.PrefetchScalarGridSpec(
            num_scalar_prefetch=prefetch, grid=grid, in_specs=in_specs, out_specs=out_specs, scratch_shapes=scratch
        ),
        out_shape=out_shape,
        compiler_params=pltpu.CompilerParams(dimension_semantics=("arbitrary",) * len(grid), vmem_limit_bytes=VMEM),
        cost_estimate=pl.CostEstimate(flops=flops, bytes_accessed=moved, transcendentals=0),
    )(*args)


def whole(shape):
    return pl.BlockSpec(shape, lambda *_: (0,) * len(shape))


def pair(rows, first=0):
    return pl.BlockSpec((rows, LANES), lambda j, *_: (0, first + j))


def pairs(count, rows, at=0):
    return pl.BlockSpec((count, rows, LANES), lambda j, *_: (at, 0, j))


def shape_of(shape, dtype):
    return jax.ShapeDtypeStruct(shape, dtype)


def shifted(x, by):
    count = lax.axis_size("img")
    return lax.ppermute(x, "img", [(i + by, i) for i in range(count) if 0 <= i + by < count])


def crossed(x, bit):
    count = lax.axis_size("img")
    return lax.ppermute(x, "img", [(i, i ^ bit) for i in range(count)])


def other_txt(x):
    return lax.ppermute(x, "txt", [(0, 1), (1, 0)])


def neighbourhood(x, low_edge, high_edge):
    beside = crossed(x, 1)
    across = crossed(x, 2)
    above, below = shifted(x, 4), shifted(x, -4)
    low, high = shifted(low_edge, -5), shifted(high_edge, 5)
    above_across, below_across = shifted(across, 4), shifted(across, -4)
    three = crossed(jnp.concatenate([across, above, below], axis=0), 1)
    two = crossed(jnp.concatenate([above_across, below_across], axis=0), 1)
    return [x, beside, across, above, below, three, above_across, below_across, two, low, high]


def index_bits(count):
    bits = count.bit_length() - 1
    assert count == 1 << bits
    return bits


def sum_over_img(x):
    for bit in range(index_bits(lax.axis_size("img"))):
        x = x + crossed(x, 1 << bit)
    return x


def sum_over_all(x):
    x = sum_over_img(x)
    return x + other_txt(x)


def own_and_other(x, bit):
    mine = (lax.axis_index("img") >> bit) & 1
    split = x.reshape(x.shape[0] // 2, 2, *x.shape[1:])
    own = lax.dynamic_index_in_dim(split, mine, 1, keepdims=False)
    other = lax.dynamic_index_in_dim(split, 1 - mine, 1, keepdims=False)
    return own, other


def halved(x, bit, sent_as):
    own, other = own_and_other(x, bit)
    return own + crossed(other.astype(sent_as), 1 << bit).astype(f32)


def scatter_sum(x, sent_as):
    count = lax.axis_size("img")
    x = x.reshape(count, x.shape[0] // count, x.shape[1])
    for bit in range(index_bits(count)):
        x = halved(x, bit, sent_as)
    return x[0]


def gather_doubling(x):
    for axis, bit in enumerate(reversed(range(index_bits(lax.axis_size("img"))))):
        mine = (lax.axis_index("img") >> bit) & 1
        got = crossed(x, 1 << bit)
        x = jnp.where(mine == 0, jnp.stack([x, got], axis), jnp.stack([got, x], axis))
    return x.reshape(-1, x.shape[-1])


def weight_gradient(left, right):
    count = lax.axis_size("img")
    bits = index_bits(count)
    tall = left.T.reshape(count, left.shape[1] // count, left.shape[0])
    rows, width = tall.shape[1], right.shape[1]

    def terms(chunks):
        return mm(chunks.reshape(-1, chunks.shape[2]), right, 1, 0).reshape(chunks.shape[0], rows, width)

    own, other = own_and_other(tall, 0)
    got = crossed(terms(other).astype(bf16), 1)
    own, other = own_and_other(own, 1)
    got_own, got_other = own_and_other(got, 1)
    got = crossed((terms(other) + got_other.astype(f32)).astype(bf16), 2)
    total = terms(own) + got_own.astype(f32) + got.astype(f32)
    for bit in range(2, bits):
        total = halved(total, bit, bf16)
    return total[0]


PIECE_COUNTS = (1, 1, 1, 1, 1, 3, 1, 1, 2, 1, 1)


def neighbour_indices(i):
    b = i ^ 1
    return [
        i, b, i ^ 2, i + 4, i - 4, b ^ 2, b + 4, b - 4, (i ^ 2) + 4, (i ^ 2) - 4, (b ^ 2) + 4, (b ^ 2) - 4, i - 5, i + 5
    ]


def token_places(row_index, image_sides):
    heights = image_sides[:, 0]
    widths = image_sides[:, 1]
    lengths = heights * (widths + 1)
    sample_ends = jnp.cumsum(lengths, dtype=jnp.int32)
    starts = sample_ends - lengths
    sample_ids = ids_of(row_index, sample_ends)
    matched = jnp.arange(image_sides.shape[0], dtype=jnp.int32)[None, :] == sample_ids[:, None]
    first_row = jnp.sum(jnp.where(matched, starts[None, :], 0), axis=1, dtype=jnp.int32)
    row_width = jnp.sum(jnp.where(matched, widths[None, :] + 1, 0), axis=1, dtype=jnp.int32)
    row_width = jnp.maximum(row_width, 1)
    offset = row_index - first_row
    return (sample_ids, offset // row_width, offset % row_width, sample_ends)


def ids_of(rows, sample_ends):
    return jnp.sum((sample_ends <= rows[..., None]).astype(jnp.int32), axis=-1, dtype=jnp.int32)


def turn_tables(row_pos, col_pos):
    quarter = HD // 4
    frequency = 10000.0 ** (-jnp.arange(quarter, dtype=f32) / quarter)
    angles = jnp.concatenate(
        [row_pos.astype(f32)[:, None] * frequency[None, :], col_pos.astype(f32)[:, None] * frequency[None, :]], axis=1
    )
    cosine, sine = jnp.cos(angles), jnp.sin(angles)
    return jnp.concatenate([cosine] * 4, axis=1), jnp.concatenate([-sine, sine, -sine, sine], axis=1)


def rms_norm(values):
    return values * lax.rsqrt(jnp.mean(values * values, axis=-1, keepdims=True) + EPS_NORM)


def rms_back(values, d_normed):
    inverse = lax.rsqrt(jnp.mean(values * values, axis=-1, keepdims=True) + EPS_NORM)
    normed = values * inverse
    return inverse * (d_normed - normed * jnp.mean(d_normed * normed, axis=-1, keepdims=True))


def on_device(
    tokens, cotangent, text_states, conditions, image_sides, master, moment_one, moment_two, average,
    small_master, small_one, small_two, small_average,
):
    n_img = lax.axis_size("img")
    n_txt = lax.axis_size("txt")
    img_index = lax.axis_index("img")
    txt_index = lax.axis_index("txt")
    tok = tokens.shape[0]
    samples = image_sides.shape[0]
    half_d = D // n_txt
    half_ff = FF // n_txt
    local_heads = half_d // HD
    n_pairs = half_d // LANES

    tables = [
        (D // n_img, 2 * half_ff),
        (half_ff // n_img, D),
        (D // n_img, 3 * half_d),
        (TXT_D // n_img, 2 * half_d),
        (half_d // n_img, D),
        (COND // n_img, 6 * half_d),
    ]
    master_lines = master.reshape(-1, LANES)
    lines = master_lines.shape[0]
    starts = [0]
    for rows, columns in tables:
        starts.append(starts[-1] + rows * columns // LANES)

    def own_rows(*which):
        shapes = [tables[w] for w in which]
        return pl.pallas_call(
            functools.partial(unflatten_kernel, shapes),
            out_shape=[shape_of(s, bf16) for s in shapes],
            compiler_params=pltpu.CompilerParams(vmem_limit_bytes=VMEM),
        )(*(master_lines[starts[w] : starts[w + 1]] for w in which))

    (own_project,) = own_rows(2)
    own_modulate, own_text = own_rows(5, 3)
    own_updown, own_down, own_output = own_rows(0, 1, 4)

    def gather(rows):
        return lax.all_gather(rows, "img", axis=0, tiled=True)

    w_project = gather(own_project)

    gain_attn = small_master[:D]
    gain_ffn = small_master[D : 2 * D]
    gain_query = small_master[2 * D : 2 * D + HD]
    gain_key = small_master[2 * D + HD : 2 * D + 2 * HD]
    gain_text = small_master[2 * D + 2 * HD : 2 * D + 3 * HD]
    gate_heads = small_master[2 * D + 3 * HD :]
    gate_local = lax.dynamic_slice_in_dim(gate_heads, txt_index * local_heads, local_heads)
    tanh_gate = jnp.tanh(gate_local)
    gate_lanes = jnp.repeat(tanh_gate, HD)[None, :]
    gain_query_pair = jnp.tile(gain_query, 2)[None, :]
    gain_key_pair = jnp.tile(gain_key, 2)[None, :]

    cond_rows = COND // n_img
    cond_own = lax.dynamic_slice_in_dim(conditions, img_index * cond_rows, cond_rows, 1)
    silu_own = jax.nn.silu(cond_own.astype(f32)).astype(bf16)
    mod_half = sum_over_img(jnp.dot(silu_own, own_modulate, preferred_element_type=f32)).astype(bf16)
    mods = lax.all_gather(mod_half.reshape(samples, 6, half_d), "txt", axis=2, tiled=True)

    row_index = img_index * tok + jnp.arange(tok, dtype=jnp.int32)
    sample_ids, row_pos, col_pos, sample_ends = token_places(row_index, image_sides)
    cosine, sine = turn_tables(row_pos, col_pos)
    one_hot = sample_ids[:, None] == jnp.arange(samples, dtype=jnp.int32)[None, :]
    per_token = jnp.dot(one_hot.astype(bf16), mods.reshape(samples, 6 * D), preferred_element_type=f32).astype(bf16)
    shift_one, scale_one, gate_one, shift_two, scale_two, gate_two = (
        per_token[:, c * D : (c + 1) * D].astype(f32) for c in range(6)
    )

    pieces = jnp.stack([jnp.asarray(p, jnp.int32) for p in neighbour_indices(img_index)])
    place = img_index % 4
    inside = (pieces >= 0) & (pieces < n_img)
    slots = jnp.arange(PIECES)
    inside &= (slots != PIECES - 2) | (place == 0)
    inside &= (slots != PIECES - 1) | (place == 3)
    column = jnp.arange(tok, dtype=jnp.int32)[None, :]
    piece_rows = pieces[:, None] * tok + column + jnp.where(slots == PIECES - 2, tok - EDGE, 0)[:, None]
    there = inside[:, None] & ((slots[:, None] < PIECES - 2) | (column < EDGE))
    piece_ids = jnp.where(there, ids_of(piece_rows, sample_ends), -1)
    flags = jnp.any((piece_ids >= sample_ids[0]) & (piece_ids <= sample_ids[-1]), axis=1).astype(jnp.int32)
    piece_ids = jnp.concatenate([piece_ids, jnp.full((16 - PIECES, tok), -1, jnp.int32)], axis=0)
    own_ids = sample_ids[:, None]

    text_rows = text_states.shape[0]
    text_len = text_rows * n_img
    text_columns = lax.all_to_all(text_states, "img", split_axis=1, concat_axis=0, tiled=True)
    text_proj = scatter_sum(jnp.dot(text_columns, own_text, preferred_element_type=f32), f32)
    text_shape = (text_rows, local_heads, HD)
    text_raw = text_proj[:, :half_d].reshape(text_shape)
    text_normed = rms_norm(text_raw)
    text_key_low = (text_normed * gain_text).reshape(text_rows, half_d).astype(bf16)
    text_low = jnp.concatenate([text_key_low, text_proj[:, half_d:].astype(bf16)], axis=1)
    all_text = gather_doubling(text_low)

    x_float = tokens.astype(f32)
    x_normed = rms_norm(x_float)
    normed_one = x_normed * gain_attn
    attn_in = (normed_one * (1.0 + scale_one) + shift_one).astype(bf16)
    queries, own_kv, raw_qk = call(
        project_kernel,
        (n_pairs,),
        [whole((tok, D)), pair(D), pair(D, n_pairs), pair(D, 2 * n_pairs)]
        + [whole((1, LANES))] * 2
        + [whole((tok, LANES))] * 2,
        [pair(tok), pairs(2, tok), pairs(2, tok)],
        [
            shape_of((tok, half_d), bf16),
            shape_of((2, tok, half_d), bf16),
            shape_of((2, tok, half_d), f32),
        ],
        (attn_in, w_project, w_project, w_project, gain_query_pair, gain_key_pair, cosine, sine),
        flops=2 * tok * D * 3 * half_d,
        moved=2 * D * 3 * half_d,
    )
    kv_pieces = neighbourhood(own_kv, own_kv[:, tok - EDGE :], own_kv[:, :EDGE])

    w_output = gather(own_output)
    w_updown = gather(own_updown)
    w_down = gather(own_down)
    w_output_other = other_txt(w_output)

    kv_specs = [pairs(2 * c, a.shape[1]) for c, a in zip(PIECE_COUNTS, kv_pieces)]
    id_specs = [whole((tok, 1)), whole((16, tok))]
    text_specs = [pair(text_len), pair(text_len, n_pairs)]
    attention_flops = 2 * 2 * tok * 12 * tok * half_d
    mixed_low, self_out, cross_out, lse_self, lse_cross, query_pack = call(
        functools.partial(attend_kernel, PIECE_COUNTS, tok),
        (n_pairs,),
        [pair(tok)] + id_specs + text_specs + [pair(1)] + kv_specs,
        [pair(tok)] * 5 + [whole((1, tok + PACK, half_d))],
        [shape_of((tok, half_d), bf16)]
        + [shape_of((tok, half_d), f32)] * 4
        + [shape_of((1, tok + PACK, half_d), bf16)],
        (flags, queries, own_ids, piece_ids, all_text, all_text, gate_lanes, *kv_pieces),
        scratch=[
            pltpu.VMEM((PIECES, 2 * tok, tok), f32),
            pltpu.VMEM((2 * tok, LANES), f32),
            pltpu.VMEM((2 * tok, LANES), f32),
            pltpu.VMEM((2 * tok, LANES), f32),
            pltpu.VMEM((PACK, tok), f32),
        ],
        prefetch=1,
        flops=attention_flops,
        moved=13 * 4 * tok * half_d,
    )

    def pack_edges(pack):
        table = pack[:, tok:]
        return (
            jnp.concatenate([pack[:, tok - EDGE : tok], table], axis=1),
            jnp.concatenate([pack[:, :EDGE], table], axis=1),
        )

    query_pieces = neighbourhood(query_pack, *pack_edges(query_pack))

    mixed_other = other_txt(mixed_low)
    attn_out = jnp.dot(mixed_low, w_output, preferred_element_type=f32) + jnp.dot(
        mixed_other, w_output_other, preferred_element_type=f32
    )
    hidden = x_float + gate_one * attn_out
    h_normed = rms_norm(hidden)
    normed_two = h_normed * gain_ffn
    ffn_in = (normed_two * (1.0 + scale_two) + shift_two).astype(bf16)
    gate_up = jnp.dot(ffn_in, w_updown, preferred_element_type=f32)
    gate, up = gate_up[:, :half_ff], gate_up[:, half_ff:]
    sigmoid = jax.nn.sigmoid(gate)
    activated = gate * sigmoid
    hidden_units = (activated * up).astype(bf16)
    branch_part = jnp.dot(hidden_units, w_down, preferred_element_type=f32)
    branch = branch_part + other_txt(branch_part)
    block_out = hidden + gate_two * branch

    d_out = cotangent.astype(f32)
    d_gate_two = d_out * branch
    d_branch = (d_out * gate_two).astype(bf16)
    d_units = mm(d_branch, w_down, 1, 1)
    d_gate = d_units * up * sigmoid * (1.0 + gate * (1.0 - sigmoid))
    d_up = d_units * activated
    d_gate_up = jnp.concatenate([d_gate.astype(bf16), d_up.astype(bf16)], axis=1)
    d_ffn_part = mm(d_gate_up, w_updown, 1, 1).astype(bf16)
    d_ffn_in = d_ffn_part.astype(f32) + other_txt(d_ffn_part).astype(f32)
    grad_down = weight_gradient(hidden_units, d_branch)
    grad_updown = weight_gradient(ffn_in, d_gate_up)

    d_scale_two = d_ffn_in * normed_two
    d_normed_two = d_ffn_in * (1.0 + scale_two)
    d_gain_ffn = jnp.sum(d_normed_two * h_normed, axis=0)
    d_hidden = d_out + rms_back(hidden, d_normed_two * gain_ffn)
    d_gate_one = d_hidden * attn_out
    d_attn = (d_hidden * gate_one).astype(bf16)
    grad_pack, d_cross_low, d_gate_lanes = call(
        functools.partial(mixed_back_kernel, tok),
        (n_pairs,),
        [whole((tok, D)), pl.BlockSpec((LANES, D), lambda j: (j, 0)), pair(tok), pair(tok), pair(1)],
        [whole((1, tok + PACK, half_d)), pair(tok), pair(1)],
        [
            shape_of((1, tok + PACK, half_d), bf16),
            shape_of((tok, half_d), bf16),
            shape_of((1, half_d), f32),
        ],
        (d_attn, w_output, self_out, cross_out, gate_lanes),
        scratch=[pltpu.VMEM((PACK, tok), f32)],
        flops=2 * tok * D * half_d,
        moved=4 * D * half_d,
    )
    grad_pieces = neighbourhood(grad_pack, *pack_edges(grad_pack))
    grad_output = weight_gradient(mixed_low, d_attn)

    turn_specs = [whole((1, LANES)), whole((tok, LANES)), whole((tok, LANES))]
    d_query_raw, d_gain_query, d_text_key, d_text_value = call(
        functools.partial(query_back_kernel, PIECE_COUNTS, tok),
        (n_pairs,),
        [pair(tok)]
        + id_specs
        + text_specs
        + [pairs(1, tok), pair(tok)]
        + [pair(tok)] * 4
        + [pairs(1, tok)]
        + turn_specs
        + kv_specs,
        [pair(tok), pair(1), pair(text_len), pair(text_len)],
        [
            shape_of((tok, half_d), bf16),
            shape_of((1, half_d), f32),
            shape_of((text_len, half_d), f32),
            shape_of((text_len, half_d), f32),
        ],
        (
            flags, queries, own_ids, piece_ids, all_text, all_text, grad_pack, d_cross_low,
            self_out, cross_out, lse_self, lse_cross, raw_qk, gain_query_pair, cosine, sine, *kv_pieces,
        ),
        scratch=[pltpu.VMEM((2 * tok, LANES), f32)],
        prefetch=1,
        flops=attention_flops * 3 // 2,
        moved=13 * 4 * tok * half_d,
    )

    def pack_specs(arrays):
        views = [pairs(c, a.shape[1] - PACK) for c, a in zip(PIECE_COUNTS, arrays)]
        rows = [
            pl.BlockSpec((c, PACK, half_d), lambda j, *_, at=(a.shape[1] - PACK) // PACK: (0, at, 0))
            for c, a in zip(PIECE_COUNTS, arrays)
        ]
        return views + rows

    d_key_raw, d_gain_key, d_value = call(
        functools.partial(key_back_kernel, PIECE_COUNTS, tok),
        (n_pairs,),
        [pairs(2, tok)]
        + id_specs
        + [pairs(1, tok, 1)]
        + turn_specs
        + pack_specs(query_pieces)
        + pack_specs(grad_pieces),
        [pair(tok), pair(1), pair(tok)],
        [
            shape_of((tok, half_d), bf16),
            shape_of((1, half_d), f32),
            shape_of((tok, half_d), bf16),
        ],
        (
            flags, own_kv, own_ids, piece_ids, raw_qk, gain_key_pair, cosine, sine,
            *query_pieces, *query_pieces, *grad_pieces, *grad_pieces,
        ),
        scratch=[pltpu.VMEM((2 * tok, LANES), f32)] * 2,
        prefetch=1,
        flops=attention_flops * 2,
        moved=13 * 4 * tok * half_d,
    )
    d_projected = jnp.concatenate([d_query_raw, d_key_raw, d_value], axis=1)
    grad_project = weight_gradient(attn_in, d_projected)
    d_attn_part = mm(d_projected, w_project, 1, 1)
    d_attn_in = d_attn_part + other_txt(d_attn_part)

    text_own = scatter_sum(jnp.concatenate([d_text_key, d_text_value], axis=1), f32)
    d_text_scaled = text_own[:, :half_d].reshape(text_shape)
    d_gain_text = jnp.sum(d_text_scaled * text_normed, axis=(0, 1))
    d_text_raw = rms_back(text_raw, d_text_scaled * gain_text).reshape(text_rows, half_d)
    d_text_proj = gather_doubling(jnp.concatenate([d_text_raw, text_own[:, half_d:]], axis=1).astype(bf16))
    grad_text = mm(text_columns, d_text_proj, 0, 0)

    d_scale_one = d_attn_in * normed_one
    d_normed_one = d_attn_in * (1.0 + scale_one)
    d_gain_attn = jnp.sum(d_normed_one * x_normed, axis=0)
    d_tokens = d_hidden + rms_back(x_float, d_normed_one * gain_attn)

    one_hot_wide = one_hot.astype(f32)

    def by_sample(values):
        summed = lax.dot_general(one_hot_wide, values, (((0,), (0,)), ((), ())), precision=HIGH)
        return lax.dynamic_slice_in_dim(summed, txt_index * half_d, half_d, 1)

    d_mod_early = sum_over_img(
        jnp.concatenate([by_sample(v) for v in (d_gate_one, d_ffn_in, d_scale_two, d_gate_two)], axis=1)
    )
    d_mod_late = sum_over_img(jnp.concatenate([by_sample(v) for v in (d_attn_in, d_scale_one)], axis=1))
    d_mod = jnp.concatenate([d_mod_late, d_mod_early], axis=1)
    grad_modulate = lax.dot_general(silu_own.astype(f32), d_mod, (((0,), (0,)), ((), ())), precision=HIGH)

    grads = [grad_updown, grad_down, grad_project, grad_text, grad_output, grad_modulate]
    reduced, squares = pl.pallas_call(
        flatten_kernel,
        out_shape=[shape_of((lines, LANES), f32), shape_of((1, LANES), f32)],
        compiler_params=pltpu.CompilerParams(vmem_limit_bytes=VMEM),
    )(*grads)

    replica = (txt_index == 0).astype(f32)
    d_gate_local = jnp.sum(d_gate_lanes.reshape(local_heads, HD), axis=1) * (1.0 - tanh_gate**2)
    gate_full = lax.dynamic_update_slice(jnp.zeros((HEADS,), f32), d_gate_local, (txt_index * local_heads,))
    small_terms = jnp.concatenate(
        [
            d_gain_attn * replica,
            d_gain_ffn * replica,
            jnp.sum(d_gain_query.reshape(local_heads, HD), axis=0),
            jnp.sum(d_gain_key.reshape(local_heads, HD), axis=0),
            d_gain_text,
            gate_full,
        ]
    )
    small_grad = sum_over_all(small_terms)
    square_big = jnp.sum(sum_over_all(squares))
    grad_square = square_big + jnp.sum(small_grad * small_grad)
    clip_factor = MAX_NORM / jnp.maximum(jnp.sqrt(grad_square), MAX_NORM)

    block = math.gcd(lines, 1024)
    line_spec = pl.BlockSpec((block, LANES), lambda i: (i, 0))
    as_lines = (lines, LANES)
    updated = call(
        update_kernel,
        (lines // block,),
        [pl.BlockSpec(memory_space=pltpu.SMEM)] + [line_spec] * 5,
        [line_spec] * 5,
        [shape_of(as_lines, f32)] * 4 + [shape_of(as_lines, bf16)],
        (clip_factor.reshape(1), reduced, *(a.reshape(as_lines) for a in (moment_one, moment_two, master, average))),
        flops=20 * lines * LANES,
        moved=38 * lines * LANES,
    )
    one_new, two_new, master_new, average_new, master_low = (a.reshape(master.shape) for a in updated)
    small_one_new, small_two_new, small_new, small_average_new = adam_update(
        small_grad * clip_factor, small_one, small_two, small_master, small_average, RATE_SMALL, 0.0
    )
    return (
        block_out,
        d_tokens,
        grad_square,
        one_new,
        two_new,
        master_new,
        average_new,
        master_low,
        small_one_new,
        small_two_new,
        small_new,
        small_average_new,
    )


def solution(mesh):
    rows = P("img", None)
    shards = P("img", "txt", None)
    in_specs = (rows, rows, rows, P(), P(), shards, shards, shards, shards, P(), P(), P(), P())
    out_specs = (rows, rows, P(), shards, shards, shards, shards, shards, P(), P(), P(), P())
    return jax.shard_map(on_device, mesh=mesh, in_specs=in_specs, out_specs=out_specs, check_vma=False)
```

```python
import functools
import math

import jax
import jax.numpy as jnp
from jax import lax
from jax.experimental import pallas as pl
from jax.experimental.pallas import tpu as pltpu
from jax.sharding import PartitionSpec as P

D = 1536
HEADS = 24
HD = 64
FF = 4096
TXT_D = 4096
COND = 1024
SIDE_MAX = 32
STEP = 10

HIGH = lax.Precision.HIGHEST
EPS_NORM = 1e-06
MAX_NORM = 1.0
BETA_ONE = 0.5
BETA_TWO = 0.5
RATE_MATRIX = 0.01
RATE_SMALL = 0.1
DECAY_WEIGHT = 0.01
ADAM_EPS = 1e-08
EMA_DECAY = 0.8

LANES = 128
EDGE = 128
PACK = 16
WIDE = 256
PIECES = 13
MASKED = -1e30
MIB = 1024 * 1024

bf16 = jnp.bfloat16
f32 = jnp.float32


def mm(a, b, on_a, on_b):
    return lax.dot_general(a, b, (((on_a,), (on_b,)), ((), ())), preferred_element_type=f32)


def lane_index(rows):
    return lax.broadcasted_iota(jnp.int32, (rows, LANES), 1)


def head_sum(values):
    low = lane_index(values.shape[0]) < HD
    first = jnp.sum(jnp.where(low, values, 0.0), axis=1, keepdims=True)
    second = jnp.sum(jnp.where(low, 0.0, values), axis=1, keepdims=True)
    return jnp.where(low, first, second)


def swap_halves(values):
    first = lane_index(values.shape[0]) % HD < HD // 2
    return jnp.where(
        first, pltpu.roll(values, LANES - HD // 2, 1), pltpu.roll(values, HD // 2, 1)
    )


def two_heads(pair):
    low = lane_index(pair.shape[0]) < HD
    zero = jnp.zeros_like(pair)
    return jnp.concatenate([jnp.where(low, pair, zero), jnp.where(low, zero, pair)], axis=0)


def one_pair(stacked):
    rows = stacked.shape[0] // 2
    low = lane_index(rows) < HD
    return jnp.where(low, stacked[:rows], stacked[rows:])


def columns_of(spread):
    return jnp.concatenate([spread[:, :1], spread[:, HD : HD + 1]], axis=0)


def norm_rope(raw, gain, cosine, sine):
    inverse = lax.rsqrt(head_sum(raw * raw) * (1.0 / HD) + EPS_NORM)
    scaled = raw * inverse * gain
    return scaled * cosine + swap_halves(scaled) * sine


def norm_rope_back(raw, gain, cosine, sine, d_out):
    inverse = lax.rsqrt(head_sum(raw * raw) * (1.0 / HD) + EPS_NORM)
    normed = raw * inverse
    d_scaled = d_out * cosine - swap_halves(d_out) * sine
    d_gain = jnp.sum(d_scaled * normed, axis=0, keepdims=True)
    d_normed = d_scaled * gain
    d_raw = inverse * (d_normed - normed * (head_sum(d_normed * normed) * (1.0 / HD)))
    return d_raw, d_gain


def split_three(values):
    high = values.astype(bf16)
    rest = values - high.astype(f32)
    middle = rest.astype(bf16)
    last = (rest - middle.astype(f32)).astype(bf16)
    return jnp.concatenate([high, middle, last], axis=1)


def joined(packed, rows):
    wide = packed.astype(f32)
    return wide[:, :rows] + wide[:, rows : 2 * rows] + wide[:, 2 * rows : 3 * rows]


def put_row(table, index, row):
    at = lax.broadcasted_iota(jnp.int32, table.shape, 0) == index
    return jnp.where(at, row, table)


def take_row(table, index):
    at = lax.broadcasted_iota(jnp.int32, table.shape, 0) == index
    return jnp.sum(jnp.where(at, table, 0.0), axis=0, keepdims=True)


def as_row(column):
    return jnp.broadcast_to(column, (column.shape[0], LANES)).T[:1]


def project_kernel(a_ref, wq_ref, wk_ref, wv_ref, gq_ref, gk_ref, cos_ref, sin_ref, q_ref, kv_ref, raw_ref):
    a = a_ref[...]
    cosine, sine = cos_ref[...], sin_ref[...]
    raw_q = mm(a, wq_ref[...], 1, 0)
    raw_k = mm(a, wk_ref[...], 1, 0)
    raw_ref[0] = raw_q
    raw_ref[1] = raw_k
    q_ref[...] = norm_rope(raw_q, gq_ref[...], cosine, sine).astype(bf16) * jnp.asarray(HD**-0.5, bf16)
    kv_ref[0] = norm_rope(raw_k, gk_ref[...], cosine, sine).astype(bf16)
    kv_ref[1] = mm(a, wv_ref[...], 1, 0).astype(bf16)


def piece_views(piece_refs, counts, per):
    views = []
    for ref, count in zip(piece_refs, counts):
        for at in range(count):
            views.append((ref, at * per))
    return views


def attend_kernel(counts, tok, flag_ref, q_ref, own_ids_ref, ids_ref, tk_ref, tv_ref, gate_ref, *rest):
    pieces = piece_views(rest[: len(counts)], counts, 2)
    mixed_ref, self_ref, cross_ref, lse_self_ref, lse_cross_ref, pack_ref = rest[len(counts) : len(counts) + 6]
    scores_ref, most_ref, total_ref, acc_ref, table_ref = rest[len(counts) + 6 :]
    step = pl.program_id(0)
    own_ids = own_ids_ref[...]
    q_pair = q_ref[...]
    q_two = two_heads(q_pair)
    own_two = jnp.concatenate([own_ids, own_ids], axis=0)
    most_ref[...] = jnp.full(most_ref.shape, MASKED, f32)
    total_ref[...] = jnp.zeros(total_ref.shape, f32)
    acc_ref[...] = jnp.zeros(acc_ref.shape, f32)
    for slot, (ref, at) in enumerate(pieces):
        rows = ref.shape[1]

        @pl.when(flag_ref[slot] > 0)
        def _(slot=slot, ref=ref, at=at, rows=rows):
            scores = mm(q_two, ref[at], 1, 1)
            scores = jnp.where(own_two == ids_ref[slot : slot + 1, :rows], scores, MASKED)
            scores_ref[slot, :, :rows] = scores
            most = most_ref[...]
            for part in range(rows // LANES):
                most = jnp.maximum(most, scores[:, part * LANES : (part + 1) * LANES])
            most_ref[...] = most

    row_most = jnp.max(most_ref[...], axis=1, keepdims=True)
    for slot, (ref, at) in enumerate(pieces):
        rows = ref.shape[1]

        @pl.when(flag_ref[slot] > 0)
        def _(slot=slot, ref=ref, at=at, rows=rows):
            weights = jnp.exp(scores_ref[slot, :, :rows] - row_most)
            total = total_ref[...]
            for part in range(rows // LANES):
                total = total + weights[:, part * LANES : (part + 1) * LANES]
            total_ref[...] = total
            acc_ref[...] += mm(weights.astype(bf16), ref[at + 1], 1, 0)

    row_total = jnp.sum(total_ref[...], axis=1, keepdims=True)
    self_out = one_pair(acc_ref[...] / row_total)
    lse_self = row_most + jnp.log(row_total)

    cross_scores = mm(q_two, tk_ref[...], 1, 1)
    cross_most = jnp.max(cross_scores, axis=1, keepdims=True)
    cross_weights = jnp.exp(cross_scores - cross_most)
    cross_total = jnp.sum(cross_weights, axis=1, keepdims=True)
    cross_out = one_pair(mm(cross_weights.astype(bf16), tv_ref[...], 1, 0) / cross_total)
    lse_cross = cross_most + jnp.log(cross_total)

    self_ref[...] = self_out
    cross_ref[...] = cross_out
    mixed_ref[...] = (self_out + gate_ref[...] * cross_out).astype(bf16)
    spread = (tok, LANES)
    low = lane_index(tok) < HD
    lse_self_ref[...] = jnp.where(
        low, jnp.broadcast_to(lse_self[:tok], spread), jnp.broadcast_to(lse_self[tok:], spread)
    )
    lse_cross_ref[...] = jnp.where(
        low, jnp.broadcast_to(lse_cross[:tok], spread), jnp.broadcast_to(lse_cross[tok:], spread)
    )

    @pl.when(step == 0)
    def _():
        table_ref[...] = jnp.zeros(table_ref.shape, f32)

    table = put_row(table_ref[...], 2 * step, as_row(lse_self[:tok]))
    table = put_row(table, 2 * step + 1, as_row(lse_self[tok:]))
    table_ref[...] = table
    pack_ref[0, :tok, pl.ds(pl.multiple_of(step * LANES, LANES), LANES)] = q_pair

    @pl.when(step == pl.num_programs(0) - 1)
    def _():
        pack_ref[0, tok:, :] = split_three(table_ref[...])


def mixed_back_kernel(tok, d_attn_ref, w_ref, self_ref, cross_ref, gate_ref, pack_ref, d_cross_ref, d_gate_ref, table_ref):
    step = pl.program_id(0)
    d_mixed = mm(d_attn_ref[...], w_ref[...], 1, 1)
    d_self = d_mixed.astype(bf16)
    d_cross_ref[...] = (gate_ref[...] * d_mixed).astype(bf16)
    d_gate_ref[...] = jnp.sum(d_mixed * cross_ref[...], axis=0, keepdims=True)
    delta = head_sum(d_self.astype(f32) * self_ref[...])

    @pl.when(step == 0)
    def _():
        table_ref[...] = jnp.zeros(table_ref.shape, f32)

    table = put_row(table_ref[...], 2 * step, as_row(delta[:, :1]))
    table = put_row(table, 2 * step + 1, as_row(delta[:, HD : HD + 1]))
    table_ref[...] = table
    pack_ref[0, :tok, pl.ds(pl.multiple_of(step * LANES, LANES), LANES)] = d_self

    @pl.when(step == pl.num_programs(0) - 1)
    def _():
        pack_ref[0, tok:, :] = split_three(table_ref[...])


def query_back_kernel(
    counts, tok, flag_ref, q_ref, own_ids_ref, ids_ref, tk_ref, tv_ref, d_self_ref, d_cross_ref,
    self_ref, cross_ref, lse_self_ref, lse_cross_ref, raw_ref, gain_ref, cos_ref, sin_ref, *rest
):
    pieces = piece_views(rest[: len(counts)], counts, 2)
    d_raw_ref, d_gain_ref, d_tk_ref, d_tv_ref, acc_ref = rest[len(counts) :]
    own_ids = own_ids_ref[...]
    own_two = jnp.concatenate([own_ids, own_ids], axis=0)
    q_two = two_heads(q_ref[...])
    d_self = d_self_ref[0]
    d_self_two = two_heads(d_self)
    delta = columns_of(head_sum(d_self.astype(f32) * self_ref[...]))
    lse = columns_of(lse_self_ref[...])

    d_cross = d_cross_ref[...]
    d_cross_two = two_heads(d_cross)
    delta_cross = columns_of(head_sum(d_cross.astype(f32) * cross_ref[...]))
    lse_cross = columns_of(lse_cross_ref[...])
    cross_p = jnp.exp(mm(q_two, tk_ref[...], 1, 1) - lse_cross)
    d_cross_p = mm(d_cross_two, tv_ref[...], 1, 1)
    d_cross_s = (cross_p * (d_cross_p - delta_cross)).astype(bf16)
    d_tv_ref[...] = mm(cross_p.astype(bf16), d_cross_two, 0, 0)
    d_tk_ref[...] = mm(d_cross_s, q_two, 0, 0)
    acc_ref[...] = mm(d_cross_s, tk_ref[...], 1, 0)
    for slot, (ref, at) in enumerate(pieces):
        rows = ref.shape[1]

        @pl.when(flag_ref[slot] > 0)
        def _(slot=slot, ref=ref, at=at, rows=rows):
            key = ref[at]
            scores = mm(q_two, key, 1, 1)
            scores = jnp.where(own_two == ids_ref[slot : slot + 1, :rows], scores, MASKED)
            weights = jnp.exp(scores - lse)
            d_weights = mm(d_self_two, ref[at + 1], 1, 1)
            d_scores = (weights * (d_weights - delta)).astype(bf16)
            acc_ref[...] += mm(d_scores, key, 1, 0)

    d_query = one_pair(acc_ref[...]) * (HD**-0.5)
    d_raw, d_gain = norm_rope_back(raw_ref[0], gain_ref[...], cos_ref[...], sin_ref[...], d_query)
    d_raw_ref[...] = d_raw.astype(bf16)
    d_gain_ref[...] = d_gain


def key_back_kernel(counts, tok, flag_ref, kv_ref, own_ids_ref, ids_ref, raw_ref, gain_ref, cos_ref, sin_ref, *rest):
    n = len(counts)
    q_views = piece_views(rest[:n], counts, 1)
    q_tables = piece_views(rest[n : 2 * n], counts, 1)
    g_views = piece_views(rest[2 * n : 3 * n], counts, 1)
    g_tables = piece_views(rest[3 * n : 4 * n], counts, 1)
    d_raw_ref, d_gain_ref, d_value_ref, acc_k_ref, acc_v_ref = rest[4 * n :]
    step = pl.program_id(0)
    own_ids = own_ids_ref[...]
    k_two = two_heads(kv_ref[0])
    v_two = two_heads(kv_ref[1])
    acc_k_ref[...] = jnp.zeros(acc_k_ref.shape, f32)
    acc_v_ref[...] = jnp.zeros(acc_v_ref.shape, f32)
    for slot in range(PIECES):
        q_ref, at = q_views[slot]
        rows = q_ref.shape[1]
        @pl.when(flag_ref[slot] > 0)
        def _(slot=slot, q_ref=q_ref, at=at, rows=rows):
            query = q_ref[at]
            d_self = g_views[slot][0][at]
            lse = joined(q_tables[slot][0][at], tok)[:, :rows]
            delta = joined(g_tables[slot][0][at], tok)[:, :rows]
            same = own_ids == ids_ref[slot : slot + 1, :rows]
            scores = mm(k_two, query, 1, 1)
            d_weights = mm(v_two, d_self, 1, 1)
            p_low, d_low = [], []
            for head in range(2):
                part = slice(head * tok, (head + 1) * tok)
                masked = jnp.where(same, scores[part], MASKED)
                weights = jnp.exp(masked - take_row(lse, 2 * step + head))
                p_low.append(weights.astype(bf16))
                d_low.append((weights * (d_weights[part] - take_row(delta, 2 * step + head))).astype(bf16))
            acc_v_ref[...] += mm(jnp.concatenate(p_low, axis=0), d_self, 1, 0)
            acc_k_ref[...] += mm(jnp.concatenate(d_low, axis=0), query, 1, 0)

    d_raw, d_gain = norm_rope_back(
        raw_ref[0], gain_ref[...], cos_ref[...], sin_ref[...], one_pair(acc_k_ref[...])
    )
    d_raw_ref[...] = d_raw.astype(bf16)
    d_gain_ref[...] = d_gain
    d_value_ref[...] = one_pair(acc_v_ref[...]).astype(bf16)


def unflatten_kernel(tables, *refs):
    for (rows, columns), lines_ref, out_ref in zip(tables, refs, refs[len(tables) :]):
        per_row = columns // LANES
        for at in range(per_row):
            out_ref[:, at * LANES : (at + 1) * LANES] = lines_ref[pl.ds(at, rows, stride=per_row), :].astype(bf16)


def pack_kernel(tables, *refs):
    *lines_refs, out_ref = refs
    top = 0
    for (rows, columns), lines_ref in zip(tables, lines_refs):
        per_row = columns // LANES
        for at in range(per_row):
            row = top + at // (WIDE // LANES) * rows
            lane = at % (WIDE // LANES) * LANES
            out_ref[row : row + rows, lane : lane + LANES] = lines_ref[pl.ds(at, rows, stride=per_row), :].astype(bf16)
        top += columns // WIDE * rows


def unpack_kernel(tables, block_ref, *out_refs):
    top = 0
    for (rows, columns), out_ref in zip(tables, out_refs):
        for at in range(columns // WIDE):
            out_ref[:, at * WIDE : (at + 1) * WIDE] = block_ref[0, top : top + rows, :]
            top += rows


def flatten_kernel(places, *refs):
    *grad_refs, lines_ref, square_ref = refs
    square = jnp.zeros((1, LANES), f32)
    for (start, column, columns), ref in zip(places, grad_refs):
        for at in range(ref.shape[1] // LANES):
            part = ref[:, at * LANES : (at + 1) * LANES]
            lines_ref[pl.ds(start + column // LANES + at, ref.shape[0], stride=columns // LANES), :] = part
            square = square + jnp.sum(part * part, axis=0, keepdims=True)
    square_ref[...] = square


def update_kernel(clip_ref, g_ref, one_ref, two_ref, w_ref, avg_ref, one_out, two_out, w_out, avg_out, low_out):
    one, two, weight, moving = adam_update(
        g_ref[...] * clip_ref[0], one_ref[...], two_ref[...], w_ref[...], avg_ref[...], RATE_MATRIX, DECAY_WEIGHT
    )
    one_out[...] = one
    two_out[...] = two
    w_out[...] = weight
    avg_out[...] = moving
    low_out[...] = weight.astype(bf16)


def adam_update(gradient, first_moment, second_moment, weight, moving, rate, decay):
    first_new = BETA_ONE * first_moment + (1.0 - BETA_ONE) * gradient
    second_new = BETA_TWO * second_moment + (1.0 - BETA_TWO) * gradient * gradient
    corr_one = 1.0 - BETA_ONE**STEP
    corr_two = 1.0 - BETA_TWO**STEP
    step_dir = first_new / corr_one / (jnp.sqrt(second_new / corr_two) + ADAM_EPS)
    weight_new = weight - rate * (step_dir + decay * weight)
    moving_new = EMA_DECAY * moving + (1.0 - EMA_DECAY) * weight_new
    return (first_new, second_new, weight_new, moving_new)


def call(kernel, grid, in_specs, out_specs, out_shape, args, scratch=(), prefetch=0, flops=0, moved=0, vmem=16):
    return pl.pallas_call(
        kernel,
        grid_spec=pltpu.PrefetchScalarGridSpec(
            num_scalar_prefetch=prefetch, grid=grid, in_specs=in_specs, out_specs=out_specs, scratch_shapes=scratch
        ),
        out_shape=out_shape,
        compiler_params=pltpu.CompilerParams(dimension_semantics=("arbitrary",) * len(grid), vmem_limit_bytes=vmem * MIB),
        cost_estimate=pl.CostEstimate(flops=flops, bytes_accessed=moved, transcendentals=0),
    )(*args)


def whole(shape):
    return pl.BlockSpec(shape, lambda *_: (0,) * len(shape))


def pair(rows, first=0):
    return pl.BlockSpec((rows, LANES), lambda j, *_: (0, first + j))


def pairs(count, rows, at=0):
    return pl.BlockSpec((count, rows, LANES), lambda j, *_: (at, 0, j))


def shape_of(shape, dtype):
    return jax.ShapeDtypeStruct(shape, dtype)


def shifted(x, by):
    count = lax.axis_size("img")
    return lax.ppermute(x, "img", [(i + by, i) for i in range(count) if 0 <= i + by < count])


def crossed(x, bit):
    count = lax.axis_size("img")
    return lax.ppermute(x, "img", [(i, i ^ bit) for i in range(count)])


def other_txt(x):
    return lax.ppermute(x, "txt", [(0, 1), (1, 0)])


def index_bits(count):
    bits = count.bit_length() - 1
    assert count == 1 << bits
    return bits


def sum_over_img(x):
    for bit in range(index_bits(lax.axis_size("img"))):
        x = x + crossed(x, 1 << bit)
    return x


def sum_over_all(x):
    x = sum_over_img(x)
    return x + other_txt(x)


def own_and_other(x, bit, below=1):
    mine = (lax.axis_index("img") >> bit) & 1
    split = x.reshape(x.shape[0] // (2 * below), 2, below, *x.shape[1:])
    own = lax.dynamic_index_in_dim(split, mine, 1, keepdims=False)
    other = lax.dynamic_index_in_dim(split, 1 - mine, 1, keepdims=False)
    return own.reshape(-1, *x.shape[1:]), other.reshape(-1, *x.shape[1:])


class TermSum:
    def __init__(self, clock, terms, order):
        count = lax.axis_size("img")
        self.clock, self.order, self.level = clock, order, 0
        self.keep = clock.stage(terms).reshape(count, terms.shape[0] // count, terms.shape[1])
        self.send()

    def send(self):
        bit = self.order[self.level]
        below = 1 << sum(other < bit for other in self.order[self.level :])
        self.keep, self.sent = own_and_other(self.keep, bit, below)
        self.clock.mark(self.sent)

    def advance(self):
        got = self.clock.stage(crossed(self.sent, 1 << self.order[self.level]))
        self.keep = self.keep + got
        self.level += 1
        if self.level == len(self.order):
            self.clock.mark(self.keep)
            return self.keep[0]
        self.send()

    def finish(self):
        while True:
            result = self.advance()
            if result is not None:
                return result


def gather_doubling(x):
    x = x[None]
    for bit in reversed(range(index_bits(lax.axis_size("img")))):
        x = doubled(x, bit)
    return x.reshape(-1, x.shape[-1])


def doubled(x, bit):
    mine = (lax.axis_index("img") >> bit) & 1
    got = crossed(x, 1 << bit)
    both = jnp.where(mine == 0, jnp.stack([x, got], 1), jnp.stack([got, x], 1))
    return both.reshape(-1, *x.shape[1:])


def tie(x, *others):
    return lax.optimization_barrier((x, others))[0]


def tall(left):
    count = lax.axis_size("img")
    return left.T.reshape(count, left.shape[1] // count, left.shape[0])


class Clock:
    def __init__(self):
        self.token = ()

    def stage(self, *arrays):
        arrays, _ = lax.optimization_barrier((arrays, self.token))
        return arrays if len(arrays) > 1 else arrays[0]

    def mark(self, *arrays):
        self.token = arrays


class GradientSum:
    def __init__(self, clock, left, right):
        bits = index_bits(left.shape[0])
        self.order = list(range(bits))
        self.level = 0
        self.clock = clock
        left, self.right = clock.stage(left, right)
        self.own, other = own_and_other(left, 0)
        self.sent = self.terms(other).astype(bf16)
        clock.mark(self.sent)

    def terms(self, chunks):
        product = mm(chunks.reshape(-1, chunks.shape[2]), self.right, 1, 0)
        return product.reshape(chunks.shape[0], chunks.shape[1], self.right.shape[1])

    def receive(self):
        self.got = self.clock.stage(crossed(self.sent, 1 << self.order[self.level]))
        self.clock.mark(self.got)
        self.level += 1

    def advance(self, received=False):
        if not received:
            self.receive()
        got = self.clock.stage(self.got)
        if self.level == len(self.order):
            return (self.keep + got.astype(f32))[0]
        bit = self.order[self.level]
        if self.level == 1:
            own, other = own_and_other(self.own, bit)
            got_own, got_other = own_and_other(got, bit)
            self.sent = (self.terms(other) + got_other.astype(f32)).astype(bf16)
            self.keep = self.terms(own) + got_own.astype(f32)
        else:
            own, other = own_and_other(self.keep + got.astype(f32), bit)
            self.sent, self.keep = other.astype(bf16), own
        self.clock.mark(self.sent)
        return self.sent


class Neighbourhood:
    def __init__(self, clock, x, end, beginning):
        count = lax.axis_size("img")
        self.clock = clock
        self.x = x
        self.across = crossed(x, 2)
        self.above, self.below = shifted(x, 4), shifted(x, -4)
        edge = jnp.where(lax.axis_index("img") % 4 == 3, end, beginning)
        pairs_low = [(i - 5, i) for i in range(0, count, 4) if i >= 5]
        pairs_high = [(i + 5, i) for i in range(3, count, 4) if i + 5 < count]
        self.edge = lax.ppermute(edge, "img", pairs_low + pairs_high)

    def second(self):
        across, above, below = self.clock.stage(self.across, self.above, self.below)
        self.across, self.above, self.below = across, above, below
        self.four_sent = jnp.concatenate([self.x, across, above, below], axis=0)
        self.above_across, self.below_across = shifted(across, 4), shifted(across, -4)
        self.clock.mark(self.four_sent)

    def third(self):
        four = crossed(self.four_sent, 1)
        self.above_across, self.below_across, self.four, self.edge = self.clock.stage(
            self.above_across, self.below_across, four, self.edge
        )
        self.two_sent = jnp.concatenate([self.above_across, self.below_across], axis=0)
        self.clock.mark(self.two_sent)

    def collect(self):
        two = self.clock.stage(crossed(self.two_sent, 1))
        self.clock.mark(two)
        return [self.x, self.across, self.above, self.below, self.four, self.above_across, self.below_across, two, self.edge]


PIECE_COUNTS = (1, 1, 1, 1, 4, 1, 1, 2, 1)


def neighbour_indices(i):
    b = i ^ 1
    edge = jnp.where(i % 4 == 0, i - 5, i + 5)
    return [i, i ^ 2, i + 4, i - 4, b, b ^ 2, b + 4, b - 4, (i ^ 2) + 4, (i ^ 2) - 4, (b ^ 2) + 4, (b ^ 2) - 4, edge]


def token_places(row_index, image_sides):
    heights = image_sides[:, 0]
    widths = image_sides[:, 1]
    lengths = heights * (widths + 1)
    sample_ends = jnp.cumsum(lengths, dtype=jnp.int32)
    starts = sample_ends - lengths
    sample_ids = ids_of(row_index, sample_ends)
    matched = jnp.arange(image_sides.shape[0], dtype=jnp.int32)[None, :] == sample_ids[:, None]
    first_row = jnp.sum(jnp.where(matched, starts[None, :], 0), axis=1, dtype=jnp.int32)
    row_width = jnp.sum(jnp.where(matched, widths[None, :] + 1, 0), axis=1, dtype=jnp.int32)
    row_width = jnp.maximum(row_width, 1)
    offset = row_index - first_row
    return (sample_ids, offset // row_width, offset % row_width, sample_ends)


def ids_of(rows, sample_ends):
    return jnp.sum((sample_ends <= rows[..., None]).astype(jnp.int32), axis=-1, dtype=jnp.int32)


def turn_tables(row_pos, col_pos):
    quarter = HD // 4
    frequency = 10000.0 ** (-jnp.arange(quarter, dtype=f32) / quarter)
    angles = jnp.concatenate(
        [row_pos.astype(f32)[:, None] * frequency[None, :], col_pos.astype(f32)[:, None] * frequency[None, :]], axis=1
    )
    cosine, sine = jnp.cos(angles), jnp.sin(angles)
    return jnp.concatenate([cosine] * 4, axis=1), jnp.concatenate([-sine, sine, -sine, sine], axis=1)


def rms_norm(values):
    return values * lax.rsqrt(jnp.mean(values * values, axis=-1, keepdims=True) + EPS_NORM)


def rms_back(values, d_normed):
    inverse = lax.rsqrt(jnp.mean(values * values, axis=-1, keepdims=True) + EPS_NORM)
    normed = values * inverse
    return inverse * (d_normed - normed * jnp.mean(d_normed * normed, axis=-1, keepdims=True))


def on_device(
    tokens, cotangent, text_states, conditions, image_sides, master, moment_one, moment_two, average,
    small_master, small_one, small_two, small_average,
):
    n_img = lax.axis_size("img")
    n_txt = lax.axis_size("txt")
    img_index = lax.axis_index("img")
    txt_index = lax.axis_index("txt")
    tok = tokens.shape[0]
    samples = image_sides.shape[0]
    half_d = D // n_txt
    half_ff = FF // n_txt
    local_heads = half_d // HD
    n_pairs = half_d // LANES

    tables = [
        (D // n_img, 2 * half_ff),
        (half_ff // n_img, D),
        (D // n_img, 3 * half_d),
        (TXT_D // n_img, 2 * half_d),
        (half_d // n_img, D),
        (COND // n_img, 6 * half_d),
    ]
    master_lines = master.reshape(-1, LANES)
    lines = master_lines.shape[0]
    starts = [0]
    for rows, columns in tables:
        starts.append(starts[-1] + rows * columns // LANES)

    def own_rows(*which):
        shapes = [tables[w] for w in which]
        return pl.pallas_call(
            functools.partial(unflatten_kernel, shapes),
            out_shape=[shape_of(s, bf16) for s in shapes],
            compiler_params=pltpu.CompilerParams(vmem_limit_bytes=32 * MIB),
        )(*(master_lines[starts[w] : starts[w + 1]] for w in which))

    def gather(rows):
        return lax.all_gather(rows, "img", axis=0, tiled=True)

    together = [0, 1, 4, 2]
    shapes = [tables[w] for w in together]
    heights = [rows * columns // WIDE for rows, columns in shapes]
    if all(rows % 16 == 0 for rows, _ in shapes) and sum(heights[:3]) % heights[3] == 0:
        block = pl.pallas_call(
            functools.partial(pack_kernel, shapes),
            out_shape=shape_of((sum(heights), WIDE), bf16),
            compiler_params=pltpu.CompilerParams(vmem_limit_bytes=32 * MIB),
        )(*(master_lines[starts[w] : starts[w + 1]] for w in together))
        blocks = gather(block[None])

        def unpack(which, height, at, gathered):
            return call(
                functools.partial(unpack_kernel, which),
                (n_img,),
                [pl.BlockSpec((1, height, WIDE), lambda i: (i, at, 0))],
                [pl.BlockSpec(shape, lambda i: (i, 0)) for shape in which],
                [shape_of((n_img * rows, columns), bf16) for rows, columns in which],
                (gathered,),
                vmem=52,
            )

    else:
        blocks = None
        w_project = gather(own_rows(2)[0])
    (own_modulate,) = own_rows(5)
    (own_text,) = own_rows(3)

    gain_attn = small_master[:D]
    gain_ffn = small_master[D : 2 * D]
    gain_query = small_master[2 * D : 2 * D + HD]
    gain_key = small_master[2 * D + HD : 2 * D + 2 * HD]
    gain_text = small_master[2 * D + 2 * HD : 2 * D + 3 * HD]
    gate_heads = small_master[2 * D + 3 * HD :]
    gate_local = lax.dynamic_slice_in_dim(gate_heads, txt_index * local_heads, local_heads)
    tanh_gate = jnp.tanh(gate_local)
    gate_lanes = jnp.repeat(tanh_gate, HD)[None, :]
    gain_query_pair = jnp.tile(gain_query, 2)[None, :]
    gain_key_pair = jnp.tile(gain_key, 2)[None, :]

    cond_rows = COND // n_img
    cond_own = lax.dynamic_slice_in_dim(conditions, img_index * cond_rows, cond_rows, 1)
    silu_own = jax.nn.silu(cond_own.astype(f32)).astype(bf16)
    mod_sum = sum_over_img(jnp.dot(silu_own, own_modulate, preferred_element_type=f32))
    mod_half = mod_sum.astype(bf16)
    mod_other = other_txt(mod_half)
    mods = jnp.where(
        txt_index == 0, jnp.stack([mod_half, mod_other], 0), jnp.stack([mod_other, mod_half], 0)
    ).reshape(n_txt, samples, 6, half_d).transpose(1, 2, 0, 3)

    row_index = img_index * tok + jnp.arange(tok, dtype=jnp.int32)
    sample_ids, row_pos, col_pos, sample_ends = token_places(row_index, image_sides)
    cosine, sine = turn_tables(row_pos, col_pos)
    one_hot = sample_ids[:, None] == jnp.arange(samples, dtype=jnp.int32)[None, :]
    per_token = jnp.dot(one_hot.astype(bf16), mods.reshape(samples, 6 * D), preferred_element_type=f32).astype(bf16)
    shift_one, scale_one, gate_one, shift_two, scale_two, gate_two = (
        per_token[:, c * D : (c + 1) * D].astype(f32) for c in range(6)
    )

    pieces = jnp.stack([jnp.asarray(p, jnp.int32) for p in neighbour_indices(img_index)])
    place = img_index % 4
    inside = (pieces >= 0) & (pieces < n_img)
    slots = jnp.arange(PIECES)
    inside &= (slots != PIECES - 1) | (place == 0) | (place == 3)
    column = jnp.arange(tok, dtype=jnp.int32)[None, :]
    edge_start = jnp.where((slots == PIECES - 1) & (place == 0), tok - EDGE, 0)
    piece_rows = pieces[:, None] * tok + column + edge_start[:, None]
    there = inside[:, None] & ((slots[:, None] < PIECES - 1) | (column < EDGE))
    piece_ids = jnp.where(there, ids_of(piece_rows, sample_ends), -1)
    flags = jnp.any((piece_ids >= sample_ids[0]) & (piece_ids <= sample_ids[-1]), axis=1).astype(jnp.int32)
    piece_ids = jnp.concatenate([piece_ids, jnp.full((16 - PIECES, tok), -1, jnp.int32)], axis=0)
    own_ids = sample_ids[:, None]

    text_rows = text_states.shape[0]
    text_len = text_rows * n_img
    text_columns = lax.all_to_all(text_states, "img", split_axis=1, concat_axis=0, tiled=True)
    z_first = [0] + list(range(2, index_bits(n_img))) + [1]
    text_proj = TermSum(Clock(), jnp.dot(text_columns, own_text, preferred_element_type=f32), z_first).finish()
    text_shape = (text_rows, local_heads, HD)
    text_raw = text_proj[:, :half_d].reshape(text_shape)
    text_normed = rms_norm(text_raw)
    text_key_low = (text_normed * gain_text).reshape(text_rows, half_d).astype(bf16)
    text_low = jnp.concatenate([text_key_low, text_proj[:, half_d:].astype(bf16)], axis=1)
    all_text = gather_doubling(text_low)

    if blocks is not None:
        blocks = tie(blocks, all_text, per_token, cosine, sine, flags, piece_ids)
        (w_project,) = unpack(shapes[3:], heights[3], sum(heights[:3]) // heights[3], blocks)
    x_float = tokens.astype(f32)
    x_normed = rms_norm(x_float)
    normed_one = x_normed * gain_attn
    attn_in = (normed_one * (1.0 + scale_one) + shift_one).astype(bf16)
    queries, own_kv, raw_qk = call(
        project_kernel,
        (n_pairs,),
        [whole((tok, D)), pair(D), pair(D, n_pairs), pair(D, 2 * n_pairs)]
        + [whole((1, LANES))] * 2
        + [whole((tok, LANES))] * 2,
        [pair(tok), pairs(2, tok), pairs(2, tok)],
        [
            shape_of((tok, half_d), bf16),
            shape_of((2, tok, half_d), bf16),
            shape_of((2, tok, half_d), f32),
        ],
        (attn_in, w_project, w_project, w_project, gain_query_pair, gain_key_pair, cosine, sine),
        flops=2 * tok * D * 3 * half_d,
        moved=2 * D * 3 * half_d,
    )
    clock = Clock()
    clock.mark(own_kv)
    kv_near = Neighbourhood(clock, own_kv, own_kv[:, tok - EDGE :], own_kv[:, :EDGE])
    if blocks is None:
        w_updown, w_down, w_output = (gather(tie(rows, own_kv)) for rows in own_rows(0, 1, 4))
    else:
        w_updown, w_down, w_output = unpack(shapes[:3], sum(heights[:3]), 0, clock.stage(blocks))
    w_output_other = other_txt(w_output)
    clock.mark(w_updown)
    kv_near.second()
    kv_near.third()
    kv_pieces = kv_near.collect()

    kv_specs = [pairs(2 * c, a.shape[1]) for c, a in zip(PIECE_COUNTS, kv_pieces)]
    id_specs = [whole((tok, 1)), whole((16, tok))]
    text_specs = [pair(text_len), pair(text_len, n_pairs)]
    mixed_low, self_out, cross_out, lse_self, lse_cross, query_pack = call(
        functools.partial(attend_kernel, PIECE_COUNTS, tok),
        (n_pairs,),
        [pair(tok)] + id_specs + text_specs + [pair(1)] + kv_specs,
        [pair(tok)] * 5 + [whole((1, tok + PACK, half_d))],
        [shape_of((tok, half_d), bf16)]
        + [shape_of((tok, half_d), f32)] * 4
        + [shape_of((1, tok + PACK, half_d), bf16)],
        (flags, clock.stage(queries), own_ids, piece_ids, all_text, all_text, gate_lanes, *kv_pieces),
        scratch=[
            pltpu.VMEM((PIECES, 2 * tok, tok), f32),
            pltpu.VMEM((2 * tok, LANES), f32),
            pltpu.VMEM((2 * tok, LANES), f32),
            pltpu.VMEM((2 * tok, LANES), f32),
            pltpu.VMEM((PACK, tok), f32),
        ],
        prefetch=1,
        vmem=32,
    )

    def pack_edges(pack):
        table = pack[:, tok:]
        ending = jnp.concatenate(
            [table[:, :, part * tok + tok - EDGE : (part + 1) * tok] for part in range(3) for _ in range(tok // EDGE)],
            axis=2,
        )
        return (
            jnp.concatenate([pack[:, tok - EDGE : tok], ending], axis=1),
            jnp.concatenate([pack[:, :EDGE], table], axis=1),
        )

    clock.mark(mixed_low)
    mixed_other = other_txt(mixed_low)
    query_near = Neighbourhood(clock, query_pack, *pack_edges(query_pack))
    mixed_other, mixed_low = clock.stage(mixed_other, mixed_low)
    attn_out = jnp.dot(mixed_low, w_output, preferred_element_type=f32) + jnp.dot(
        mixed_other, w_output_other, preferred_element_type=f32
    )
    hidden = x_float + gate_one * attn_out
    h_normed = rms_norm(hidden)
    normed_two = h_normed * gain_ffn
    ffn_in = (normed_two * (1.0 + scale_two) + shift_two).astype(bf16)
    clock.mark(ffn_in)
    query_near.second()
    ffn_in = clock.stage(ffn_in)
    gate_up = jnp.dot(ffn_in, w_updown, preferred_element_type=f32)
    gate, up = gate_up[:, :half_ff], gate_up[:, half_ff:]
    sigmoid = jax.nn.sigmoid(gate)
    activated = gate * sigmoid
    hidden_units = (activated * up).astype(bf16)
    clock.mark(hidden_units)
    query_near.third()

    d_out = cotangent.astype(f32)
    d_branch = (d_out * gate_two).astype(bf16)
    down_sum = GradientSum(clock, tall(hidden_units), d_branch)
    query_pieces = query_near.collect()
    d_units = mm(clock.stage(d_branch), w_down, 1, 1)
    d_gate = (d_units * up * sigmoid * (1.0 + gate * (1.0 - sigmoid))).astype(bf16)
    d_up = (d_units * activated).astype(bf16)
    d_gate_up = jnp.concatenate([d_gate, d_up], axis=1)
    clock.mark(d_gate_up)
    down_sum.advance()
    d_gate_up = clock.stage(d_gate_up)
    d_ffn_part = mm(d_gate_up, w_updown, 1, 1).astype(bf16)
    clock.mark(d_ffn_part)
    d_ffn_other = other_txt(d_ffn_part)
    ffn_tall = tall(ffn_in)
    gate_sum = GradientSum(clock, ffn_tall, d_gate)
    up_sum = GradientSum(clock, ffn_tall, d_up)
    gate_sum.receive()
    up_sum.receive()
    d_ffn_part, d_ffn_other = clock.stage(d_ffn_part, d_ffn_other)
    d_ffn_in = d_ffn_part.astype(f32) + d_ffn_other.astype(f32)
    d_scale_two = d_ffn_in * normed_two
    d_normed_two = d_ffn_in * (1.0 + scale_two)
    d_gain_ffn = jnp.sum(d_normed_two * h_normed, axis=0)
    d_hidden = d_out + rms_back(hidden, d_normed_two * gain_ffn)
    d_attn = (d_hidden * gate_one).astype(bf16)
    clock.mark(d_attn)
    grad_pack, d_cross_low, d_gate_lanes = call(
        functools.partial(mixed_back_kernel, tok),
        (n_pairs,),
        [whole((tok, D)), pl.BlockSpec((LANES, D), lambda j: (j, 0)), pair(tok), pair(tok), pair(1)],
        [whole((1, tok + PACK, half_d)), pair(tok), pair(1)],
        [
            shape_of((1, tok + PACK, half_d), bf16),
            shape_of((tok, half_d), bf16),
            shape_of((1, half_d), f32),
        ],
        (clock.stage(d_attn), w_output, self_out, cross_out, gate_lanes),
        scratch=[pltpu.VMEM((PACK, tok), f32)],
        flops=2 * tok * D * half_d,
        moved=4 * D * half_d,
    )
    clock.mark(grad_pack)
    grad_near = Neighbourhood(clock, grad_pack, *pack_edges(grad_pack))
    down_sum.receive()
    gate_sum.advance(received=True)
    grad_near.second()
    down_sum.advance(received=True)
    turn_specs = [whole((1, LANES)), whole((tok, LANES)), whole((tok, LANES))]

    def query_back(first, count, d_cross):
        def at(rows, also=0):
            return pair(rows, first + also)

        def some(arrays, rows, index=0):
            return pl.BlockSpec((arrays, rows, LANES), lambda j, *_: (index, 0, first + j))

        return call(
            functools.partial(query_back_kernel, PIECE_COUNTS, tok),
            (count,),
            [at(tok)]
            + id_specs
            + [at(text_len), at(text_len, n_pairs)]
            + [some(1, tok), at(tok)]
            + [at(tok)] * 4
            + [some(1, tok)]
            + turn_specs
            + [some(2 * c, a.shape[1]) for c, a in zip(PIECE_COUNTS, kv_pieces)],
            [pair(tok), pair(1), pair(text_len), pair(text_len)],
            [
                shape_of((tok, count * LANES), bf16),
                shape_of((1, count * LANES), f32),
                shape_of((text_len, count * LANES), f32),
                shape_of((text_len, count * LANES), f32),
            ],
            (
                flags, queries, own_ids, piece_ids, all_text, all_text, grad_pack, d_cross,
                self_out, cross_out, lse_self, lse_cross, raw_qk, gain_query_pair, cosine, sine, *kv_pieces,
            ),
            scratch=[pltpu.VMEM((2 * tok, LANES), f32)],
            prefetch=1,
        )

    head_half = n_pairs // 2
    first_half = query_back(0, head_half, clock.stage(d_cross_low))
    clock.mark(first_half[0])
    grad_near.third()
    up_sum.advance(received=True)
    output_sum = GradientSum(clock, tall(mixed_low), d_attn)
    grad_pieces = grad_near.collect()
    second_half = query_back(head_half, n_pairs - head_half, clock.stage(d_cross_low))
    clock.mark(second_half[0])
    d_query_raw, d_gain_query, d_text_key, d_text_value = (
        jnp.concatenate(halves, axis=1) for halves in zip(first_half, second_half)
    )
    gate_sum.advance()
    text_sum = TermSum(clock, jnp.concatenate([d_text_key, d_text_value], axis=1), z_first)
    down_sum.advance()
    text_sum.advance()
    attn_tall = tall(attn_in)

    def pack_specs(arrays):
        views = [pairs(c, a.shape[1] - PACK) for c, a in zip(PIECE_COUNTS, arrays)]
        rows = [
            pl.BlockSpec((c, PACK, half_d), lambda j, *_, at=(a.shape[1] - PACK) // PACK: (0, at, 0))
            for c, a in zip(PIECE_COUNTS, arrays)
        ]
        return views + rows

    d_key_raw, d_gain_key, d_value = call(
        functools.partial(key_back_kernel, PIECE_COUNTS, tok),
        (n_pairs,),
        [pairs(2, tok)]
        + id_specs
        + [pairs(1, tok, 1)]
        + turn_specs
        + pack_specs(query_pieces)
        + pack_specs(grad_pieces),
        [pair(tok), pair(1), pair(tok)],
        [
            shape_of((tok, half_d), bf16),
            shape_of((1, half_d), f32),
            shape_of((tok, half_d), bf16),
        ],
        (
            flags, clock.stage(own_kv), own_ids, piece_ids, raw_qk, gain_key_pair,
            cosine, sine, *query_pieces, *query_pieces, *grad_pieces, *grad_pieces,
        ),
        scratch=[pltpu.VMEM((2 * tok, LANES), f32)] * 2,
        prefetch=1,
    )
    clock.mark(d_value)
    query_sum = GradientSum(clock, attn_tall, d_query_raw)
    key_value_sum = GradientSum(clock, attn_tall, jnp.concatenate([d_key_raw, d_value], axis=1))
    d_query_raw, d_key_raw, d_value = clock.stage(d_query_raw, d_key_raw, d_value)
    d_projected = jnp.concatenate([d_query_raw, d_key_raw, d_value], axis=1)
    d_attn_part = mm(d_projected, w_project, 1, 1).astype(bf16)
    clock.mark(d_attn_part)
    d_attn_other = other_txt(d_attn_part)
    output_sum.advance()
    query_sum.advance()
    text_sum.advance()
    up_sum.advance()
    key_value_sum.advance()
    gate_sum.advance()
    branch_part = jnp.dot(clock.stage(hidden_units), w_down, preferred_element_type=f32)
    clock.mark(branch_part)
    d_attn_other = clock.stage(d_attn_other)
    d_attn_in = d_attn_part.astype(f32) + d_attn_other.astype(f32)
    branch = branch_part + other_txt(branch_part)
    block_out = hidden + gate_two * branch
    d_gate_two = d_out * branch
    d_gate_one = d_hidden * attn_out

    text_own = text_sum.finish()
    d_text_scaled = text_own[:, :half_d].reshape(text_shape)
    d_gain_text = jnp.sum(d_text_scaled * text_normed, axis=(0, 1))
    d_text_raw = rms_back(text_raw, d_text_scaled * gain_text).reshape(text_rows, half_d)
    d_text_proj = gather_doubling(jnp.concatenate([d_text_raw, text_own[:, half_d:]], axis=1).astype(bf16))
    grad_text = mm(text_columns, d_text_proj, 0, 0)

    d_scale_one = d_attn_in * normed_one
    d_normed_one = d_attn_in * (1.0 + scale_one)
    d_gain_attn = jnp.sum(d_normed_one * x_normed, axis=0)
    d_tokens = d_hidden + rms_back(x_float, d_normed_one * gain_attn)

    one_hot_wide = one_hot.astype(f32)

    def by_sample(values):
        summed = lax.dot_general(one_hot_wide, values, (((0,), (0,)), ((), ())), precision=HIGH)
        return lax.dynamic_slice_in_dim(summed, txt_index * half_d, half_d, 1)

    d_mod = jnp.concatenate(
        [by_sample(v) for v in (d_attn_in, d_scale_one, d_gate_one, d_ffn_in, d_scale_two, d_gate_two)], axis=1
    )

    replica = (txt_index == 0).astype(f32)
    d_gate_local = jnp.sum(d_gate_lanes.reshape(local_heads, HD), axis=1) * (1.0 - tanh_gate**2)
    gate_full = lax.dynamic_update_slice(jnp.zeros((HEADS,), f32), d_gate_local, (txt_index * local_heads,))
    small_terms = jnp.concatenate(
        [
            d_gain_attn * replica,
            d_gain_ffn * replica,
            jnp.sum(d_gain_query.reshape(local_heads, HD), axis=0),
            jnp.sum(d_gain_key.reshape(local_heads, HD), axis=0),
            jnp.zeros((HD,), f32),
            gate_full,
        ]
    )
    small_count = small_terms.shape[0]
    small_row = jnp.pad(small_terms, (0, d_mod.shape[1] - small_count))[None]
    sums = sum_over_img(jnp.concatenate([d_mod, small_row], axis=0))
    d_mod = sums[:samples]
    small_row = sums[samples:, :]
    small_grad = (small_row + other_txt(small_row))[0, :small_count]
    grad_modulate = lax.dot_general(silu_own.astype(f32), d_mod, (((0,), (0,)), ((), ())), precision=HIGH)

    pending = [down_sum, gate_sum, output_sum, query_sum, up_sum, key_value_sum]
    while pending:
        for one in list(pending):
            one.result = one.advance()
            if one.level == len(one.order):
                pending.remove(one)
    grad_down, grad_gate, grad_output, grad_query, grad_up, grad_key_value = (
        one.result for one in (down_sum, gate_sum, output_sum, query_sum, up_sum, key_value_sum)
    )
    grads = [grad_gate, grad_up, grad_down, grad_query, grad_key_value, grad_text, grad_output, grad_modulate]
    places = [
        (starts[0], 0, 2 * half_ff),
        (starts[0], half_ff, 2 * half_ff),
        (starts[1], 0, D),
        (starts[2], 0, 3 * half_d),
        (starts[2], half_d, 3 * half_d),
        (starts[3], 0, 2 * half_d),
        (starts[4], 0, D),
        (starts[5], 0, 6 * half_d),
    ]
    reduced, squares = pl.pallas_call(
        functools.partial(flatten_kernel, places),
        out_shape=[shape_of((lines, LANES), f32), shape_of((1, LANES), f32)],
        compiler_params=pltpu.CompilerParams(vmem_limit_bytes=32 * MIB),
    )(*grads)

    last = sum_over_all(jnp.concatenate([squares, jnp.pad(d_gain_text, (0, LANES - HD))[None]], axis=0))
    small_grad = lax.dynamic_update_slice(small_grad, last[1, :HD], (2 * D + 2 * HD,))
    grad_square = jnp.sum(last[0]) + jnp.sum(small_grad * small_grad)
    clip_factor = MAX_NORM / jnp.maximum(jnp.sqrt(grad_square), MAX_NORM)

    block = math.gcd(lines, 512)
    line_spec = pl.BlockSpec((block, LANES), lambda i: (i, 0))
    as_lines = (lines, LANES)
    updated = call(
        update_kernel,
        (lines // block,),
        [pl.BlockSpec(memory_space=pltpu.SMEM)] + [line_spec] * 5,
        [line_spec] * 5,
        [shape_of(as_lines, f32)] * 4 + [shape_of(as_lines, bf16)],
        (clip_factor.reshape(1), reduced, *(a.reshape(as_lines) for a in (moment_one, moment_two, master, average))),
        vmem=52,
        flops=20 * lines * LANES,
        moved=38 * lines * LANES,
    )
    one_new, two_new, master_new, average_new, master_low = (a.reshape(master.shape) for a in updated)
    small_one_new, small_two_new, small_new, small_average_new = adam_update(
        small_grad * clip_factor, small_one, small_two, small_master, small_average, RATE_SMALL, 0.0
    )
    return (
        block_out,
        d_tokens,
        grad_square,
        one_new,
        two_new,
        master_new,
        average_new,
        master_low,
        small_one_new,
        small_two_new,
        small_new,
        small_average_new,
    )


def solution(mesh):
    rows = P("img", None)
    shards = P("img", "txt", None)
    in_specs = (rows, rows, rows, P(), P(), shards, shards, shards, shards, P(), P(), P(), P())
    out_specs = (rows, rows, P(), shards, shards, shards, shards, shards, P(), P(), P(), P())
    return jax.shard_map(on_device, mesh=mesh, in_specs=in_specs, out_specs=out_specs, check_vma=False)
```

```python
import functools
import math

import jax
import jax.numpy as jnp
from jax import lax
from jax.experimental import pallas as pl
from jax.experimental.pallas import tpu as pltpu
from jax.sharding import PartitionSpec as P

D = 1536
HEADS = 24
HD = 64
FF = 4096
TXT_D = 4096
COND = 1024
SIDE_MAX = 32
STEP = 10

HIGH = lax.Precision.HIGHEST
EPS_NORM = 1e-06
MAX_NORM = 1.0
BETA_ONE = 0.5
BETA_TWO = 0.5
RATE_MATRIX = 0.01
RATE_SMALL = 0.1
DECAY_WEIGHT = 0.01
ADAM_EPS = 1e-08
EMA_DECAY = 0.8

LANES = 128
EDGE = 128
TABLE = 16
PACK = 2 * TABLE
WIDE = 256
PIECES = 13
MASKED = -1e30
MIB = 1024 * 1024

bf16 = jnp.bfloat16
f32 = jnp.float32


def mm(a, b, on_a, on_b):
    return lax.dot_general(a, b, (((on_a,), (on_b,)), ((), ())), preferred_element_type=f32)


def lane_index(rows):
    return lax.broadcasted_iota(jnp.int32, (rows, LANES), 1)


def head_sum(values):
    low = lane_index(values.shape[0]) < HD
    first = jnp.sum(jnp.where(low, values, 0.0), axis=1, keepdims=True)
    second = jnp.sum(jnp.where(low, 0.0, values), axis=1, keepdims=True)
    return jnp.where(low, first, second)


def swap_halves(values):
    first = lane_index(values.shape[0]) % HD < HD // 2
    return jnp.where(
        first, pltpu.roll(values, LANES - HD // 2, 1), pltpu.roll(values, HD // 2, 1)
    )


def two_heads(pair):
    low = lane_index(pair.shape[0]) < HD
    zero = jnp.zeros_like(pair)
    return jnp.concatenate([jnp.where(low, pair, zero), jnp.where(low, zero, pair)], axis=0)


def one_pair(stacked):
    rows = stacked.shape[0] // 2
    low = lane_index(rows) < HD
    return jnp.where(low, stacked[:rows], stacked[rows:])


def columns_of(spread):
    return jnp.concatenate([spread[:, :1], spread[:, HD : HD + 1]], axis=0)


def norm_rope(raw, gain, cosine, sine):
    inverse = lax.rsqrt(head_sum(raw * raw) * (1.0 / HD) + EPS_NORM)
    scaled = raw * inverse * gain
    return scaled * cosine + swap_halves(scaled) * sine


def norm_rope_back(raw, gain, cosine, sine, d_out):
    inverse = lax.rsqrt(head_sum(raw * raw) * (1.0 / HD) + EPS_NORM)
    normed = raw * inverse
    d_scaled = d_out * cosine - swap_halves(d_out) * sine
    d_gain = jnp.sum(d_scaled * normed, axis=0, keepdims=True)
    d_normed = d_scaled * gain
    d_raw = inverse * (d_normed - normed * (head_sum(d_normed * normed) * (1.0 / HD)))
    return d_raw, d_gain


def split_three(values):
    high = values.astype(bf16)
    rest = values - high.astype(f32)
    middle = rest.astype(bf16)
    last = (rest - middle.astype(f32)).astype(bf16)
    return jnp.concatenate([high, middle, last], axis=1)


def joined(packed, rows):
    wide = packed.astype(f32)
    return wide[:, :rows] + wide[:, rows : 2 * rows] + wide[:, 2 * rows : 3 * rows]


def put_row(table, index, row):
    at = lax.broadcasted_iota(jnp.int32, table.shape, 0) == index
    return jnp.where(at, row, table)


def take_row(table, index):
    at = lax.broadcasted_iota(jnp.int32, table.shape, 0) == index
    return jnp.sum(jnp.where(at, table, 0.0), axis=0, keepdims=True)


def as_row(column):
    return jnp.broadcast_to(column, (column.shape[0], LANES)).T[:1]


def tile(ref):
    return ref[...].reshape(-1, WIDE)


def tiles(ref, count):
    if len(ref.shape) == 2:
        return [ref[:, at * WIDE : (at + 1) * WIDE] for at in range(count)]
    rows = ref.shape[1] // count
    return [ref[:, at * rows : (at + 1) * rows, :].reshape(-1, WIDE) for at in range(count)]


def add_transposed(acc_ref, a_ref, w_ref):
    count = a_ref.shape[1] // WIDE
    blocks = tiles(w_ref, count)
    for row in range(0, acc_ref.shape[1], WIDE):
        part = slice(row, row + WIDE)
        total = mm(a_ref[:, :WIDE], blocks[0][part], 1, 1)
        for at in range(1, count):
            total = total + mm(a_ref[:, at * WIDE : (at + 1) * WIDE], blocks[at][part], 1, 1)
        acc_ref[:, part] += total


def project_kernel(a_ref, wq_ref, wk_ref, wv_ref, gq_ref, gk_ref, cos_ref, sin_ref, q_ref, kv_ref, raw_ref):
    a = a_ref[...]
    cosine, sine = cos_ref[...], sin_ref[...]
    raw_q = mm(a, tile(wq_ref), 1, 0)
    raw_k = mm(a, tile(wk_ref), 1, 0)
    raw_ref[0] = raw_q
    raw_ref[1] = raw_k
    for at in range(0, WIDE, LANES):
        part = slice(at, at + LANES)
        query = norm_rope(raw_q[:, part], gq_ref[...], cosine, sine).astype(bf16)
        q_ref[:, part] = query * jnp.asarray(HD**-0.5, bf16)
        kv_ref[0, :, part] = norm_rope(raw_k[:, part], gk_ref[...], cosine, sine).astype(bf16)
    kv_ref[1] = mm(a, tile(wv_ref), 1, 0).astype(bf16)


def times_kernel(a_ref, w_ref, out_ref):
    out_ref[...] = mm(a_ref[...], tile(w_ref), 1, 0)


def two_times_kernel(a_ref, w_ref, other_a_ref, other_w_ref, out_ref):
    out_ref[...] = mm(a_ref[...], tile(w_ref), 1, 0) + mm(other_a_ref[...], tile(other_w_ref), 1, 0)


def times_transposed_kernel(a_ref, w_ref, out_ref, acc_ref):
    step = pl.program_id(0)

    @pl.when(step == 0)
    def _():
        acc_ref[...] = jnp.zeros(acc_ref.shape, f32)

    add_transposed(acc_ref, a_ref, w_ref)

    @pl.when(step == pl.num_programs(0) - 1)
    def _():
        out_ref[...] = acc_ref[...].astype(out_ref.dtype)


def hidden_kernel(b_ref, w_gate_ref, w_up_ref, gate_ref, up_ref, hidden_ref, turned_ref):
    gate = mm(b_ref[...], tile(w_gate_ref), 1, 0)
    up = mm(b_ref[...], tile(w_up_ref), 1, 0)
    hidden = (gate * jax.nn.sigmoid(gate) * up).astype(bf16)
    gate_ref[...] = gate
    up_ref[...] = up
    hidden_ref[...] = hidden
    turned_ref[...] = hidden.T


def hidden_back_kernel(d_branch_ref, w_ref, gate_ref, up_ref, d_gate_ref, d_up_ref, acc_ref):
    step = pl.program_id(0)

    @pl.when(step == 0)
    def _():
        acc_ref[...] = jnp.zeros(acc_ref.shape, f32)

    add_transposed(acc_ref, d_branch_ref, w_ref)

    @pl.when(step == pl.num_programs(0) - 1)
    def _():
        for at in range(0, acc_ref.shape[1], WIDE):
            part = slice(at, at + WIDE)
            d_units, gate = acc_ref[:, part], gate_ref[:, part]
            sigmoid = jax.nn.sigmoid(gate)
            d_gate = d_units * up_ref[:, part] * sigmoid * (1.0 + gate * (1.0 - sigmoid))
            d_gate_ref[:, part] = d_gate.astype(bf16)
            d_up_ref[:, part] = (d_units * (gate * sigmoid)).astype(bf16)


def piece_views(piece_refs, counts, per):
    views = []
    for ref, count in zip(piece_refs, counts):
        for at in range(count):
            views.append((ref, at * per))
    return views


def attend_kernel(counts, tok, flag_ref, q_ref, own_ids_ref, ids_ref, tk_ref, tv_ref, gate_ref, *rest):
    pieces = piece_views(rest[: len(counts)], counts, 2)
    mixed_ref, self_ref, cross_ref, lse_self_ref, lse_cross_ref, split_ref = rest[len(counts) : len(counts) + 6]
    scores_ref, most_ref, total_ref, acc_ref, table_ref = rest[len(counts) + 6 :]
    step = pl.program_id(0)
    own_ids = own_ids_ref[...]
    q_pair = q_ref[...]
    q_two = two_heads(q_pair)
    own_two = jnp.concatenate([own_ids, own_ids], axis=0)
    most_ref[...] = jnp.full(most_ref.shape, MASKED, f32)
    total_ref[...] = jnp.zeros(total_ref.shape, f32)
    acc_ref[...] = jnp.zeros(acc_ref.shape, f32)
    for slot, (ref, at) in enumerate(pieces):
        rows = ref.shape[1]

        @pl.when(flag_ref[slot] > 0)
        def _(slot=slot, ref=ref, at=at, rows=rows):
            scores = mm(q_two, ref[at], 1, 1)
            scores = jnp.where(own_two == ids_ref[slot : slot + 1, :rows], scores, MASKED)
            scores_ref[slot, :, :rows] = scores
            most = most_ref[...]
            for part in range(rows // LANES):
                most = jnp.maximum(most, scores[:, part * LANES : (part + 1) * LANES])
            most_ref[...] = most

    row_most = jnp.max(most_ref[...], axis=1, keepdims=True)
    for slot, (ref, at) in enumerate(pieces):
        rows = ref.shape[1]

        @pl.when(flag_ref[slot] > 0)
        def _(slot=slot, ref=ref, at=at, rows=rows):
            weights = jnp.exp(scores_ref[slot, :, :rows] - row_most)
            total = total_ref[...]
            for part in range(rows // LANES):
                total = total + weights[:, part * LANES : (part + 1) * LANES]
            total_ref[...] = total
            acc_ref[...] += mm(weights.astype(bf16), ref[at + 1], 1, 0)

    row_total = jnp.sum(total_ref[...], axis=1, keepdims=True)
    self_out = one_pair(acc_ref[...] / row_total)
    lse_self = row_most + jnp.log(row_total)

    cross_scores = mm(q_two, tk_ref[...], 1, 1)
    cross_most = jnp.max(cross_scores, axis=1, keepdims=True)
    cross_weights = jnp.exp(cross_scores - cross_most)
    cross_total = jnp.sum(cross_weights, axis=1, keepdims=True)
    cross_out = one_pair(mm(cross_weights.astype(bf16), tv_ref[...], 1, 0) / cross_total)
    lse_cross = cross_most + jnp.log(cross_total)

    self_ref[...] = self_out
    cross_ref[...] = cross_out
    mixed_ref[...] = (self_out + gate_ref[...] * cross_out).astype(bf16)
    spread = (tok, LANES)
    low = lane_index(tok) < HD
    lse_self_ref[...] = jnp.where(
        low, jnp.broadcast_to(lse_self[:tok], spread), jnp.broadcast_to(lse_self[tok:], spread)
    )
    lse_cross_ref[...] = jnp.where(
        low, jnp.broadcast_to(lse_cross[:tok], spread), jnp.broadcast_to(lse_cross[tok:], spread)
    )

    @pl.when(step == 0)
    def _():
        table_ref[...] = jnp.zeros(table_ref.shape, f32)

    table = put_row(table_ref[...], 2 * step, as_row(lse_self[:tok]))
    table = put_row(table, 2 * step + 1, as_row(lse_self[tok:]))
    table_ref[...] = table

    @pl.when(step == pl.num_programs(0) - 1)
    def _():
        split_ref[...] = split_three(table_ref[...])


def mixed_back_kernel(tok, d_attn_ref, w_ref, self_ref, cross_ref, gate_ref, lse_ref, pack_ref, d_cross_ref, d_gate_ref, acc_ref):
    step = pl.program_id(0)

    @pl.when(step == 0)
    def _():
        acc_ref[...] = jnp.zeros(acc_ref.shape, f32)

    add_transposed(acc_ref, d_attn_ref, w_ref)

    @pl.when(step == pl.num_programs(0) - 1)
    def _():
        rows = []
        for at in range(0, acc_ref.shape[1], LANES):
            part = slice(at, at + LANES)
            d_mixed = acc_ref[:, part]
            d_self = d_mixed.astype(bf16)
            d_cross_ref[:, part] = (gate_ref[:, part] * d_mixed).astype(bf16)
            d_gate_ref[:, part] = jnp.sum(d_mixed * cross_ref[:, part], axis=0, keepdims=True)
            delta = head_sum(d_self.astype(f32) * self_ref[:, part])
            rows += [as_row(delta[:, :1]), as_row(delta[:, HD : HD + 1])]
            pack_ref[0, :tok, part] = d_self
        rows += [jnp.zeros_like(rows[0])] * (TABLE - len(rows))
        pack_ref[0, tok : tok + TABLE, :] = split_three(jnp.concatenate(rows, axis=0))
        pack_ref[0, tok + TABLE :, :] = lse_ref[...]


def query_back_kernel(
    counts, tok, flag_ref, q_ref, own_ids_ref, ids_ref, tk_ref, tv_ref, d_self_ref, d_cross_ref,
    self_ref, cross_ref, lse_self_ref, lse_cross_ref, raw_ref, gain_ref, cos_ref, sin_ref, *rest
):
    pieces = piece_views(rest[: len(counts)], counts, 2)
    d_raw_ref, d_gain_ref, d_tk_ref, d_tv_ref, acc_ref = rest[len(counts) :]
    own_ids = own_ids_ref[...]
    own_two = jnp.concatenate([own_ids, own_ids], axis=0)
    q_two = two_heads(q_ref[...])
    d_self = d_self_ref[0]
    d_self_two = two_heads(d_self)
    delta = columns_of(head_sum(d_self.astype(f32) * self_ref[...]))
    lse = columns_of(lse_self_ref[...])

    d_cross = d_cross_ref[...]
    d_cross_two = two_heads(d_cross)
    delta_cross = columns_of(head_sum(d_cross.astype(f32) * cross_ref[...]))
    lse_cross = columns_of(lse_cross_ref[...])
    cross_p = jnp.exp(mm(q_two, tk_ref[...], 1, 1) - lse_cross)
    d_cross_p = mm(d_cross_two, tv_ref[...], 1, 1)
    d_cross_s = (cross_p * (d_cross_p - delta_cross)).astype(bf16)
    d_tv_ref[...] = mm(cross_p.astype(bf16), d_cross_two, 0, 0)
    d_tk_ref[...] = mm(d_cross_s, q_two, 0, 0)
    acc_ref[...] = mm(d_cross_s, tk_ref[...], 1, 0)
    for slot, (ref, at) in enumerate(pieces):
        rows = ref.shape[1]

        @pl.when(flag_ref[slot] > 0)
        def _(slot=slot, ref=ref, at=at, rows=rows):
            key = ref[at]
            scores = mm(q_two, key, 1, 1)
            scores = jnp.where(own_two == ids_ref[slot : slot + 1, :rows], scores, MASKED)
            weights = jnp.exp(scores - lse)
            d_weights = mm(d_self_two, ref[at + 1], 1, 1)
            d_scores = (weights * (d_weights - delta)).astype(bf16)
            acc_ref[...] += mm(d_scores, key, 1, 0)

    d_query = one_pair(acc_ref[...]) * (HD**-0.5)
    d_raw, d_gain = norm_rope_back(raw_ref[0], gain_ref[...], cos_ref[...], sin_ref[...], d_query)
    d_raw_ref[...] = d_raw.astype(bf16)
    d_gain_ref[...] = d_gain


def key_back_kernel(counts, tok, flag_ref, kv_ref, own_ids_ref, ids_ref, raw_ref, gain_ref, cos_ref, sin_ref, *rest):
    n = len(counts)
    q_views = piece_views(rest[:n], counts, 1)
    g_views = piece_views(rest[n : 2 * n], counts, 1)
    g_tables = piece_views(rest[2 * n : 3 * n], counts, 1)
    d_raw_ref, d_gain_ref, d_value_ref, acc_k_ref, acc_v_ref = rest[3 * n :]
    step = pl.program_id(0)
    own_ids = own_ids_ref[...]
    k_two = two_heads(kv_ref[0])
    v_two = two_heads(kv_ref[1])
    acc_k_ref[...] = jnp.zeros(acc_k_ref.shape, f32)
    acc_v_ref[...] = jnp.zeros(acc_v_ref.shape, f32)
    for slot in range(PIECES):
        q_ref, at = q_views[slot]
        rows = q_ref.shape[1]
        @pl.when(flag_ref[slot] > 0)
        def _(slot=slot, q_ref=q_ref, at=at, rows=rows):
            query = q_ref[at]
            d_self = g_views[slot][0][at]
            tables = joined(g_tables[slot][0][at], tok)[:, :rows]
            delta, lse = tables[:TABLE], tables[TABLE:]
            same = own_ids == ids_ref[slot : slot + 1, :rows]
            scores = mm(k_two, query, 1, 1)
            d_weights = mm(v_two, d_self, 1, 1)
            p_low, d_low = [], []
            for head in range(2):
                part = slice(head * tok, (head + 1) * tok)
                masked = jnp.where(same, scores[part], MASKED)
                weights = jnp.exp(masked - take_row(lse, 2 * step + head))
                p_low.append(weights.astype(bf16))
                d_low.append((weights * (d_weights[part] - take_row(delta, 2 * step + head))).astype(bf16))
            acc_v_ref[...] += mm(jnp.concatenate(p_low, axis=0), d_self, 1, 0)
            acc_k_ref[...] += mm(jnp.concatenate(d_low, axis=0), query, 1, 0)

    d_raw, d_gain = norm_rope_back(
        raw_ref[0], gain_ref[...], cos_ref[...], sin_ref[...], one_pair(acc_k_ref[...])
    )
    d_raw_ref[...] = d_raw.astype(bf16)
    d_gain_ref[...] = d_gain
    d_value_ref[...] = one_pair(acc_v_ref[...]).astype(bf16)


def unflatten_kernel(tables, *refs):
    for (rows, columns), lines_ref, out_ref in zip(tables, refs, refs[len(tables) :]):
        per_row = columns // LANES
        for at in range(per_row):
            out_ref[:, at * LANES : (at + 1) * LANES] = lines_ref[pl.ds(at, rows, stride=per_row), :].astype(bf16)


def pack_kernel(tables, *refs):
    *lines_refs, out_ref = refs
    top = 0
    for (rows, columns), lines_ref in zip(tables, lines_refs):
        per_row = columns // LANES
        for at in range(per_row):
            row = top + at // (WIDE // LANES) * rows
            lane = at % (WIDE // LANES) * LANES
            out_ref[row : row + rows, lane : lane + LANES] = lines_ref[pl.ds(at, rows, stride=per_row), :].astype(bf16)
        top += columns // WIDE * rows


def flatten_kernel(places, *refs):
    *grad_refs, lines_ref, square_ref = refs
    square = jnp.zeros((1, LANES), f32)
    for (start, column, columns), ref in zip(places, grad_refs):
        for at in range(ref.shape[1] // LANES):
            part = ref[:, at * LANES : (at + 1) * LANES].astype(f32)
            lines_ref[pl.ds(start + column // LANES + at, ref.shape[0], stride=columns // LANES), :] = part
            square = square + jnp.sum(part * part, axis=0, keepdims=True)
    square_ref[...] = square


def update_kernel(clip_ref, g_ref, one_ref, two_ref, w_ref, avg_ref, one_out, two_out, w_out, avg_out, low_out):
    one, two, weight, moving = adam_update(
        g_ref[...] * clip_ref[0], one_ref[...], two_ref[...], w_ref[...], avg_ref[...], RATE_MATRIX, DECAY_WEIGHT
    )
    one_out[...] = one
    two_out[...] = two
    w_out[...] = weight
    avg_out[...] = moving
    low_out[...] = weight.astype(bf16)


def adam_update(gradient, first_moment, second_moment, weight, moving, rate, decay):
    first_new = BETA_ONE * first_moment + (1.0 - BETA_ONE) * gradient
    second_new = BETA_TWO * second_moment + (1.0 - BETA_TWO) * gradient * gradient
    corr_one = 1.0 - BETA_ONE**STEP
    corr_two = 1.0 - BETA_TWO**STEP
    step_dir = first_new / corr_one / (jnp.sqrt(second_new / corr_two) + ADAM_EPS)
    weight_new = weight - rate * (step_dir + decay * weight)
    moving_new = EMA_DECAY * moving + (1.0 - EMA_DECAY) * weight_new
    return (first_new, second_new, weight_new, moving_new)


def call(kernel, grid, in_specs, out_specs, out_shape, args, scratch=(), prefetch=0, flops=0, moved=0, vmem=58):
    return pl.pallas_call(
        kernel,
        grid_spec=pltpu.PrefetchScalarGridSpec(
            num_scalar_prefetch=prefetch, grid=grid, in_specs=in_specs, out_specs=out_specs, scratch_shapes=scratch
        ),
        out_shape=out_shape,
        compiler_params=pltpu.CompilerParams(dimension_semantics=("arbitrary",) * len(grid), vmem_limit_bytes=vmem * MIB),
        cost_estimate=pl.CostEstimate(flops=flops, bytes_accessed=moved, transcendentals=0),
    )(*args)


def whole(shape):
    return pl.BlockSpec(shape, lambda *_: (0,) * len(shape))


def pair(rows, first=0):
    return pl.BlockSpec((rows, LANES), lambda j, *_: (0, first + j))


def pairs(count, rows, at=0):
    return pl.BlockSpec((count, rows, LANES), lambda j, *_: (at, 0, j))


def shape_of(shape, dtype):
    return jax.ShapeDtypeStruct(shape, dtype)


def shifted(x, by):
    count = lax.axis_size("img")
    return lax.ppermute(x, "img", [(i + by, i) for i in range(count) if 0 <= i + by < count])


def crossed(x, bit):
    count = lax.axis_size("img")
    return lax.ppermute(x, "img", [(i, i ^ bit) for i in range(count)])


def other_txt(x):
    return lax.ppermute(x, "txt", [(0, 1), (1, 0)])


def index_bits(count):
    bits = count.bit_length() - 1
    assert count == 1 << bits
    return bits


def sum_over_img(x):
    for bit in range(index_bits(lax.axis_size("img"))):
        x = x + crossed(x, 1 << bit)
    return x


def sum_over_all(x):
    x = sum_over_img(x)
    return x + other_txt(x)


def own_and_other(x, bit, below=1):
    mine = (lax.axis_index("img") >> bit) & 1
    split = x.reshape(x.shape[0] // (2 * below), 2, below, *x.shape[1:])
    own = lax.dynamic_index_in_dim(split, mine, 1, keepdims=False)
    other = lax.dynamic_index_in_dim(split, 1 - mine, 1, keepdims=False)
    return own.reshape(-1, *x.shape[1:]), other.reshape(-1, *x.shape[1:])


class TermSum:
    def __init__(self, clock, terms, order):
        count = lax.axis_size("img")
        self.clock, self.order, self.level = clock, order, 0
        self.keep = clock.stage(terms).reshape(count, terms.shape[0] // count, terms.shape[1])
        self.send()

    def send(self):
        bit = self.order[self.level]
        below = 1 << sum(other < bit for other in self.order[self.level :])
        self.keep, self.sent = own_and_other(self.keep, bit, below)
        self.clock.mark(self.sent)

    def advance(self):
        got = self.clock.stage(crossed(self.sent, 1 << self.order[self.level]))
        self.keep = self.keep + got
        self.level += 1
        if self.level == len(self.order):
            self.clock.mark(self.keep)
            return self.keep[0]
        self.send()

    def finish(self):
        while True:
            result = self.advance()
            if result is not None:
                return result


def gather_doubling(x):
    x = x[None]
    for bit in reversed(range(index_bits(lax.axis_size("img")))):
        x = doubled(x, bit)
    return x.reshape(-1, x.shape[-1])


def doubled(x, bit):
    mine = (lax.axis_index("img") >> bit) & 1
    got = crossed(x, 1 << bit)
    both = jnp.where(mine == 0, jnp.stack([x, got], 1), jnp.stack([got, x], 1))
    return both.reshape(-1, *x.shape[1:])


def tie(x, *others):
    return lax.optimization_barrier((x, others))[0]


def tall(left):
    count = lax.axis_size("img")
    return left.T.reshape(count, left.shape[1] // count, left.shape[0])


class Clock:
    def __init__(self):
        self.token = ()

    def stage(self, *arrays):
        arrays, _ = lax.optimization_barrier((arrays, self.token))
        return arrays if len(arrays) > 1 else arrays[0]

    def mark(self, *arrays):
        self.token = arrays


class SmallSum:
    def __init__(self, clock, x):
        self.clock, self.x, self.level = clock, x, 0
        self.levels = index_bits(lax.axis_size("img"))
        clock.mark(x)

    def advance(self):
        got = self.clock.stage(crossed(self.x, 1 << self.level))
        self.x = self.x + got
        self.clock.mark(self.x)
        self.level += 1

    def finish(self):
        while self.level < self.levels:
            self.advance()
        return self.x


class GradientSum:
    def __init__(self, clock, left, right):
        bits = index_bits(left.shape[0])
        self.order = list(range(bits))
        self.level = 0
        self.clock = clock
        left, self.right = clock.stage(left, right)
        self.own, other = own_and_other(left, 0)
        self.sent = self.terms(other).astype(bf16)
        self.result = None
        clock.mark(self.sent)

    def terms(self, chunks):
        product = mm(chunks.reshape(-1, chunks.shape[2]), self.right, 1, 0)
        return product.reshape(chunks.shape[0], chunks.shape[1], self.right.shape[1])

    def receive(self):
        self.got = self.clock.stage(crossed(self.sent, 1 << self.order[self.level]))
        self.clock.mark(self.got)
        self.level += 1

    def advance(self, received=False):
        if not received:
            self.receive()
        got = self.clock.stage(self.got)
        if self.level == len(self.order):
            self.result = (self.keep + got.astype(f32))[0]
            return self.result
        bit = self.order[self.level]
        if self.level == 1:
            own, other = own_and_other(self.own, bit)
            got_own, got_other = own_and_other(got, bit)
            self.sent = (self.terms(other) + got_other.astype(f32)).astype(bf16)
            self.keep = self.terms(own) + got_own.astype(f32)
        else:
            own, other = own_and_other(self.keep + got.astype(f32), bit)
            self.sent, self.keep = other.astype(bf16), own
        self.clock.mark(self.sent)


class Neighbourhood:
    def __init__(self, clock, x, end, beginning):
        count = lax.axis_size("img")
        self.clock = clock
        self.x = x
        self.across = crossed(x, 2)
        self.above, self.below = shifted(x, 4), shifted(x, -4)
        edge = jnp.where(lax.axis_index("img") % 4 == 3, end, beginning)
        pairs_low = [(i - 5, i) for i in range(0, count, 4) if i >= 5]
        pairs_high = [(i + 5, i) for i in range(3, count, 4) if i + 5 < count]
        self.edge = lax.ppermute(edge, "img", pairs_low + pairs_high)

    def second(self):
        across, above, below = self.clock.stage(self.across, self.above, self.below)
        self.across, self.above, self.below = across, above, below
        self.four_sent = jnp.concatenate([self.x, across, above, below], axis=0)
        self.above_across, self.below_across = shifted(across, 4), shifted(across, -4)
        self.clock.mark(self.four_sent)

    def third(self):
        four = crossed(self.four_sent, 1)
        self.above_across, self.below_across, self.four, self.edge = self.clock.stage(
            self.above_across, self.below_across, four, self.edge
        )
        self.two_sent = jnp.concatenate([self.above_across, self.below_across], axis=0)
        self.clock.mark(self.two_sent)

    def collect(self):
        two = self.clock.stage(crossed(self.two_sent, 1))
        self.clock.mark(two)
        return [self.x, self.across, self.above, self.below, self.four, self.above_across, self.below_across, two, self.edge]


PIECE_COUNTS = (1, 1, 1, 1, 4, 1, 1, 2, 1)


def neighbour_indices(i):
    b = i ^ 1
    edge = jnp.where(i % 4 == 0, i - 5, i + 5)
    return [i, i ^ 2, i + 4, i - 4, b, b ^ 2, b + 4, b - 4, (i ^ 2) + 4, (i ^ 2) - 4, (b ^ 2) + 4, (b ^ 2) - 4, edge]


def token_places(row_index, image_sides):
    heights = image_sides[:, 0]
    widths = image_sides[:, 1]
    lengths = heights * (widths + 1)
    sample_ends = jnp.cumsum(lengths, dtype=jnp.int32)
    starts = sample_ends - lengths
    sample_ids = ids_of(row_index, sample_ends)
    matched = jnp.arange(image_sides.shape[0], dtype=jnp.int32)[None, :] == sample_ids[:, None]
    first_row = jnp.sum(jnp.where(matched, starts[None, :], 0), axis=1, dtype=jnp.int32)
    row_width = jnp.sum(jnp.where(matched, widths[None, :] + 1, 0), axis=1, dtype=jnp.int32)
    row_width = jnp.maximum(row_width, 1)
    offset = row_index - first_row
    return (sample_ids, offset // row_width, offset % row_width, sample_ends)


def ids_of(rows, sample_ends):
    return jnp.sum((sample_ends <= rows[..., None]).astype(jnp.int32), axis=-1, dtype=jnp.int32)


def turn_tables(row_pos, col_pos):
    quarter = HD // 4
    frequency = 10000.0 ** (-jnp.arange(quarter, dtype=f32) / quarter)
    angles = jnp.concatenate(
        [row_pos.astype(f32)[:, None] * frequency[None, :], col_pos.astype(f32)[:, None] * frequency[None, :]], axis=1
    )
    cosine, sine = jnp.cos(angles), jnp.sin(angles)
    return jnp.concatenate([cosine] * 4, axis=1), jnp.concatenate([-sine, sine, -sine, sine], axis=1)


def rms_norm(values):
    return values * lax.rsqrt(jnp.mean(values * values, axis=-1, keepdims=True) + EPS_NORM)


def rms_back(values, d_normed):
    inverse = lax.rsqrt(jnp.mean(values * values, axis=-1, keepdims=True) + EPS_NORM)
    normed = values * inverse
    return inverse * (d_normed - normed * jnp.mean(d_normed * normed, axis=-1, keepdims=True))


def on_device(
    tokens, cotangent, text_states, conditions, image_sides, master, moment_one, moment_two, average,
    small_master, small_one, small_two, small_average,
):
    n_img = lax.axis_size("img")
    n_txt = lax.axis_size("txt")
    img_index = lax.axis_index("img")
    txt_index = lax.axis_index("txt")
    tok = tokens.shape[0]
    samples = image_sides.shape[0]
    half_d = D // n_txt
    half_ff = FF // n_txt
    local_heads = half_d // HD
    n_pairs = half_d // LANES

    tables = [
        (D // n_img, 2 * half_ff),
        (half_ff // n_img, D),
        (D // n_img, 3 * half_d),
        (TXT_D // n_img, 2 * half_d),
        (half_d // n_img, D),
        (COND // n_img, 6 * half_d),
    ]
    master_lines = master.reshape(-1, LANES)
    lines = master_lines.shape[0]
    starts = [0]
    for rows, columns in tables:
        starts.append(starts[-1] + rows * columns // LANES)

    def own_rows(*which):
        shapes = [tables[w] for w in which]
        return pl.pallas_call(
            functools.partial(unflatten_kernel, shapes),
            out_shape=[shape_of(s, bf16) for s in shapes],
            compiler_params=pltpu.CompilerParams(vmem_limit_bytes=58 * MIB),
        )(*(master_lines[starts[w] : starts[w + 1]] for w in which))

    def scatter(terms):
        return lax.psum_scatter(terms, "img", scatter_dimension=0, tiled=True)

    def gather(rows):
        return lax.all_gather(rows, "img", axis=0, tiled=True)

    together = [0, 1, 4, 2]
    shapes = [tables[w] for w in together]
    heights = [rows * columns // WIDE for rows, columns in shapes]
    if all(rows % 16 == 0 for rows, _ in shapes):
        block = pl.pallas_call(
            functools.partial(pack_kernel, shapes),
            out_shape=shape_of((sum(heights), WIDE), bf16),
            compiler_params=pltpu.CompilerParams(vmem_limit_bytes=58 * MIB),
        )(*(master_lines[starts[w] : starts[w + 1]] for w in together))
        blocks = gather(block[None])
    else:
        blocks = None
        natural = dict(zip(together, (gather(rows) for rows in own_rows(*together))))

    def weight(which):
        if blocks is None:
            array = natural[which]
            return array, lambda at, group=1: pl.BlockSpec((array.shape[0], group * WIDE), lambda j, *_: (0, at(j)))
        place = together.index(which)
        rows = shapes[place][0]
        first = sum(heights[:place]) // rows
        assert first * rows == sum(heights[:place])

        def spec(at, group=1):
            assert first % group == 0
            return pl.BlockSpec((n_img, group * rows, WIDE), lambda j, *_: (0, first // group + at(j), 0))

        return blocks, spec

    (own_modulate,) = own_rows(5)
    (own_text,) = own_rows(3)

    gain_attn = small_master[:D]
    gain_ffn = small_master[D : 2 * D]
    gain_query = small_master[2 * D : 2 * D + HD]
    gain_key = small_master[2 * D + HD : 2 * D + 2 * HD]
    gain_text = small_master[2 * D + 2 * HD : 2 * D + 3 * HD]
    gate_heads = small_master[2 * D + 3 * HD :]
    gate_local = lax.dynamic_slice_in_dim(gate_heads, txt_index * local_heads, local_heads)
    tanh_gate = jnp.tanh(gate_local)
    gate_lanes = jnp.repeat(tanh_gate, HD)[None, :]
    gain_query_pair = jnp.tile(gain_query, 2)[None, :]
    gain_key_pair = jnp.tile(gain_key, 2)[None, :]

    cond_rows = COND // n_img
    cond_own = lax.dynamic_slice_in_dim(conditions, img_index * cond_rows, cond_rows, 1)
    silu_own = jax.nn.silu(cond_own.astype(f32)).astype(bf16)
    mod_sum = sum_over_img(jnp.dot(silu_own, own_modulate, preferred_element_type=f32))
    mod_half = mod_sum.astype(bf16)
    mod_other = other_txt(mod_half)
    mods = jnp.where(
        txt_index == 0, jnp.stack([mod_half, mod_other], 0), jnp.stack([mod_other, mod_half], 0)
    ).reshape(n_txt, samples, 6, half_d).transpose(1, 2, 0, 3)

    row_index = img_index * tok + jnp.arange(tok, dtype=jnp.int32)
    sample_ids, row_pos, col_pos, sample_ends = token_places(row_index, image_sides)
    cosine, sine = turn_tables(row_pos, col_pos)
    one_hot = sample_ids[:, None] == jnp.arange(samples, dtype=jnp.int32)[None, :]
    per_token = jnp.dot(one_hot.astype(bf16), mods.reshape(samples, 6 * D), preferred_element_type=f32).astype(bf16)
    shift_one, scale_one, gate_one, shift_two, scale_two, gate_two = (
        per_token[:, c * D : (c + 1) * D].astype(f32) for c in range(6)
    )

    pieces = jnp.stack([jnp.asarray(p, jnp.int32) for p in neighbour_indices(img_index)])
    place = img_index % 4
    inside = (pieces >= 0) & (pieces < n_img)
    slots = jnp.arange(PIECES)
    inside &= (slots != PIECES - 1) | (place == 0) | (place == 3)
    column = jnp.arange(tok, dtype=jnp.int32)[None, :]
    edge_start = jnp.where((slots == PIECES - 1) & (place == 0), tok - EDGE, 0)
    piece_rows = pieces[:, None] * tok + column + edge_start[:, None]
    there = inside[:, None] & ((slots[:, None] < PIECES - 1) | (column < EDGE))
    piece_ids = jnp.where(there, ids_of(piece_rows, sample_ends), -1)
    flags = jnp.any((piece_ids >= sample_ids[0]) & (piece_ids <= sample_ids[-1]), axis=1).astype(jnp.int32)
    piece_ids = jnp.concatenate([piece_ids, jnp.full((16 - PIECES, tok), -1, jnp.int32)], axis=0)
    own_ids = sample_ids[:, None]

    text_rows = text_states.shape[0]
    text_len = text_rows * n_img
    text_columns = lax.all_to_all(text_states, "img", split_axis=1, concat_axis=0, tiled=True)
    z_first = [0] + list(range(2, index_bits(n_img))) + [1]
    text_proj = TermSum(Clock(), jnp.dot(text_columns, own_text, preferred_element_type=f32), z_first).finish()
    text_shape = (text_rows, local_heads, HD)
    text_raw = text_proj[:, :half_d].reshape(text_shape)
    text_normed = rms_norm(text_raw)
    text_key_low = (text_normed * gain_text).reshape(text_rows, half_d).astype(bf16)
    text_low = jnp.concatenate([text_key_low, text_proj[:, half_d:].astype(bf16)], axis=1)
    all_text = gather_doubling(text_low)

    if blocks is not None:
        blocks = tie(blocks, all_text, per_token, cosine, sine, flags, piece_ids)
    x_float = tokens.astype(f32)
    x_normed = rms_norm(x_float)
    normed_one = x_normed * gain_attn
    attn_in = (normed_one * (1.0 + scale_one) + shift_one).astype(bf16)
    def wide(rows, group=1):
        return pl.BlockSpec((rows, group * WIDE), lambda j, *_: (0, j))

    thirds = half_d // WIDE
    w_project, project_spec = weight(2)
    queries, own_kv, raw_qk = call(
        project_kernel,
        (thirds,),
        [whole((tok, D))]
        + [project_spec(lambda j, c=c: c * thirds + j) for c in range(3)]
        + [whole((1, LANES))] * 2
        + [whole((tok, LANES))] * 2,
        [wide(tok)] + [pl.BlockSpec((2, tok, WIDE), lambda j: (0, 0, j))] * 2,
        [
            shape_of((tok, half_d), bf16),
            shape_of((2, tok, half_d), bf16),
            shape_of((2, tok, half_d), f32),
        ],
        (attn_in, w_project, w_project, w_project, gain_query_pair, gain_key_pair, cosine, sine),
        flops=2 * tok * D * 3 * half_d,
        moved=2 * D * 3 * half_d,
    )
    clock = Clock()
    clock.mark(own_kv)
    kv_near = Neighbourhood(clock, own_kv, own_kv[:, tok - EDGE :], own_kv[:, :EDGE])
    w_updown, updown_spec = weight(0)
    w_down, down_spec = weight(1)
    w_output, output_spec = weight(4)
    if blocks is None:
        w_output_other = other_txt(w_output)
        other_spec = output_spec
    else:
        top = sum(heights[:2])
        w_output_other = other_txt(clock.stage(blocks)[:, top : top + heights[2]])
        other_spec = lambda at: pl.BlockSpec((n_img, shapes[2][0], WIDE), lambda j, *_: (0, at(j), 0))

    def step(j):
        return j

    kv_near.second()
    kv_near.third()
    kv_pieces = kv_near.collect()

    kv_specs = [pairs(2 * c, a.shape[1]) for c, a in zip(PIECE_COUNTS, kv_pieces)]
    id_specs = [whole((tok, 1)), whole((16, tok))]
    text_specs = [pair(text_len), pair(text_len, n_pairs)]
    own_queries = queries[None]
    query_near = Neighbourhood(clock, own_queries, own_queries[:, tok - EDGE :], own_queries[:, :EDGE])
    mixed_low, self_out, cross_out, lse_self, lse_cross, lse_split = call(
        functools.partial(attend_kernel, PIECE_COUNTS, tok),
        (n_pairs,),
        [pair(tok)] + id_specs + text_specs + [pair(1)] + kv_specs,
        [pair(tok)] * 5 + [whole((TABLE, 3 * tok))],
        [shape_of((tok, half_d), bf16)]
        + [shape_of((tok, half_d), f32)] * 4
        + [shape_of((TABLE, 3 * tok), bf16)],
        (flags, clock.stage(queries), own_ids, piece_ids, all_text, all_text, gate_lanes, *kv_pieces),
        scratch=[
            pltpu.VMEM((PIECES, 2 * tok, tok), f32),
            pltpu.VMEM((2 * tok, LANES), f32),
            pltpu.VMEM((2 * tok, LANES), f32),
            pltpu.VMEM((2 * tok, LANES), f32),
            pltpu.VMEM((TABLE, tok), f32),
        ],
        prefetch=1,
    )

    def pack_edges(pack):
        table = pack[:, tok:]
        ending = jnp.concatenate(
            [table[:, :, part * tok + tok - EDGE : (part + 1) * tok] for part in range(3) for _ in range(tok // EDGE)],
            axis=2,
        )
        return (
            jnp.concatenate([pack[:, tok - EDGE : tok], ending], axis=1),
            jnp.concatenate([pack[:, :EDGE], table], axis=1),
        )

    clock.mark(mixed_low)
    mixed_other = other_txt(mixed_low)
    query_near.second()
    mixed_other, mixed_low = clock.stage(mixed_other, mixed_low)
    attn_out = call(
        two_times_kernel,
        (D // WIDE,),
        [whole((tok, half_d)), output_spec(step), whole((tok, half_d)), other_spec(step)],
        [wide(tok)],
        [shape_of((tok, D), f32)],
        (mixed_low, w_output, mixed_other, w_output_other),
        flops=4 * tok * half_d * D,
        moved=4 * half_d * D,
    )[0]
    clock.mark(attn_out)
    hidden = x_float + gate_one * attn_out
    h_normed = rms_norm(hidden)
    normed_two = h_normed * gain_ffn
    ffn_in = (normed_two * (1.0 + scale_two) + shift_two).astype(bf16)
    clock.mark(ffn_in)
    query_near.third()
    gate, up, hidden_units, hidden_turned = call(
        hidden_kernel,
        (half_ff // WIDE,),
        [whole((tok, D)), updown_spec(step), updown_spec(lambda j: half_ff // WIDE + j)],
        [wide(tok)] * 3 + [pl.BlockSpec((WIDE, tok), lambda j: (j, 0))],
        [shape_of((tok, half_ff), f32)] * 2 + [shape_of((tok, half_ff), bf16), shape_of((half_ff, tok), bf16)],
        (clock.stage(ffn_in), w_updown, w_updown),
        flops=4 * tok * D * half_ff,
        moved=4 * D * half_ff,
    )
    clock.mark(hidden_turned)
    query_pieces = query_near.collect()
    d_out = cotangent.astype(f32)
    d_branch = (d_out * gate_two).astype(bf16)
    down_terms = mm(clock.stage(hidden_turned), d_branch, 1, 0).astype(bf16)
    clock.mark(down_terms)
    grad_down = scatter(down_terms)
    d_gate, d_up = call(
        hidden_back_kernel,
        (D // WIDE // 3,),
        [wide(tok, 3), down_spec(step, 3), whole((tok, half_ff)), whole((tok, half_ff))],
        [whole((tok, half_ff))] * 2,
        [shape_of((tok, half_ff), bf16)] * 2,
        (clock.stage(d_branch), w_down, gate, up),
        scratch=[pltpu.VMEM((tok, half_ff), f32)],
        flops=2 * tok * D * half_ff,
        moved=2 * D * half_ff,
    )
    clock.mark(d_gate, d_up)
    d_gate_up = clock.stage(jnp.concatenate([d_gate, d_up], axis=1))
    d_ffn_part = call(
        times_transposed_kernel,
        (2 * half_ff // WIDE // 4,),
        [wide(tok, 4), updown_spec(step, 4)],
        [whole((tok, D))],
        [shape_of((tok, D), bf16)],
        (d_gate_up, w_updown),
        scratch=[pltpu.VMEM((tok, D), f32)],
        flops=4 * tok * D * half_ff,
        moved=4 * D * half_ff,
    )[0]
    clock.mark(d_ffn_part)
    d_ffn_other = other_txt(d_ffn_part)
    updown_terms = mm(clock.stage(ffn_in), d_gate_up, 0, 0).astype(bf16)
    clock.mark(updown_terms)
    grad_updown = scatter(updown_terms)
    d_ffn_part, d_ffn_other = clock.stage(d_ffn_part, d_ffn_other)
    d_ffn_in = d_ffn_part.astype(f32) + d_ffn_other.astype(f32)
    d_scale_two = d_ffn_in * normed_two
    d_normed_two = d_ffn_in * (1.0 + scale_two)
    d_gain_ffn = jnp.sum(d_normed_two * h_normed, axis=0)
    d_hidden = d_out + rms_back(hidden, d_normed_two * gain_ffn)
    d_attn = (d_hidden * gate_one).astype(bf16)
    clock.mark(d_attn)
    grad_pack, d_cross_low, d_gate_lanes = call(
        functools.partial(mixed_back_kernel, tok),
        (D // WIDE // 3,),
        [wide(tok, 3), output_spec(step, 3), whole((tok, half_d)), whole((tok, half_d)), whole((1, half_d)), whole((TABLE, 3 * tok))],
        [whole((1, tok + PACK, half_d)), whole((tok, half_d)), whole((1, half_d))],
        [
            shape_of((1, tok + PACK, half_d), bf16),
            shape_of((tok, half_d), bf16),
            shape_of((1, half_d), f32),
        ],
        (clock.stage(d_attn), w_output, self_out, cross_out, gate_lanes, lse_split),
        scratch=[pltpu.VMEM((tok, half_d), f32)],
        flops=2 * tok * D * half_d,
        moved=2 * D * half_d,
    )
    clock.mark(grad_pack)
    grad_near = Neighbourhood(clock, grad_pack, *pack_edges(grad_pack))
    branch_part = call(
        times_kernel,
        (D // WIDE,),
        [whole((tok, half_ff)), down_spec(step)],
        [wide(tok)],
        [shape_of((tok, D), f32)],
        (clock.stage(hidden_units), w_down),
        flops=2 * tok * D * half_ff,
        moved=2 * D * half_ff,
    )[0]
    clock.mark(branch_part)
    branch_other = other_txt(branch_part)
    output_sum = GradientSum(clock, tall(mixed_low), d_attn)
    grad_near.second()
    turn_specs = [whole((1, LANES)), whole((tok, LANES)), whole((tok, LANES))]

    def query_back(first, count, d_cross):
        def at(rows, also=0):
            return pair(rows, first + also)

        def some(arrays, rows, index=0):
            return pl.BlockSpec((arrays, rows, LANES), lambda j, *_: (index, 0, first + j))

        return call(
            functools.partial(query_back_kernel, PIECE_COUNTS, tok),
            (count,),
            [at(tok)]
            + id_specs
            + [at(text_len), at(text_len, n_pairs)]
            + [some(1, tok), at(tok)]
            + [at(tok)] * 4
            + [some(1, tok)]
            + turn_specs
            + [some(2 * c, a.shape[1]) for c, a in zip(PIECE_COUNTS, kv_pieces)],
            [pair(tok), pair(1), pair(text_len), pair(text_len)],
            [
                shape_of((tok, count * LANES), bf16),
                shape_of((1, count * LANES), f32),
                shape_of((text_len, count * LANES), f32),
                shape_of((text_len, count * LANES), f32),
            ],
            (
                flags, queries, own_ids, piece_ids, all_text, all_text, grad_pack, d_cross,
                self_out, cross_out, lse_self, lse_cross, raw_qk, gain_query_pair, cosine, sine, *kv_pieces,
            ),
            scratch=[pltpu.VMEM((2 * tok, LANES), f32)],
            prefetch=1,
        )

    head_half = n_pairs // 2
    first_half = query_back(0, head_half, clock.stage(d_cross_low))
    clock.mark(first_half[0])
    grad_near.third()
    output_sum.advance()
    grad_pieces = grad_near.collect()
    second_half = query_back(head_half, n_pairs - head_half, clock.stage(d_cross_low))
    clock.mark(second_half[0])
    d_query_raw, d_gain_query, d_text_key, d_text_value = (
        jnp.concatenate(halves, axis=1) for halves in zip(first_half, second_half)
    )
    attn_tall = tall(attn_in)
    text_sum = TermSum(clock, jnp.concatenate([d_text_key, d_text_value], axis=1), z_first)
    query_sum = GradientSum(clock, attn_tall, d_query_raw)
    output_sum.advance()
    text_sum.advance()
    branch_other = clock.stage(branch_other)

    query_specs = [pairs(c, a.shape[1]) for c, a in zip(PIECE_COUNTS, query_pieces)]
    pack_specs = [pairs(c, a.shape[1] - PACK) for c, a in zip(PIECE_COUNTS, grad_pieces)] + [
        pl.BlockSpec((c, PACK, half_d), lambda j, *_, at=(a.shape[1] - PACK) // PACK: (0, at, 0))
        for c, a in zip(PIECE_COUNTS, grad_pieces)
    ]

    d_key_raw, d_gain_key, d_value = call(
        functools.partial(key_back_kernel, PIECE_COUNTS, tok),
        (n_pairs,),
        [pairs(2, tok)]
        + id_specs
        + [pairs(1, tok, 1)]
        + turn_specs
        + query_specs
        + pack_specs,
        [pair(tok), pair(1), pair(tok)],
        [
            shape_of((tok, half_d), bf16),
            shape_of((1, half_d), f32),
            shape_of((tok, half_d), bf16),
        ],
        (
            flags, clock.stage(own_kv), own_ids, piece_ids, raw_qk, gain_key_pair,
            cosine, sine, *query_pieces, *grad_pieces, *grad_pieces,
        ),
        scratch=[pltpu.VMEM((2 * tok, LANES), f32)] * 2,
        prefetch=1,
    )
    clock.mark(d_value)
    key_value_sum = GradientSum(clock, attn_tall, jnp.concatenate([d_key_raw, d_value], axis=1))
    d_projected = clock.stage(jnp.concatenate([d_query_raw, d_key_raw, d_value], axis=1))
    d_attn_part = call(
        times_transposed_kernel,
        (thirds,),
        [wide(tok, 3), project_spec(step, 3)],
        [whole((tok, D))],
        [shape_of((tok, D), bf16)],
        (d_projected, w_project),
        scratch=[pltpu.VMEM((tok, D), f32)],
        flops=6 * tok * D * half_d,
        moved=6 * D * half_d,
    )[0]
    clock.mark(d_attn_part)
    d_attn_other = other_txt(d_attn_part)
    query_sum.advance()
    key_value_sum.advance()
    text_sum.advance()
    output_sum.advance()
    d_attn_other = clock.stage(d_attn_other)
    d_attn_in = d_attn_part.astype(f32) + d_attn_other.astype(f32)
    branch = branch_part + branch_other
    block_out = hidden + gate_two * branch
    d_gate_two = d_out * branch
    d_gate_one = d_hidden * attn_out
    d_scale_one = d_attn_in * normed_one
    d_normed_one = d_attn_in * (1.0 + scale_one)
    d_gain_attn = jnp.sum(d_normed_one * x_normed, axis=0)
    d_tokens = d_hidden + rms_back(x_float, d_normed_one * gain_attn)

    one_hot_wide = one_hot.astype(f32)

    def by_sample(values):
        summed = lax.dot_general(one_hot_wide, values, (((0,), (0,)), ((), ())), precision=HIGH)
        return lax.dynamic_slice_in_dim(summed, txt_index * half_d, half_d, 1)

    d_mod = jnp.concatenate(
        [by_sample(v) for v in (d_attn_in, d_scale_one, d_gate_one, d_ffn_in, d_scale_two, d_gate_two)], axis=1
    )

    replica = (txt_index == 0).astype(f32)
    d_gate_local = jnp.sum(d_gate_lanes.reshape(local_heads, HD), axis=1) * (1.0 - tanh_gate**2)
    gate_full = lax.dynamic_update_slice(jnp.zeros((HEADS,), f32), d_gate_local, (txt_index * local_heads,))
    small_terms = jnp.concatenate(
        [
            d_gain_attn * replica,
            d_gain_ffn * replica,
            jnp.sum(d_gain_query.reshape(local_heads, HD), axis=0),
            jnp.sum(d_gain_key.reshape(local_heads, HD), axis=0),
            jnp.zeros((HD,), f32),
            gate_full,
        ]
    )
    small_count = small_terms.shape[0]
    small_row = jnp.pad(small_terms, (0, d_mod.shape[1] - small_count))[None]
    small_sum = SmallSum(clock, jnp.concatenate([d_mod, small_row], axis=0))
    query_sum.advance()
    text_sum.advance()
    small_sum.advance()
    key_value_sum.advance()

    text_own = text_sum.finish()
    d_text_scaled = text_own[:, :half_d].reshape(text_shape)
    d_gain_text = jnp.sum(d_text_scaled * text_normed, axis=(0, 1))
    d_text_raw = rms_back(text_raw, d_text_scaled * gain_text).reshape(text_rows, half_d)
    d_text_proj = gather_doubling(jnp.concatenate([d_text_raw, text_own[:, half_d:]], axis=1).astype(bf16))
    grad_text = mm(text_columns, d_text_proj, 0, 0)

    small_sum.advance()
    query_sum.advance()
    key_value_sum.advance()
    sums = small_sum.finish()
    d_mod = sums[:samples]
    small_row = sums[samples:, :]
    small_grad = (small_row + other_txt(small_row))[0, :small_count]
    grad_modulate = lax.dot_general(silu_own.astype(f32), d_mod, (((0,), (0,)), ((), ())), precision=HIGH)

    pending = [output_sum, query_sum, key_value_sum]
    while pending:
        for one in list(pending):
            if one.result is None:
                one.result = one.advance()
            if one.result is not None:
                pending.remove(one)
    grads = [grad_updown, grad_down, query_sum.result, grad_text, output_sum.result, grad_modulate, key_value_sum.result]
    places = [(start, 0, columns) for start, (_, columns) in zip(starts, tables)]
    places.append((starts[2], half_d, 3 * half_d))
    reduced, squares = pl.pallas_call(
        functools.partial(flatten_kernel, places),
        out_shape=[shape_of((lines, LANES), f32), shape_of((1, LANES), f32)],
        compiler_params=pltpu.CompilerParams(vmem_limit_bytes=58 * MIB),
    )(*grads)

    last = sum_over_all(jnp.concatenate([squares, jnp.pad(d_gain_text, (0, LANES - HD))[None]], axis=0))
    small_grad = lax.dynamic_update_slice(small_grad, last[1, :HD], (2 * D + 2 * HD,))
    grad_square = jnp.sum(last[0]) + jnp.sum(small_grad * small_grad)
    clip_factor = MAX_NORM / jnp.maximum(jnp.sqrt(grad_square), MAX_NORM)

    block = math.gcd(lines, 1024)
    line_spec = pl.BlockSpec((block, LANES), lambda i: (i, 0))
    as_lines = (lines, LANES)
    updated = call(
        update_kernel,
        (lines // block,),
        [pl.BlockSpec(memory_space=pltpu.SMEM)] + [line_spec] * 5,
        [line_spec] * 5,
        [shape_of(as_lines, f32)] * 4 + [shape_of(as_lines, bf16)],
        (clip_factor.reshape(1), reduced, *(a.reshape(as_lines) for a in (moment_one, moment_two, master, average))),
        flops=20 * lines * LANES,
        moved=38 * lines * LANES,
    )
    one_new, two_new, master_new, average_new, master_low = (a.reshape(master.shape) for a in updated)
    small_one_new, small_two_new, small_new, small_average_new = adam_update(
        small_grad * clip_factor, small_one, small_two, small_master, small_average, RATE_SMALL, 0.0
    )
    return (
        block_out,
        d_tokens,
        grad_square,
        one_new,
        two_new,
        master_new,
        average_new,
        master_low,
        small_one_new,
        small_two_new,
        small_new,
        small_average_new,
    )


def solution(mesh):
    rows = P("img", None)
    shards = P("img", "txt", None)
    in_specs = (rows, rows, rows, P(), P(), shards, shards, shards, shards, P(), P(), P(), P())
    out_specs = (rows, rows, P(), shards, shards, shards, shards, shards, P(), P(), P(), P())
    return jax.shard_map(on_device, mesh=mesh, in_specs=in_specs, out_specs=out_specs, check_vma=False)
```

```python
import functools
import math

import jax
import jax.numpy as jnp
from jax import lax
from jax.experimental import pallas as pl
from jax.experimental.pallas import tpu as pltpu
from jax.sharding import PartitionSpec as P

D = 1536
HEADS = 24
HD = 64
FF = 4096
TXT_D = 4096
COND = 1024
SIDE_MAX = 32
STEP = 10

HIGH = lax.Precision.HIGHEST
EPS_NORM = 1e-06
MAX_NORM = 1.0
BETA_ONE = 0.5
BETA_TWO = 0.5
RATE_MATRIX = 0.01
RATE_SMALL = 0.1
DECAY_WEIGHT = 0.01
ADAM_EPS = 1e-08
EMA_DECAY = 0.8

LANES = 128
EDGE = 128
TABLE = 16
PACK = 2 * TABLE
WIDE = 256
PIECES = 13
MASKED = -1e30
MIB = 1024 * 1024

bf16 = jnp.bfloat16
f32 = jnp.float32


def mm(a, b, on_a, on_b):
    return lax.dot_general(a, b, (((on_a,), (on_b,)), ((), ())), preferred_element_type=f32)


def lane_index(rows):
    return lax.broadcasted_iota(jnp.int32, (rows, LANES), 1)


def head_sum(values):
    low = lane_index(values.shape[0]) < HD
    first = jnp.sum(jnp.where(low, values, 0.0), axis=1, keepdims=True)
    second = jnp.sum(jnp.where(low, 0.0, values), axis=1, keepdims=True)
    return jnp.where(low, first, second)


def swap_halves(values):
    first = lane_index(values.shape[0]) % HD < HD // 2
    return jnp.where(
        first, pltpu.roll(values, LANES - HD // 2, 1), pltpu.roll(values, HD // 2, 1)
    )


def two_heads(pair):
    low = lane_index(pair.shape[0]) < HD
    zero = jnp.zeros_like(pair)
    return jnp.concatenate([jnp.where(low, pair, zero), jnp.where(low, zero, pair)], axis=0)


def one_pair(stacked):
    rows = stacked.shape[0] // 2
    low = lane_index(rows) < HD
    return jnp.where(low, stacked[:rows], stacked[rows:])


def columns_of(spread):
    return jnp.concatenate([spread[:, :1], spread[:, HD : HD + 1]], axis=0)


def norm_rope(raw, gain, cosine, sine):
    inverse = lax.rsqrt(head_sum(raw * raw) * (1.0 / HD) + EPS_NORM)
    scaled = raw * inverse * gain
    return scaled * cosine + swap_halves(scaled) * sine


def norm_rope_back(raw, gain, cosine, sine, d_out):
    inverse = lax.rsqrt(head_sum(raw * raw) * (1.0 / HD) + EPS_NORM)
    normed = raw * inverse
    d_scaled = d_out * cosine - swap_halves(d_out) * sine
    d_gain = jnp.sum(d_scaled * normed, axis=0, keepdims=True)
    d_normed = d_scaled * gain
    d_raw = inverse * (d_normed - normed * (head_sum(d_normed * normed) * (1.0 / HD)))
    return d_raw, d_gain


def split_three(values):
    high = values.astype(bf16)
    rest = values - high.astype(f32)
    middle = rest.astype(bf16)
    last = (rest - middle.astype(f32)).astype(bf16)
    return jnp.concatenate([high, middle, last], axis=1)


def joined(packed, rows):
    wide = packed.astype(f32)
    return wide[:, :rows] + wide[:, rows : 2 * rows] + wide[:, 2 * rows : 3 * rows]


def put_row(table, index, row):
    at = lax.broadcasted_iota(jnp.int32, table.shape, 0) == index
    return jnp.where(at, row, table)


def take_row(table, index):
    at = lax.broadcasted_iota(jnp.int32, table.shape, 0) == index
    return jnp.sum(jnp.where(at, table, 0.0), axis=0, keepdims=True)


def as_row(column):
    return jnp.broadcast_to(column, (column.shape[0], LANES)).T[:1]


def tile(ref):
    return ref[...].reshape(-1, WIDE)


def tiles(ref, count):
    if len(ref.shape) == 2:
        return [ref[:, at * WIDE : (at + 1) * WIDE] for at in range(count)]
    rows = ref.shape[1] // count
    return [ref[:, at * rows : (at + 1) * rows, :].reshape(-1, WIDE) for at in range(count)]


def add_transposed(acc_ref, a_ref, w_ref):
    count = a_ref.shape[1] // WIDE
    blocks = tiles(w_ref, count)
    for row in range(0, acc_ref.shape[1], WIDE):
        part = slice(row, row + WIDE)
        total = mm(a_ref[:, :WIDE], blocks[0][part], 1, 1)
        for at in range(1, count):
            total = total + mm(a_ref[:, at * WIDE : (at + 1) * WIDE], blocks[at][part], 1, 1)
        acc_ref[:, part] += total


def project_kernel(a_ref, wq_ref, wk_ref, wv_ref, gq_ref, gk_ref, cos_ref, sin_ref, qkv_ref, raw_ref):
    a = a_ref[...]
    cosine, sine = cos_ref[...], sin_ref[...]
    raw_q = mm(a, tile(wq_ref), 1, 0)
    raw_k = mm(a, tile(wk_ref), 1, 0)
    raw_ref[0] = raw_q
    raw_ref[1] = raw_k
    for at in range(0, WIDE, LANES):
        part = slice(at, at + LANES)
        query = norm_rope(raw_q[:, part], gq_ref[...], cosine, sine).astype(bf16)
        qkv_ref[0, :, part] = query * jnp.asarray(HD**-0.5, bf16)
        qkv_ref[1, :, part] = norm_rope(raw_k[:, part], gk_ref[...], cosine, sine).astype(bf16)
    qkv_ref[2] = mm(a, tile(wv_ref), 1, 0).astype(bf16)


def times_kernel(a_ref, w_ref, out_ref):
    out_ref[...] = mm(a_ref[...], tile(w_ref), 1, 0).astype(out_ref.dtype)


def times_transposed_kernel(a_ref, w_ref, out_ref, acc_ref):
    step = pl.program_id(0)

    @pl.when(step == 0)
    def _():
        acc_ref[...] = jnp.zeros(acc_ref.shape, f32)

    add_transposed(acc_ref, a_ref, w_ref)

    @pl.when(step == pl.num_programs(0) - 1)
    def _():
        out_ref[...] = acc_ref[...].astype(out_ref.dtype)


def input_back_kernel(d_query_ref, d_key_value_ref, w_ref, out_ref, acc_ref):
    step = pl.program_id(0)
    half = d_query_ref.shape[1]

    @pl.when(step == 0)
    def _():
        acc_ref[...] = jnp.zeros(acc_ref.shape, f32)
        add_transposed(acc_ref, d_query_ref, w_ref)

    for at in range(2):

        @pl.when(step == at + 1)
        def _(at=at):
            add_transposed(acc_ref, d_key_value_ref.at[:, at * half : (at + 1) * half], w_ref)

    @pl.when(step == 2)
    def _():
        out_ref[...] = acc_ref[...].astype(out_ref.dtype)


def hidden_kernel(b_ref, w_gate_ref, w_up_ref, gate_ref, up_ref, hidden_ref, turned_ref):
    gate = mm(b_ref[...], tile(w_gate_ref), 1, 0)
    up = mm(b_ref[...], tile(w_up_ref), 1, 0)
    hidden = (gate * jax.nn.sigmoid(gate) * up).astype(bf16)
    gate_ref[...] = gate
    up_ref[...] = up
    hidden_ref[...] = hidden
    turned_ref[...] = hidden.T


def hidden_back_kernel(d_branch_ref, w_ref, gate_ref, up_ref, d_ref, acc_ref):
    step = pl.program_id(0)

    @pl.when(step == 0)
    def _():
        acc_ref[...] = jnp.zeros(acc_ref.shape, f32)

    add_transposed(acc_ref, d_branch_ref, w_ref)

    @pl.when(step == pl.num_programs(0) - 1)
    def _():
        for at in range(0, acc_ref.shape[1], WIDE):
            part = slice(at, at + WIDE)
            d_units, gate = acc_ref[:, part], gate_ref[:, part]
            sigmoid = jax.nn.sigmoid(gate)
            d_gate = d_units * up_ref[:, part] * sigmoid * (1.0 + gate * (1.0 - sigmoid))
            d_ref[:, part] = d_gate.astype(bf16)
            d_ref[:, acc_ref.shape[1] + at : acc_ref.shape[1] + at + WIDE] = (d_units * (gate * sigmoid)).astype(bf16)


def piece_views(piece_refs, counts, per):
    views = []
    for ref, count in zip(piece_refs, counts):
        for at in range(count):
            views.append((ref, at * per))
    return views


def attend_kernel(counts, tok, flag_ref, q_ref, own_ids_ref, ids_ref, tk_ref, tv_ref, gate_ref, *rest):
    pieces = piece_views(rest[: len(counts)], counts, 3)
    mixed_ref, self_ref, cross_ref, lse_self_ref, lse_cross_ref, split_ref = rest[len(counts) : len(counts) + 6]
    scores_ref, most_ref, total_ref, acc_ref, table_ref = rest[len(counts) + 6 :]
    step = pl.program_id(0)
    own_ids = own_ids_ref[...]
    q_two = two_heads(q_ref[0])
    own_two = jnp.concatenate([own_ids, own_ids], axis=0)
    most_ref[...] = jnp.full(most_ref.shape, MASKED, f32)
    total_ref[...] = jnp.zeros(total_ref.shape, f32)
    acc_ref[...] = jnp.zeros(acc_ref.shape, f32)
    for slot, (ref, at) in enumerate(pieces):
        rows = ref.shape[1]

        @pl.when(flag_ref[slot] > 0)
        def _(slot=slot, ref=ref, at=at, rows=rows):
            scores = mm(q_two, ref[at + 1], 1, 1)
            scores = jnp.where(own_two == ids_ref[slot : slot + 1, :rows], scores, MASKED)
            scores_ref[slot, :, :rows] = scores
            most = most_ref[...]
            for part in range(rows // LANES):
                most = jnp.maximum(most, scores[:, part * LANES : (part + 1) * LANES])
            most_ref[...] = most

    row_most = jnp.max(most_ref[...], axis=1, keepdims=True)
    for slot, (ref, at) in enumerate(pieces):
        rows = ref.shape[1]

        @pl.when(flag_ref[slot] > 0)
        def _(slot=slot, ref=ref, at=at, rows=rows):
            weights = jnp.exp(scores_ref[slot, :, :rows] - row_most)
            total = total_ref[...]
            for part in range(rows // LANES):
                total = total + weights[:, part * LANES : (part + 1) * LANES]
            total_ref[...] = total
            acc_ref[...] += mm(weights.astype(bf16), ref[at + 2], 1, 0)

    row_total = jnp.sum(total_ref[...], axis=1, keepdims=True)
    self_out = one_pair(acc_ref[...] / row_total)
    lse_self = row_most + jnp.log(row_total)

    cross_scores = mm(q_two, tk_ref[...], 1, 1)
    cross_most = jnp.max(cross_scores, axis=1, keepdims=True)
    cross_weights = jnp.exp(cross_scores - cross_most)
    cross_total = jnp.sum(cross_weights, axis=1, keepdims=True)
    cross_out = one_pair(mm(cross_weights.astype(bf16), tv_ref[...], 1, 0) / cross_total)
    lse_cross = cross_most + jnp.log(cross_total)

    self_ref[...] = self_out
    cross_ref[...] = cross_out
    mixed_ref[...] = (self_out + gate_ref[...] * cross_out).astype(bf16)
    spread = (tok, LANES)
    low = lane_index(tok) < HD
    lse_self_ref[...] = jnp.where(
        low, jnp.broadcast_to(lse_self[:tok], spread), jnp.broadcast_to(lse_self[tok:], spread)
    )
    lse_cross_ref[...] = jnp.where(
        low, jnp.broadcast_to(lse_cross[:tok], spread), jnp.broadcast_to(lse_cross[tok:], spread)
    )

    @pl.when(step == 0)
    def _():
        table_ref[...] = jnp.zeros(table_ref.shape, f32)

    table = put_row(table_ref[...], 2 * step, as_row(lse_self[:tok]))
    table = put_row(table, 2 * step + 1, as_row(lse_self[tok:]))
    table_ref[...] = table

    @pl.when(step == pl.num_programs(0) - 1)
    def _():
        split_ref[...] = split_three(table_ref[...])


def mixed_back_kernel(tok, d_attn_ref, w_ref, self_ref, cross_ref, gate_ref, lse_ref, pack_ref, d_cross_ref, d_gate_ref, acc_ref):
    step = pl.program_id(0)

    @pl.when(step == 0)
    def _():
        acc_ref[...] = jnp.zeros(acc_ref.shape, f32)

    add_transposed(acc_ref, d_attn_ref, w_ref)

    @pl.when(step == pl.num_programs(0) - 1)
    def _():
        rows = []
        for at in range(0, acc_ref.shape[1], LANES):
            part = slice(at, at + LANES)
            d_mixed = acc_ref[:, part]
            d_self = d_mixed.astype(bf16)
            d_cross_ref[:, part] = (gate_ref[:, part] * d_mixed).astype(bf16)
            d_gate_ref[:, part] = jnp.sum(d_mixed * cross_ref[:, part], axis=0, keepdims=True)
            delta = head_sum(d_self.astype(f32) * self_ref[:, part])
            rows += [as_row(delta[:, :1]), as_row(delta[:, HD : HD + 1])]
            pack_ref[0, :tok, part] = d_self
        rows += [jnp.zeros_like(rows[0])] * (TABLE - len(rows))
        pack_ref[0, tok : tok + TABLE, :] = split_three(jnp.concatenate(rows, axis=0))
        pack_ref[0, tok + TABLE :, :] = lse_ref[...]


def query_back_kernel(
    counts, tok, flag_ref, q_ref, own_ids_ref, ids_ref, tk_ref, tv_ref, d_self_ref, d_cross_ref,
    self_ref, cross_ref, lse_self_ref, lse_cross_ref, raw_ref, gain_ref, cos_ref, sin_ref, *rest
):
    pieces = piece_views(rest[: len(counts)], counts, 3)
    d_raw_ref, d_gain_ref, d_tk_ref, d_tv_ref, acc_ref = rest[len(counts) :]
    own_ids = own_ids_ref[...]
    own_two = jnp.concatenate([own_ids, own_ids], axis=0)
    q_two = two_heads(q_ref[0])
    d_self = d_self_ref[0]
    d_self_two = two_heads(d_self)
    delta = columns_of(head_sum(d_self.astype(f32) * self_ref[...]))
    lse = columns_of(lse_self_ref[...])

    d_cross = d_cross_ref[...]
    d_cross_two = two_heads(d_cross)
    delta_cross = columns_of(head_sum(d_cross.astype(f32) * cross_ref[...]))
    lse_cross = columns_of(lse_cross_ref[...])
    cross_p = jnp.exp(mm(q_two, tk_ref[...], 1, 1) - lse_cross)
    d_cross_p = mm(d_cross_two, tv_ref[...], 1, 1)
    d_cross_s = (cross_p * (d_cross_p - delta_cross)).astype(bf16)
    d_tv_ref[...] = mm(cross_p.astype(bf16), d_cross_two, 0, 0)
    d_tk_ref[...] = mm(d_cross_s, q_two, 0, 0)
    acc_ref[...] = mm(d_cross_s, tk_ref[...], 1, 0)
    for slot, (ref, at) in enumerate(pieces):
        rows = ref.shape[1]

        @pl.when(flag_ref[slot] > 0)
        def _(slot=slot, ref=ref, at=at, rows=rows):
            key = ref[at + 1]
            scores = mm(q_two, key, 1, 1)
            scores = jnp.where(own_two == ids_ref[slot : slot + 1, :rows], scores, MASKED)
            weights = jnp.exp(scores - lse)
            d_weights = mm(d_self_two, ref[at + 2], 1, 1)
            d_scores = (weights * (d_weights - delta)).astype(bf16)
            acc_ref[...] += mm(d_scores, key, 1, 0)

    d_query = one_pair(acc_ref[...]) * (HD**-0.5)
    d_raw, d_gain = norm_rope_back(raw_ref[0], gain_ref[...], cos_ref[...], sin_ref[...], d_query)
    d_raw_ref[...] = d_raw.astype(bf16)
    d_gain_ref[...] = d_gain


def key_back_kernel(counts, tok, flag_ref, k_ref, v_ref, own_ids_ref, ids_ref, raw_ref, gain_ref, cos_ref, sin_ref, *rest):
    n = len(counts)
    q_views = piece_views(rest[:n], counts, 3)
    g_views = piece_views(rest[n : 2 * n], counts, 1)
    g_tables = piece_views(rest[2 * n : 3 * n], counts, 1)
    d_both_ref, d_gain_ref, acc_k_ref, acc_v_ref = rest[3 * n :]
    step = pl.program_id(0)
    own_ids = own_ids_ref[...]
    k_two = two_heads(k_ref[0])
    v_two = two_heads(v_ref[0])
    acc_k_ref[...] = jnp.zeros(acc_k_ref.shape, f32)
    acc_v_ref[...] = jnp.zeros(acc_v_ref.shape, f32)
    for slot in range(PIECES):
        q_ref, q_at = q_views[slot]
        g_ref, at = g_views[slot]
        rows = q_ref.shape[1]
        @pl.when(flag_ref[slot] > 0)
        def _(slot=slot, q_ref=q_ref, q_at=q_at, g_ref=g_ref, at=at, rows=rows):
            query = q_ref[q_at]
            d_self = g_ref[at]
            tables = joined(g_tables[slot][0][at], tok)[:, :rows]
            delta, lse = tables[:TABLE], tables[TABLE:]
            same = own_ids == ids_ref[slot : slot + 1, :rows]
            scores = mm(k_two, query, 1, 1)
            d_weights = mm(v_two, d_self, 1, 1)
            p_low, d_low = [], []
            for head in range(2):
                part = slice(head * tok, (head + 1) * tok)
                masked = jnp.where(same, scores[part], MASKED)
                weights = jnp.exp(masked - take_row(lse, 2 * step + head))
                p_low.append(weights.astype(bf16))
                d_low.append((weights * (d_weights[part] - take_row(delta, 2 * step + head))).astype(bf16))
            acc_v_ref[...] += mm(jnp.concatenate(p_low, axis=0), d_self, 1, 0)
            acc_k_ref[...] += mm(jnp.concatenate(d_low, axis=0), query, 1, 0)

    d_raw, d_gain = norm_rope_back(
        raw_ref[0], gain_ref[...], cos_ref[...], sin_ref[...], one_pair(acc_k_ref[...])
    )
    d_gain_ref[...] = d_gain
    place = pl.multiple_of(step * LANES, LANES)
    d_both_ref[:, pl.ds(place, LANES)] = d_raw.astype(bf16)
    half = pl.num_programs(0) * LANES
    d_both_ref[:, pl.ds(pl.multiple_of(half + place, LANES), LANES)] = one_pair(acc_v_ref[...]).astype(bf16)


def place_rows(lines_ref, start, table, out_ref, top=None):
    rows, columns = table
    per_row = columns // LANES
    for at in range(per_row):
        part = lines_ref[pl.ds(start + at, rows, stride=per_row), :].astype(bf16)
        if top is None:
            out_ref[:, at * LANES : (at + 1) * LANES] = part
        else:
            row, lane = top + at // (WIDE // LANES) * rows, at % (WIDE // LANES) * LANES
            out_ref[row : row + rows, lane : lane + LANES] = part


def own_rows_kernel(tables, starts, packed, apart, lines_ref, *out_refs):
    top = 0
    for which in packed:
        rows, columns = tables[which]
        place_rows(lines_ref, starts[which], tables[which], out_refs[0], top)
        top += columns // WIDE * rows
    for which, ref in zip(apart, out_refs[bool(packed) :]):
        place_rows(lines_ref, starts[which], tables[which], ref)


def flatten_kernel(places, *refs):
    *in_refs, lines_ref, square_ref = refs
    grad_refs = in_refs[: len(places)]
    square = jnp.zeros((1, LANES), f32)
    for (start, column, columns), ref in zip(places, grad_refs):
        for at in range(ref.shape[1] // LANES):
            part = ref[:, at * LANES : (at + 1) * LANES].astype(f32)
            lines_ref[pl.ds(start + column // LANES + at, ref.shape[0], stride=columns // LANES), :] = part
            square = square + jnp.sum(part * part, axis=0, keepdims=True)
    square_ref[...] = square


def update_kernel(clip_ref, g_ref, one_ref, two_ref, w_ref, avg_ref, one_out, two_out, w_out, avg_out, low_out):
    one, two, weight, moving = adam_update(
        g_ref[...] * clip_ref[0], one_ref[...], two_ref[...], w_ref[...], avg_ref[...], RATE_MATRIX, DECAY_WEIGHT
    )
    one_out[...] = one
    two_out[...] = two
    w_out[...] = weight
    avg_out[...] = moving
    low_out[...] = weight.astype(bf16)


def adam_update(gradient, first_moment, second_moment, weight, moving, rate, decay):
    first_new = BETA_ONE * first_moment + (1.0 - BETA_ONE) * gradient
    second_new = BETA_TWO * second_moment + (1.0 - BETA_TWO) * gradient * gradient
    corr_one = 1.0 - BETA_ONE**STEP
    corr_two = 1.0 - BETA_TWO**STEP
    step_dir = first_new / corr_one / (jnp.sqrt(second_new / corr_two) + ADAM_EPS)
    weight_new = weight - rate * (step_dir + decay * weight)
    moving_new = EMA_DECAY * moving + (1.0 - EMA_DECAY) * weight_new
    return (first_new, second_new, weight_new, moving_new)


def call(kernel, grid, in_specs, out_specs, out_shape, args, scratch=(), prefetch=0, flops=0, moved=0, vmem=58):
    return pl.pallas_call(
        kernel,
        grid_spec=pltpu.PrefetchScalarGridSpec(
            num_scalar_prefetch=prefetch, grid=grid, in_specs=in_specs, out_specs=out_specs, scratch_shapes=scratch
        ),
        out_shape=out_shape,
        compiler_params=pltpu.CompilerParams(dimension_semantics=("arbitrary",) * len(grid), vmem_limit_bytes=vmem * MIB),
        cost_estimate=pl.CostEstimate(flops=flops, bytes_accessed=moved, transcendentals=0),
    )(*args)


def whole(shape):
    return pl.BlockSpec(shape, lambda *_: (0,) * len(shape))


def pair(rows, first=0):
    return pl.BlockSpec((rows, LANES), lambda j, *_: (0, first + j))


def pairs(count, rows, at=0):
    return pl.BlockSpec((count, rows, LANES), lambda j, *_: (at, 0, j))


def shape_of(shape, dtype):
    return jax.ShapeDtypeStruct(shape, dtype)


def shifted(x, by):
    count = lax.axis_size("img")
    return lax.ppermute(x, "img", [(i + by, i) for i in range(count) if 0 <= i + by < count])


def crossed(x, bit):
    count = lax.axis_size("img")
    return lax.ppermute(x, "img", [(i, i ^ bit) for i in range(count)])


def other_txt(x):
    return lax.ppermute(x, "txt", [(0, 1), (1, 0)])


def index_bits(count):
    bits = count.bit_length() - 1
    assert count == 1 << bits
    return bits


def sum_over_img(x):
    for bit in range(index_bits(lax.axis_size("img"))):
        x = x + crossed(x, 1 << bit)
    return x


def sum_over_all(x):
    bits = index_bits(lax.axis_size("img"))
    for bit in range(0, bits - 1, 2):
        low, high = 1 << bit, 2 << bit
        x = (x + crossed(x, low)) + (crossed(x, high) + crossed(x, low | high))
    if bits % 2:
        x = x + crossed(x, 1 << (bits - 1))
    return x + other_txt(x)


def own_and_other(x, bit, below=1):
    mine = (lax.axis_index("img") >> bit) & 1
    split = x.reshape(x.shape[0] // (2 * below), 2, below, *x.shape[1:])
    own = lax.dynamic_index_in_dim(split, mine, 1, keepdims=False)
    other = lax.dynamic_index_in_dim(split, 1 - mine, 1, keepdims=False)
    return own.reshape(-1, *x.shape[1:]), other.reshape(-1, *x.shape[1:])


class TermSum:
    def __init__(self, clock, terms, order, sent_as):
        count = lax.axis_size("img")
        self.sent_as = sent_as
        self.clock, self.order, self.level = clock, order, 0
        self.keep = clock.stage(terms).reshape(count, terms.shape[0] // count, terms.shape[1])
        self.send()

    def send(self):
        bit = self.order[self.level]
        below = 1 << sum(other < bit for other in self.order[self.level :])
        self.keep, sent = own_and_other(self.keep, bit, below)
        self.sent = sent.astype(self.sent_as)
        self.clock.mark(self.sent)

    def receive(self):
        self.got = self.clock.stage(crossed(self.sent, 1 << self.order[self.level]))
        self.clock.mark(self.got)

    def advance(self, received=False):
        if not received:
            self.receive()
        self.keep = self.keep + self.clock.stage(self.got).astype(f32)
        self.level += 1
        if self.level == len(self.order):
            self.clock.mark(self.keep)
            return self.keep[0]
        self.send()

    def finish(self):
        while True:
            result = self.advance()
            if result is not None:
                return result


def gather_doubling(x):
    x = x[None]
    for bit in reversed(range(index_bits(lax.axis_size("img")))):
        x = doubled(x, bit)
    return x.reshape(-1, x.shape[-1])


def doubled(x, bit):
    mine = (lax.axis_index("img") >> bit) & 1
    got = crossed(x, 1 << bit)
    both = jnp.where(mine == 0, jnp.stack([x, got], 1), jnp.stack([got, x], 1))
    return both.reshape(-1, *x.shape[1:])


def tie(x, *others):
    return lax.optimization_barrier((x, others))[0]


def tall(left):
    count = lax.axis_size("img")
    return left.T.reshape(count, left.shape[1] // count, left.shape[0])


class Clock:
    def __init__(self):
        self.token = ()
        self.kept = []

    def stage(self, *arrays):
        arrays, passed = lax.optimization_barrier((arrays, self.token))
        self.kept += passed
        return arrays if len(arrays) > 1 else arrays[0]

    def mark(self, *arrays):
        self.token = arrays


class SmallSum:
    def __init__(self, clock, x, row):
        self.x, self.row = clock.stage(x, row)
        self.clock, self.level = clock, 0
        self.levels = index_bits(lax.axis_size("img"))
        self.send()

    def send(self):
        high = lax.reduce_precision(self.row, 8, 7)
        low = lax.reduce_precision(self.row - high, 8, 7)
        self.row = high + low
        self.sent = jnp.concatenate([self.x, high, low], axis=0).astype(bf16)
        self.clock.mark(self.sent)

    def advance(self):
        got = self.clock.stage(crossed(self.sent, 1 << self.level)).astype(f32)
        count = self.x.shape[0]
        self.x = self.x + got[:count]
        self.row = self.row + (got[count : count + 1] + got[count + 1 :])
        self.level += 1
        if self.level < self.levels:
            self.send()
        else:
            self.clock.mark(self.x)


class SmallGather:
    def __init__(self, clock, x):
        x = clock.stage(x)
        self.clock, self.x, self.bit = clock, x[None], index_bits(lax.axis_size("img"))
        clock.mark(x)

    def advance(self):
        self.bit -= 1
        mine = (lax.axis_index("img") >> self.bit) & 1
        got = self.clock.stage(crossed(self.x, 1 << self.bit))
        both = jnp.where(mine == 0, jnp.stack([self.x, got], 1), jnp.stack([got, self.x], 1))
        self.x = both.reshape(-1, *got.shape[1:])
        self.clock.mark(self.x)

    def result(self):
        return self.x.reshape(-1, self.x.shape[-1])


class GradientSum:
    def __init__(self, clock, left, right):
        bits = index_bits(left.shape[0])
        self.order = list(range(bits))
        self.level = 0
        self.clock = clock
        left, self.right = clock.stage(left, right)
        self.own, other = own_and_other(left, 0)
        self.sent = self.terms(other).astype(bf16)
        self.result = None
        clock.mark(self.sent)

    def terms(self, chunks):
        product = mm(chunks.reshape(-1, chunks.shape[2]), self.right, 1, 0)
        return product.reshape(chunks.shape[0], chunks.shape[1], self.right.shape[1])

    def receive(self):
        self.got = self.clock.stage(crossed(self.sent, 1 << self.order[self.level]))
        self.clock.mark(self.got)
        self.level += 1

    def advance(self, received=False, beside=None):
        if beside is not None:
            self.got, *beside = self.clock.stage(crossed(self.sent, 1 << self.order[self.level]), *beside)
            self.clock.mark(self.got)
            self.level += 1
        elif not received:
            self.receive()
        got = self.clock.stage(self.got)
        if self.level == len(self.order):
            self.result = (self.keep + got.astype(f32))[0]
            return self.result
        bit = self.order[self.level]
        if self.level == 1:
            own, other = own_and_other(self.own, bit)
            got_own, got_other = own_and_other(got, bit)
            self.sent = (self.terms(other) + got_other.astype(f32)).astype(bf16)
            self.keep = self.terms(own) + got_own.astype(f32)
        else:
            own, other = own_and_other(self.keep + got.astype(f32), bit)
            self.sent, self.keep = other.astype(bf16), own
        self.clock.mark(self.sent)
        return beside


class Neighbourhood:
    def __init__(self, clock, x, end, beginning):
        count = lax.axis_size("img")
        self.clock = clock
        self.x = x
        self.across = crossed(x, 2)
        self.above, self.below = shifted(x, 4), shifted(x, -4)
        edge = jnp.where(lax.axis_index("img") % 4 == 3, end, beginning)
        pairs_low = [(i - 5, i) for i in range(0, count, 4) if i >= 5]
        pairs_high = [(i + 5, i) for i in range(3, count, 4) if i + 5 < count]
        self.edge = lax.ppermute(edge, "img", pairs_low + pairs_high)

    def second(self):
        across, above, below, self.edge = self.clock.stage(self.across, self.above, self.below, self.edge)
        self.across, self.above, self.below = across, above, below
        self.four_sent = jnp.concatenate([self.x, across, above, below], axis=0)
        self.above_across, self.below_across = shifted(across, 4), shifted(across, -4)
        self.clock.mark(self.four_sent)

    def third(self):
        four = crossed(self.four_sent, 1)
        self.above_across, self.below_across, self.four = self.clock.stage(self.above_across, self.below_across, four)
        self.two_sent = jnp.concatenate([self.above_across, self.below_across], axis=0)
        self.clock.mark(self.two_sent)

    def collect(self):
        two = self.clock.stage(crossed(self.two_sent, 1))
        self.clock.mark(two)
        return [self.x, self.across, self.above, self.below, self.four, self.above_across, self.below_across, two, self.edge]


PIECE_COUNTS = (1, 1, 1, 1, 4, 1, 1, 2, 1)


def neighbour_indices(i):
    b = i ^ 1
    edge = jnp.where(i % 4 == 0, i - 5, i + 5)
    return [i, i ^ 2, i + 4, i - 4, b, b ^ 2, b + 4, b - 4, (i ^ 2) + 4, (i ^ 2) - 4, (b ^ 2) + 4, (b ^ 2) - 4, edge]


def token_places(row_index, image_sides):
    heights = image_sides[:, 0]
    widths = image_sides[:, 1]
    lengths = heights * (widths + 1)
    sample_ends = jnp.cumsum(lengths, dtype=jnp.int32)
    starts = sample_ends - lengths
    sample_ids = ids_of(row_index, sample_ends)
    matched = jnp.arange(image_sides.shape[0], dtype=jnp.int32)[None, :] == sample_ids[:, None]
    first_row = jnp.sum(jnp.where(matched, starts[None, :], 0), axis=1, dtype=jnp.int32)
    row_width = jnp.sum(jnp.where(matched, widths[None, :] + 1, 0), axis=1, dtype=jnp.int32)
    row_width = jnp.maximum(row_width, 1)
    offset = row_index - first_row
    return (sample_ids, offset // row_width, offset % row_width, sample_ends)


def ids_of(rows, sample_ends):
    return jnp.sum((sample_ends <= rows[..., None]).astype(jnp.int32), axis=-1, dtype=jnp.int32)


def turn_tables(row_pos, col_pos):
    quarter = HD // 4
    frequency = 10000.0 ** (-jnp.arange(quarter, dtype=f32) / quarter)
    angles = jnp.concatenate(
        [row_pos.astype(f32)[:, None] * frequency[None, :], col_pos.astype(f32)[:, None] * frequency[None, :]], axis=1
    )
    cosine, sine = jnp.cos(angles), jnp.sin(angles)
    return jnp.concatenate([cosine] * 4, axis=1), jnp.concatenate([-sine, sine, -sine, sine], axis=1)


def rms_norm(values):
    return values * lax.rsqrt(jnp.mean(values * values, axis=-1, keepdims=True) + EPS_NORM)


def rms_back(values, d_normed):
    inverse = lax.rsqrt(jnp.mean(values * values, axis=-1, keepdims=True) + EPS_NORM)
    normed = values * inverse
    return inverse * (d_normed - normed * jnp.mean(d_normed * normed, axis=-1, keepdims=True))


def on_device(
    tokens, cotangent, text_states, conditions, image_sides, master, moment_one, moment_two, average,
    small_master, small_one, small_two, small_average,
):
    n_img = lax.axis_size("img")
    n_txt = lax.axis_size("txt")
    img_index = lax.axis_index("img")
    txt_index = lax.axis_index("txt")
    tok = tokens.shape[0]
    samples = image_sides.shape[0]
    half_d = D // n_txt
    half_ff = FF // n_txt
    local_heads = half_d // HD
    n_pairs = half_d // LANES

    tables = [
        (D // n_img, 2 * half_ff),
        (half_ff // n_img, D),
        (D // n_img, 3 * half_d),
        (TXT_D // n_img, 2 * half_d),
        (half_d // n_img, D),
        (COND // n_img, 6 * half_d),
    ]
    master_lines = master.reshape(-1, LANES)
    lines = master_lines.shape[0]
    starts = [0]
    for rows, columns in tables:
        starts.append(starts[-1] + rows * columns // LANES)

    def scatter(terms):
        return lax.psum_scatter(terms, "img", scatter_dimension=0, tiled=True)

    def gather(rows):
        return lax.all_gather(rows, "img", axis=0, tiled=True)

    together = [0, 1, 4, 2]
    shapes = [tables[w] for w in together]
    heights = [rows * columns // WIDE for rows, columns in shapes]
    in_blocks = all(rows % 16 == 0 for rows, _ in shapes)
    packed = together if in_blocks else []
    apart = [5, 3] if in_blocks else [5, 3] + together
    own = pl.pallas_call(
        functools.partial(own_rows_kernel, tables, starts, packed, apart),
        out_shape=[shape_of((sum(heights), WIDE), bf16)] * in_blocks + [shape_of(tables[w], bf16) for w in apart],
        compiler_params=pltpu.CompilerParams(vmem_limit_bytes=58 * MIB),
    )(master_lines)
    own_modulate, own_text = own[in_blocks : in_blocks + 2]
    if in_blocks:
        blocks = gather(own[0][None])
    else:
        blocks = None
        natural = dict(zip(together, (gather(rows) for rows in own[2:])))

    def weight(which):
        if blocks is None:
            array = natural[which]
            return array, lambda at, group=1: pl.BlockSpec((array.shape[0], group * WIDE), lambda j, *_: (0, at(j)))
        place = together.index(which)
        rows = shapes[place][0]
        first = sum(heights[:place]) // rows
        assert first * rows == sum(heights[:place])

        def spec(at, group=1):
            assert first % group == 0
            return pl.BlockSpec((n_img, group * rows, WIDE), lambda j, *_: (0, first // group + at(j), 0))

        return blocks, spec


    gain_attn = small_master[:D]
    gain_ffn = small_master[D : 2 * D]
    gain_query = small_master[2 * D : 2 * D + HD]
    gain_key = small_master[2 * D + HD : 2 * D + 2 * HD]
    gain_text = small_master[2 * D + 2 * HD : 2 * D + 3 * HD]
    gate_heads = small_master[2 * D + 3 * HD :]
    gate_local = lax.dynamic_slice_in_dim(gate_heads, txt_index * local_heads, local_heads)
    tanh_gate = jnp.tanh(gate_local)
    gate_lanes = jnp.repeat(tanh_gate, HD)[None, :]
    gain_query_pair = jnp.tile(gain_query, 2)[None, :]
    gain_key_pair = jnp.tile(gain_key, 2)[None, :]

    cond_rows = COND // n_img
    cond_own = lax.dynamic_slice_in_dim(conditions, img_index * cond_rows, cond_rows, 1)
    silu_own = jax.nn.silu(cond_own.astype(f32)).astype(bf16)
    mod_sum = sum_over_img(jnp.dot(silu_own, own_modulate, preferred_element_type=f32))
    mod_half = mod_sum.astype(bf16)
    mod_other = other_txt(mod_half)
    mods = jnp.where(
        txt_index == 0, jnp.stack([mod_half, mod_other], 0), jnp.stack([mod_other, mod_half], 0)
    ).reshape(n_txt, samples, 6, half_d).transpose(1, 2, 0, 3)

    row_index = img_index * tok + jnp.arange(tok, dtype=jnp.int32)
    sample_ids, row_pos, col_pos, sample_ends = token_places(row_index, image_sides)
    cosine, sine = turn_tables(row_pos, col_pos)
    one_hot = sample_ids[:, None] == jnp.arange(samples, dtype=jnp.int32)[None, :]
    per_token = jnp.dot(one_hot.astype(bf16), mods.reshape(samples, 6 * D), preferred_element_type=f32).astype(bf16)
    shift_one, scale_one, gate_one, shift_two, scale_two, gate_two = (
        per_token[:, c * D : (c + 1) * D].astype(f32) for c in range(6)
    )

    pieces = jnp.stack([jnp.asarray(p, jnp.int32) for p in neighbour_indices(img_index)])
    place = img_index % 4
    inside = (pieces >= 0) & (pieces < n_img)
    slots = jnp.arange(PIECES)
    inside &= (slots != PIECES - 1) | (place == 0) | (place == 3)
    column = jnp.arange(tok, dtype=jnp.int32)[None, :]
    edge_start = jnp.where((slots == PIECES - 1) & (place == 0), tok - EDGE, 0)
    piece_rows = pieces[:, None] * tok + column + edge_start[:, None]
    there = inside[:, None] & ((slots[:, None] < PIECES - 1) | (column < EDGE))
    piece_ids = jnp.where(there, ids_of(piece_rows, sample_ends), -1)
    flags = jnp.any((piece_ids >= sample_ids[0]) & (piece_ids <= sample_ids[-1]), axis=1).astype(jnp.int32)
    piece_ids = jnp.concatenate([piece_ids, jnp.full((16 - PIECES, tok), -1, jnp.int32)], axis=0)
    own_ids = sample_ids[:, None]

    text_rows = text_states.shape[0]
    text_len = text_rows * n_img
    text_columns = lax.all_to_all(text_states, "img", split_axis=1, concat_axis=0, tiled=True)
    z_first = [0] + list(range(2, index_bits(n_img))) + [1]
    text_proj = TermSum(Clock(), jnp.dot(text_columns, own_text, preferred_element_type=f32), z_first, bf16).finish()
    text_shape = (text_rows, local_heads, HD)
    text_raw = text_proj[:, :half_d].reshape(text_shape)
    text_normed = rms_norm(text_raw)
    text_key_low = (text_normed * gain_text).reshape(text_rows, half_d).astype(bf16)
    text_low = jnp.concatenate([text_key_low, text_proj[:, half_d:].astype(bf16)], axis=1)
    all_text = gather_doubling(text_low)

    if blocks is not None:
        blocks = tie(blocks, all_text, per_token, cosine, sine, flags, piece_ids)
    x_float = tokens.astype(f32)
    x_normed = rms_norm(x_float)
    normed_one = x_normed * gain_attn
    attn_in = (normed_one * (1.0 + scale_one) + shift_one).astype(bf16)
    def wide(rows, group=1):
        return pl.BlockSpec((rows, group * WIDE), lambda j, *_: (0, j))

    thirds = half_d // WIDE
    w_project, project_spec = weight(2)
    own_qkv, raw_qk = call(
        project_kernel,
        (thirds,),
        [whole((tok, D))]
        + [project_spec(lambda j, c=c: c * thirds + j) for c in range(3)]
        + [whole((1, LANES))] * 2
        + [whole((tok, LANES))] * 2,
        [pl.BlockSpec((n, tok, WIDE), lambda j: (0, 0, j)) for n in (3, 2)],
        [shape_of((3, tok, half_d), bf16), shape_of((2, tok, half_d), f32)],
        (attn_in, w_project, w_project, w_project, gain_query_pair, gain_key_pair, cosine, sine),
        flops=2 * tok * D * 3 * half_d,
        moved=2 * D * 3 * half_d,
    )
    clock = Clock()
    clock.mark(own_qkv)
    qkv_near = Neighbourhood(clock, own_qkv, own_qkv[:, tok - EDGE :], own_qkv[:, :EDGE])
    w_updown, updown_spec = weight(0)
    w_down, down_spec = weight(1)
    w_output, output_spec = weight(4)
    def step(j):
        return j

    qkv_near.second()
    qkv_near.third()
    qkv_pieces = qkv_near.collect()

    qkv_specs = [pairs(3 * c, a.shape[1]) for c, a in zip(PIECE_COUNTS, qkv_pieces)]
    id_specs = [whole((tok, 1)), whole((16, tok))]
    text_specs = [pair(text_len), pair(text_len, n_pairs)]
    mixed_low, self_out, cross_out, lse_self, lse_cross, lse_split = call(
        functools.partial(attend_kernel, PIECE_COUNTS, tok),
        (n_pairs,),
        [pairs(1, tok)] + id_specs + text_specs + [pair(1)] + qkv_specs,
        [pair(tok)] * 5 + [whole((TABLE, 3 * tok))],
        [shape_of((tok, half_d), bf16)]
        + [shape_of((tok, half_d), f32)] * 4
        + [shape_of((TABLE, 3 * tok), bf16)],
        (flags, clock.stage(own_qkv), own_ids, piece_ids, all_text, all_text, gate_lanes, *qkv_pieces),
        scratch=[
            pltpu.VMEM((PIECES, 2 * tok, tok), f32),
            pltpu.VMEM((2 * tok, LANES), f32),
            pltpu.VMEM((2 * tok, LANES), f32),
            pltpu.VMEM((2 * tok, LANES), f32),
            pltpu.VMEM((TABLE, tok), f32),
        ],
        prefetch=1,
    )

    def pack_edges(pack):
        table = pack[:, tok:]
        ending = jnp.concatenate(
            [table[:, :, part * tok + tok - EDGE : (part + 1) * tok] for part in range(3) for _ in range(tok // EDGE)],
            axis=2,
        )
        return (
            jnp.concatenate([pack[:, tok - EDGE : tok], ending], axis=1),
            jnp.concatenate([pack[:, :EDGE], table], axis=1),
        )

    clock.mark(mixed_low)
    attn_part = call(
        times_kernel,
        (D // WIDE,),
        [whole((tok, half_d)), output_spec(step)],
        [wide(tok)],
        [shape_of((tok, D), bf16)],
        (clock.stage(mixed_low), w_output),
        flops=2 * tok * half_d * D,
        moved=2 * half_d * D,
    )[0]
    clock.mark(attn_part)
    attn_other = clock.stage(other_txt(attn_part))
    attn_out = attn_part.astype(f32) + attn_other.astype(f32)
    hidden = x_float + gate_one * attn_out
    h_normed = rms_norm(hidden)
    normed_two = h_normed * gain_ffn
    ffn_in = (normed_two * (1.0 + scale_two) + shift_two).astype(bf16)
    clock.mark(ffn_in)
    gate, up, hidden_units, hidden_turned = call(
        hidden_kernel,
        (half_ff // WIDE,),
        [whole((tok, D)), updown_spec(step), updown_spec(lambda j: half_ff // WIDE + j)],
        [wide(tok)] * 3 + [pl.BlockSpec((WIDE, tok), lambda j: (j, 0))],
        [shape_of((tok, half_ff), f32)] * 2 + [shape_of((tok, half_ff), bf16), shape_of((half_ff, tok), bf16)],
        (clock.stage(ffn_in), w_updown, w_updown),
        flops=4 * tok * D * half_ff,
        moved=4 * D * half_ff,
    )
    clock.mark(hidden_turned)
    d_out = cotangent.astype(f32)
    d_branch = (d_out * gate_two).astype(bf16)
    down_terms = mm(clock.stage(hidden_turned), d_branch, 1, 0).astype(bf16)
    clock.mark(down_terms)
    grad_down = scatter(down_terms)
    d_gate_up = call(
        hidden_back_kernel,
        (D // WIDE // 3,),
        [wide(tok, 3), down_spec(step, 3), whole((tok, half_ff)), whole((tok, half_ff))],
        [whole((tok, 2 * half_ff))],
        [shape_of((tok, 2 * half_ff), bf16)],
        (clock.stage(d_branch), w_down, gate, up),
        scratch=[pltpu.VMEM((tok, half_ff), f32)],
        flops=2 * tok * D * half_ff,
        moved=2 * D * half_ff,
    )[0]
    clock.mark(d_gate_up)
    d_gate_up = clock.stage(d_gate_up)
    d_ffn_part = call(
        times_transposed_kernel,
        (2 * half_ff // WIDE // 4,),
        [wide(tok, 4), updown_spec(step, 4)],
        [whole((tok, D))],
        [shape_of((tok, D), bf16)],
        (d_gate_up, w_updown),
        scratch=[pltpu.VMEM((tok, D), f32)],
        flops=4 * tok * D * half_ff,
        moved=4 * D * half_ff,
    )[0]
    clock.mark(d_ffn_part)
    d_ffn_other = other_txt(d_ffn_part)
    updown_terms = mm(clock.stage(ffn_in), d_gate_up, 0, 0).astype(bf16)
    clock.mark(updown_terms)
    grad_updown = scatter(updown_terms)
    d_ffn_part, d_ffn_other = clock.stage(d_ffn_part, d_ffn_other)
    d_ffn_in = d_ffn_part.astype(f32) + d_ffn_other.astype(f32)
    d_scale_two = d_ffn_in * normed_two
    d_normed_two = d_ffn_in * (1.0 + scale_two)
    d_gain_ffn = jnp.sum(d_normed_two * h_normed, axis=0)
    d_hidden = d_out + rms_back(hidden, d_normed_two * gain_ffn)
    d_attn = (d_hidden * gate_one).astype(bf16)
    clock.mark(d_attn)
    grad_pack, d_cross_low, d_gate_lanes = call(
        functools.partial(mixed_back_kernel, tok),
        (D // WIDE // 3,),
        [wide(tok, 3), output_spec(step, 3), whole((tok, half_d)), whole((tok, half_d)), whole((1, half_d)), whole((TABLE, 3 * tok))],
        [whole((1, tok + PACK, half_d)), whole((tok, half_d)), whole((1, half_d))],
        [
            shape_of((1, tok + PACK, half_d), bf16),
            shape_of((tok, half_d), bf16),
            shape_of((1, half_d), f32),
        ],
        (clock.stage(d_attn), w_output, self_out, cross_out, gate_lanes, lse_split),
        scratch=[pltpu.VMEM((tok, half_d), f32)],
        flops=2 * tok * D * half_d,
        moved=2 * D * half_d,
    )
    clock.mark(grad_pack)
    grad_near = Neighbourhood(clock, grad_pack, *pack_edges(grad_pack))
    branch_part = call(
        times_kernel,
        (D // WIDE,),
        [whole((tok, half_ff)), down_spec(step)],
        [wide(tok)],
        [shape_of((tok, D), f32)],
        (clock.stage(hidden_units), w_down),
        flops=2 * tok * D * half_ff,
        moved=2 * D * half_ff,
    )[0]
    clock.mark(branch_part)
    branch_other = other_txt(branch_part)
    grad_near.second()
    turn_specs = [whole((1, LANES)), whole((tok, LANES)), whole((tok, LANES))]

    def query_back(first, count, d_cross):
        def at(rows, also=0):
            return pair(rows, first + also)

        def some(arrays, rows, index=0):
            return pl.BlockSpec((arrays, rows, LANES), lambda j, *_: (index, 0, first + j))

        return call(
            functools.partial(query_back_kernel, PIECE_COUNTS, tok),
            (count,),
            [some(1, tok)]
            + id_specs
            + [at(text_len), at(text_len, n_pairs)]
            + [some(1, tok), at(tok)]
            + [at(tok)] * 4
            + [some(1, tok)]
            + turn_specs
            + [some(3 * c, a.shape[1]) for c, a in zip(PIECE_COUNTS, qkv_pieces)],
            [pair(tok), pair(1), pair(text_len), pair(text_len)],
            [
                shape_of((tok, count * LANES), bf16),
                shape_of((1, count * LANES), f32),
                shape_of((text_len, count * LANES), f32),
                shape_of((text_len, count * LANES), f32),
            ],
            (
                flags, own_qkv, own_ids, piece_ids, all_text, all_text, grad_pack, d_cross,
                self_out, cross_out, lse_self, lse_cross, raw_qk, gain_query_pair, cosine, sine, *qkv_pieces,
            ),
            scratch=[pltpu.VMEM((2 * tok, LANES), f32)],
            prefetch=1,
        )

    head_half = n_pairs // 2
    first_half = query_back(0, head_half, clock.stage(d_cross_low))
    clock.mark(first_half[0])
    grad_near.third()
    output_sum = GradientSum(clock, tall(mixed_low), d_attn)
    grad_pieces = grad_near.collect()
    output_sum.advance()
    second_half = query_back(head_half, n_pairs - head_half, clock.stage(d_cross_low))
    clock.mark(second_half[0])
    grad_down, branch_other = clock.stage(grad_down, branch_other)
    clock.mark(grad_down, branch_other)
    d_query_raw, d_gain_query, d_text_key, d_text_value = (
        jnp.concatenate(halves, axis=1) for halves in zip(first_half, second_half)
    )
    attn_tall = tall(attn_in)
    text_sum = TermSum(clock, jnp.concatenate([d_text_key, d_text_value], axis=1), z_first, bf16)
    query_sum = GradientSum(clock, attn_tall, d_query_raw)
    text_sum.advance()
    query_sum.advance()

    pack_specs = [pairs(c, a.shape[1] - PACK) for c, a in zip(PIECE_COUNTS, grad_pieces)] + [
        pl.BlockSpec((c, PACK, half_d), lambda j, *_, at=(a.shape[1] - PACK) // PACK: (0, at, 0))
        for c, a in zip(PIECE_COUNTS, grad_pieces)
    ]

    d_key_value, d_gain_key = call(
        functools.partial(key_back_kernel, PIECE_COUNTS, tok),
        (n_pairs,),
        [pairs(1, tok, 1), pairs(1, tok, 2)]
        + id_specs
        + [pairs(1, tok, 1)]
        + turn_specs
        + qkv_specs
        + pack_specs,
        [whole((tok, 2 * half_d)), pair(1)],
        [shape_of((tok, 2 * half_d), bf16), shape_of((1, half_d), f32)],
        (
            flags, clock.stage(own_qkv), own_qkv, own_ids, piece_ids, raw_qk, gain_key_pair,
            cosine, sine, *qkv_pieces, *grad_pieces, *grad_pieces,
        ),
        scratch=[pltpu.VMEM((2 * tok, LANES), f32)] * 2,
        prefetch=1,
    )
    clock.mark(d_key_value)
    key_value_sum = GradientSum(clock, attn_tall, d_key_value)
    d_key_value = clock.stage(d_key_value)
    d_attn_part = call(
        input_back_kernel,
        (3,),
        [whole((tok, half_d)), whole((tok, 2 * half_d)), project_spec(step, thirds)],
        [whole((tok, D))],
        [shape_of((tok, D), bf16)],
        (d_query_raw, d_key_value, w_project),
        scratch=[pltpu.VMEM((tok, D), f32)],
        flops=6 * tok * D * half_d,
        moved=6 * D * half_d,
    )[0]
    clock.mark(d_attn_part)
    d_attn_other = other_txt(d_attn_part)
    key_value_sum.advance()
    text_sum.advance()
    output_sum.advance()

    one_hot_wide = one_hot.astype(f32)

    def by_sample(values):
        summed = lax.dot_general(one_hot_wide, values, (((0,), (0,)), ((), ())), precision=HIGH)
        return lax.dynamic_slice_in_dim(summed, txt_index * half_d, half_d, 1)

    d_hidden_late, d_ffn_late = clock.stage(d_hidden, d_ffn_in)
    branch = branch_part + branch_other
    block_out = hidden + gate_two * branch
    d_mod_early = jnp.concatenate(
        [
            by_sample(v)
            for v in (d_hidden_late * attn_out, d_ffn_late, d_ffn_late * normed_two, d_out * branch)
        ],
        axis=1,
    )
    clock.mark(d_mod_early)
    text_own = text_sum.finish()
    d_text_scaled = text_own[:, :half_d].reshape(text_shape)
    d_gain_text = jnp.sum(d_text_scaled * text_normed, axis=(0, 1))
    d_text_raw = rms_back(text_raw, d_text_scaled * gain_text).reshape(text_rows, half_d)
    text_gather = SmallGather(clock, jnp.concatenate([d_text_raw, text_own[:, half_d:]], axis=1).astype(bf16))
    query_sum.advance()
    d_attn_other = clock.stage(d_attn_other)
    d_attn_in = d_attn_part.astype(f32) + d_attn_other.astype(f32)
    d_scale_one = d_attn_in * normed_one
    d_normed_one = d_attn_in * (1.0 + scale_one)
    d_gain_attn = jnp.sum(d_normed_one * x_normed, axis=0)
    d_tokens = d_hidden + rms_back(x_float, d_normed_one * gain_attn)
    d_mod = jnp.concatenate([by_sample(d_attn_in), by_sample(d_scale_one), d_mod_early], axis=1)

    replica = (txt_index == 0).astype(f32)
    d_gate_local = jnp.sum(d_gate_lanes.reshape(local_heads, HD), axis=1) * (1.0 - tanh_gate**2)
    gate_full = lax.dynamic_update_slice(jnp.zeros((HEADS,), f32), d_gate_local, (txt_index * local_heads,))
    small_terms = jnp.concatenate(
        [
            d_gain_attn * replica,
            d_gain_ffn * replica,
            jnp.sum(d_gain_query.reshape(local_heads, HD), axis=0),
            jnp.sum(d_gain_key.reshape(local_heads, HD), axis=0),
            jnp.zeros((HD,), f32),
            gate_full,
        ]
    )
    small_count = small_terms.shape[0]
    small_row = jnp.pad(small_terms, (0, d_mod.shape[1] - small_count))[None]
    small_sum = SmallSum(clock, d_mod, small_row)
    text_gather.advance()
    (grad_updown,) = key_value_sum.advance(beside=(grad_updown,))
    small_sum.advance()
    small_sum.advance()
    key_value_sum.advance()
    small_sum.advance()
    text_gather.advance()
    output_sum.advance()
    query_sum.advance()
    text_gather.advance()
    small_sum.advance()
    key_value_sum.advance()
    output_sum.advance()
    query_sum.advance()
    while text_gather.bit:
        text_gather.advance()
    grad_text = mm(text_columns, text_gather.result(), 0, 0)
    pending = [one for one in (output_sum, query_sum, key_value_sum) if one.result is None]
    while pending or small_sum.level < small_sum.levels:
        if small_sum.level < small_sum.levels:
            small_sum.advance()
        for one in list(pending):
            if one.result is None:
                one.advance()
            if one.result is not None:
                pending.remove(one)
    d_mod, small_row = small_sum.x, small_sum.row
    small_grad = (small_row + other_txt(small_row))[0, :small_count]
    grad_modulate = lax.dot_general(silu_own.astype(f32), d_mod, (((0,), (0,)), ((), ())), precision=HIGH)

    grads = [grad_updown, grad_down, query_sum.result, grad_text, output_sum.result, grad_modulate, key_value_sum.result]
    places = [(start, 0, columns) for start, (_, columns) in zip(starts, tables)]
    places.append((starts[2], half_d, 3 * half_d))
    reduced, squares = pl.pallas_call(
        functools.partial(flatten_kernel, places),
        out_shape=[shape_of((lines, LANES), f32), shape_of((1, LANES), f32)],
        in_specs=[pl.BlockSpec(memory_space=pltpu.VMEM)] * len(grads)
        + [pl.BlockSpec(memory_space=pl.ANY)] * len(clock.kept),
        compiler_params=pltpu.CompilerParams(vmem_limit_bytes=58 * MIB),
    )(*grads, *clock.kept)

    last = sum_over_all(jnp.concatenate([squares, jnp.pad(d_gain_text, (0, LANES - HD))[None]], axis=0))
    small_grad = lax.dynamic_update_slice(small_grad, last[1, :HD], (2 * D + 2 * HD,))
    grad_square = jnp.sum(last[0]) + jnp.sum(small_grad * small_grad)
    clip_factor = MAX_NORM / jnp.maximum(jnp.sqrt(grad_square), MAX_NORM)

    block = math.gcd(lines, 2048)
    line_spec = pl.BlockSpec((block, LANES), lambda i: (i, 0))
    as_lines = (lines, LANES)
    updated = call(
        update_kernel,
        (lines // block,),
        [pl.BlockSpec(memory_space=pltpu.SMEM)] + [line_spec] * 5,
        [line_spec] * 5,
        [shape_of(as_lines, f32)] * 4 + [shape_of(as_lines, bf16)],
        (clip_factor.reshape(1), reduced, *(a.reshape(as_lines) for a in (moment_one, moment_two, master, average))),
        flops=20 * lines * LANES,
        moved=38 * lines * LANES,
    )
    one_new, two_new, master_new, average_new, master_low = (a.reshape(master.shape) for a in updated)
    small_one_new, small_two_new, small_new, small_average_new = adam_update(
        small_grad * clip_factor, small_one, small_two, small_master, small_average, RATE_SMALL, 0.0
    )
    return (
        block_out,
        d_tokens,
        grad_square,
        one_new,
        two_new,
        master_new,
        average_new,
        master_low,
        small_one_new,
        small_two_new,
        small_new,
        small_average_new,
    )


def solution(mesh):
    rows = P("img", None)
    shards = P("img", "txt", None)
    in_specs = (rows, rows, rows, P(), P(), shards, shards, shards, shards, P(), P(), P(), P())
    out_specs = (rows, rows, P(), shards, shards, shards, shards, shards, P(), P(), P(), P())
    return jax.shard_map(on_device, mesh=mesh, in_specs=in_specs, out_specs=out_specs, check_vma=False)
```

```python
import functools
import math

import jax
import jax.numpy as jnp
from jax import lax
from jax.experimental import pallas as pl
from jax.experimental.pallas import tpu as pltpu
from jax.sharding import PartitionSpec as P

D = 1536
HEADS = 24
HD = 64
FF = 4096
TXT_D = 4096
COND = 1024
SIDE_MAX = 32
STEP = 10

HIGH = lax.Precision.HIGHEST
EPS_NORM = 1e-06
MAX_NORM = 1.0
BETA_ONE = 0.5
BETA_TWO = 0.5
RATE_MATRIX = 0.01
RATE_SMALL = 0.1
DECAY_WEIGHT = 0.01
ADAM_EPS = 1e-08
EMA_DECAY = 0.8

LANES = 128
EDGE = 128
TABLE = 16
PACK = 2 * TABLE
WIDE = 256
PIECES = 13
MASKED = -1e30
MIB = 1024 * 1024

bf16 = jnp.bfloat16
f32 = jnp.float32


def mm(a, b, on_a, on_b):
    return lax.dot_general(a, b, (((on_a,), (on_b,)), ((), ())), preferred_element_type=f32)


def lane_index(rows):
    return lax.broadcasted_iota(jnp.int32, (rows, LANES), 1)


def head_sum(values):
    low = lane_index(values.shape[0]) < HD
    first = jnp.sum(jnp.where(low, values, 0.0), axis=1, keepdims=True)
    second = jnp.sum(jnp.where(low, 0.0, values), axis=1, keepdims=True)
    return jnp.where(low, first, second)


def swap_halves(values):
    first = lane_index(values.shape[0]) % HD < HD // 2
    return jnp.where(
        first, pltpu.roll(values, LANES - HD // 2, 1), pltpu.roll(values, HD // 2, 1)
    )


def two_heads(pair):
    low = lane_index(pair.shape[0]) < HD
    zero = jnp.zeros_like(pair)
    return jnp.concatenate([jnp.where(low, pair, zero), jnp.where(low, zero, pair)], axis=0)


def one_pair(stacked):
    rows = stacked.shape[0] // 2
    low = lane_index(rows) < HD
    return jnp.where(low, stacked[:rows], stacked[rows:])


def columns_of(spread):
    return jnp.concatenate([spread[:, :1], spread[:, HD : HD + 1]], axis=0)


def norm_rope(raw, gain, cosine, sine):
    inverse = lax.rsqrt(head_sum(raw * raw) * (1.0 / HD) + EPS_NORM)
    scaled = raw * inverse * gain
    return scaled * cosine + swap_halves(scaled) * sine


def norm_rope_back(raw, gain, cosine, sine, d_out):
    inverse = lax.rsqrt(head_sum(raw * raw) * (1.0 / HD) + EPS_NORM)
    normed = raw * inverse
    d_scaled = d_out * cosine - swap_halves(d_out) * sine
    d_gain = jnp.sum(d_scaled * normed, axis=0, keepdims=True)
    d_normed = d_scaled * gain
    d_raw = inverse * (d_normed - normed * (head_sum(d_normed * normed) * (1.0 / HD)))
    return d_raw, d_gain


def split_three(values):
    high = values.astype(bf16)
    rest = values - high.astype(f32)
    middle = rest.astype(bf16)
    last = (rest - middle.astype(f32)).astype(bf16)
    return jnp.concatenate([high, middle, last], axis=1)


def joined(packed, rows):
    wide = packed.astype(f32)
    return wide[:, :rows] + wide[:, rows : 2 * rows] + wide[:, 2 * rows : 3 * rows]


def put_row(table, index, row):
    at = lax.broadcasted_iota(jnp.int32, table.shape, 0) == index
    return jnp.where(at, row, table)


def take_row(table, index):
    at = lax.broadcasted_iota(jnp.int32, table.shape, 0) == index
    return jnp.sum(jnp.where(at, table, 0.0), axis=0, keepdims=True)


def as_row(column):
    return jnp.broadcast_to(column, (column.shape[0], LANES)).T[:1]


def tile(ref):
    return ref[...].reshape(-1, WIDE)


def tiles(ref, count):
    if len(ref.shape) == 2:
        return [ref[:, at * WIDE : (at + 1) * WIDE] for at in range(count)]
    rows = ref.shape[1] // count
    return [ref[:, at * rows : (at + 1) * rows, :].reshape(-1, WIDE) for at in range(count)]


def add_transposed(acc_ref, a_ref, w_ref):
    count = a_ref.shape[1] // WIDE
    blocks = tiles(w_ref, count)
    for row in range(0, acc_ref.shape[1], WIDE):
        part = slice(row, row + WIDE)
        total = mm(a_ref[:, :WIDE], blocks[0][part], 1, 1)
        for at in range(1, count):
            total = total + mm(a_ref[:, at * WIDE : (at + 1) * WIDE], blocks[at][part], 1, 1)
        acc_ref[:, part] += total


def project_kernel(a_ref, wq_ref, wk_ref, wv_ref, gq_ref, gk_ref, cos_ref, sin_ref, qkv_ref, raw_ref):
    a = a_ref[...]
    cosine, sine = cos_ref[...], sin_ref[...]
    raw_q = mm(a, tile(wq_ref), 1, 0)
    raw_k = mm(a, tile(wk_ref), 1, 0)
    raw_ref[0] = raw_q
    raw_ref[1] = raw_k
    for at in range(0, WIDE, LANES):
        part = slice(at, at + LANES)
        query = norm_rope(raw_q[:, part], gq_ref[...], cosine, sine).astype(bf16)
        qkv_ref[0, :, part] = query * jnp.asarray(HD**-0.5, bf16)
        qkv_ref[1, :, part] = norm_rope(raw_k[:, part], gk_ref[...], cosine, sine).astype(bf16)
    qkv_ref[2] = mm(a, tile(wv_ref), 1, 0).astype(bf16)


def times_kernel(a_ref, w_ref, out_ref):
    out_ref[...] = mm(a_ref[...], tile(w_ref), 1, 0).astype(out_ref.dtype)


def times_transposed_kernel(a_ref, w_ref, out_ref, acc_ref):
    step = pl.program_id(0)

    @pl.when(step == 0)
    def _():
        acc_ref[...] = jnp.zeros(acc_ref.shape, f32)

    add_transposed(acc_ref, a_ref, w_ref)

    @pl.when(step == pl.num_programs(0) - 1)
    def _():
        out_ref[...] = acc_ref[...].astype(out_ref.dtype)


def input_back_kernel(d_query_ref, d_key_value_ref, w_ref, out_ref, acc_ref):
    step = pl.program_id(0)
    half = d_query_ref.shape[1]

    @pl.when(step == 0)
    def _():
        acc_ref[...] = jnp.zeros(acc_ref.shape, f32)
        add_transposed(acc_ref, d_query_ref, w_ref)

    for at in range(2):

        @pl.when(step == at + 1)
        def _(at=at):
            add_transposed(acc_ref, d_key_value_ref.at[:, at * half : (at + 1) * half], w_ref)

    @pl.when(step == 2)
    def _():
        out_ref[...] = acc_ref[...].astype(out_ref.dtype)


def hidden_kernel(b_ref, w_gate_ref, w_up_ref, gate_ref, up_ref, hidden_ref, turned_ref):
    gate = mm(b_ref[...], tile(w_gate_ref), 1, 0)
    up = mm(b_ref[...], tile(w_up_ref), 1, 0)
    hidden = (gate * jax.nn.sigmoid(gate) * up).astype(bf16)
    gate_ref[...] = gate
    up_ref[...] = up
    hidden_ref[...] = hidden
    turned_ref[...] = hidden.T


def hidden_back_kernel(d_branch_ref, w_ref, gate_ref, up_ref, d_ref, acc_ref):
    step = pl.program_id(0)

    @pl.when(step == 0)
    def _():
        acc_ref[...] = jnp.zeros(acc_ref.shape, f32)

    add_transposed(acc_ref, d_branch_ref, w_ref)

    @pl.when(step == pl.num_programs(0) - 1)
    def _():
        for at in range(0, acc_ref.shape[1], WIDE):
            part = slice(at, at + WIDE)
            d_units, gate = acc_ref[:, part], gate_ref[:, part]
            sigmoid = jax.nn.sigmoid(gate)
            d_gate = d_units * up_ref[:, part] * sigmoid * (1.0 + gate * (1.0 - sigmoid))
            d_ref[:, part] = d_gate.astype(bf16)
            d_ref[:, acc_ref.shape[1] + at : acc_ref.shape[1] + at + WIDE] = (d_units * (gate * sigmoid)).astype(bf16)


def piece_views(piece_refs, counts, per):
    views = []
    for ref, count in zip(piece_refs, counts):
        for at in range(count):
            views.append((ref, at * per))
    return views


def attend_kernel(counts, tok, flag_ref, q_ref, own_ids_ref, ids_ref, tk_ref, tv_ref, gate_ref, *rest):
    pieces = piece_views(rest[: len(counts)], counts, 3)
    mixed_ref, self_ref, cross_ref, lse_self_ref, lse_cross_ref, split_ref = rest[len(counts) : len(counts) + 6]
    scores_ref, most_ref, total_ref, acc_ref, table_ref = rest[len(counts) + 6 :]
    step = pl.program_id(0)
    own_ids = own_ids_ref[...]
    q_two = two_heads(q_ref[0])
    own_two = jnp.concatenate([own_ids, own_ids], axis=0)
    most_ref[...] = jnp.full(most_ref.shape, MASKED, f32)
    total_ref[...] = jnp.zeros(total_ref.shape, f32)
    acc_ref[...] = jnp.zeros(acc_ref.shape, f32)
    for slot, (ref, at) in enumerate(pieces):
        rows = ref.shape[1]

        @pl.when(flag_ref[slot] > 0)
        def _(slot=slot, ref=ref, at=at, rows=rows):
            scores = mm(q_two, ref[at + 1], 1, 1)
            scores = jnp.where(own_two == ids_ref[slot : slot + 1, :rows], scores, MASKED)
            scores_ref[slot, :, :rows] = scores
            most = most_ref[...]
            for part in range(rows // LANES):
                most = jnp.maximum(most, scores[:, part * LANES : (part + 1) * LANES])
            most_ref[...] = most

    row_most = jnp.max(most_ref[...], axis=1, keepdims=True)
    for slot, (ref, at) in enumerate(pieces):
        rows = ref.shape[1]

        @pl.when(flag_ref[slot] > 0)
        def _(slot=slot, ref=ref, at=at, rows=rows):
            weights = jnp.exp(scores_ref[slot, :, :rows] - row_most)
            total = total_ref[...]
            for part in range(rows // LANES):
                total = total + weights[:, part * LANES : (part + 1) * LANES]
            total_ref[...] = total
            acc_ref[...] += mm(weights.astype(bf16), ref[at + 2], 1, 0)

    row_total = jnp.sum(total_ref[...], axis=1, keepdims=True)
    self_out = one_pair(acc_ref[...] / row_total)
    lse_self = row_most + jnp.log(row_total)

    cross_scores = mm(q_two, tk_ref[...], 1, 1)
    cross_most = jnp.max(cross_scores, axis=1, keepdims=True)
    cross_weights = jnp.exp(cross_scores - cross_most)
    cross_total = jnp.sum(cross_weights, axis=1, keepdims=True)
    cross_out = one_pair(mm(cross_weights.astype(bf16), tv_ref[...], 1, 0) / cross_total)
    lse_cross = cross_most + jnp.log(cross_total)

    self_ref[...] = self_out
    cross_ref[...] = cross_out
    mixed_ref[...] = (self_out + gate_ref[...] * cross_out).astype(bf16)
    spread = (tok, LANES)
    low = lane_index(tok) < HD
    lse_self_ref[...] = jnp.where(
        low, jnp.broadcast_to(lse_self[:tok], spread), jnp.broadcast_to(lse_self[tok:], spread)
    )
    lse_cross_ref[...] = jnp.where(
        low, jnp.broadcast_to(lse_cross[:tok], spread), jnp.broadcast_to(lse_cross[tok:], spread)
    )

    @pl.when(step == 0)
    def _():
        table_ref[...] = jnp.zeros(table_ref.shape, f32)

    table = put_row(table_ref[...], 2 * step, as_row(lse_self[:tok]))
    table = put_row(table, 2 * step + 1, as_row(lse_self[tok:]))
    table_ref[...] = table

    @pl.when(step == pl.num_programs(0) - 1)
    def _():
        split_ref[...] = split_three(table_ref[...])


def mixed_back_kernel(tok, d_attn_ref, w_ref, self_ref, cross_ref, gate_ref, lse_ref, pack_ref, d_cross_ref, d_gate_ref, acc_ref):
    step = pl.program_id(0)

    @pl.when(step == 0)
    def _():
        acc_ref[...] = jnp.zeros(acc_ref.shape, f32)

    add_transposed(acc_ref, d_attn_ref, w_ref)

    @pl.when(step == pl.num_programs(0) - 1)
    def _():
        rows = []
        for at in range(0, acc_ref.shape[1], LANES):
            part = slice(at, at + LANES)
            d_mixed = acc_ref[:, part]
            d_self = d_mixed.astype(bf16)
            d_cross_ref[:, part] = (gate_ref[:, part] * d_mixed).astype(bf16)
            d_gate_ref[:, part] = jnp.sum(d_mixed * cross_ref[:, part], axis=0, keepdims=True)
            delta = head_sum(d_self.astype(f32) * self_ref[:, part])
            rows += [as_row(delta[:, :1]), as_row(delta[:, HD : HD + 1])]
            pack_ref[0, :tok, part] = d_self
        rows += [jnp.zeros_like(rows[0])] * (TABLE - len(rows))
        pack_ref[0, tok : tok + TABLE, :] = split_three(jnp.concatenate(rows, axis=0))
        pack_ref[0, tok + TABLE :, :] = lse_ref[...]


def query_back_kernel(
    counts, tok, flag_ref, q_ref, own_ids_ref, ids_ref, tk_ref, tv_ref, d_self_ref, d_cross_ref,
    self_ref, cross_ref, lse_self_ref, lse_cross_ref, raw_ref, gain_ref, cos_ref, sin_ref, *rest
):
    pieces = piece_views(rest[: len(counts)], counts, 3)
    d_raw_ref, d_gain_ref, d_tk_ref, d_tv_ref, acc_ref = rest[len(counts) :]
    own_ids = own_ids_ref[...]
    own_two = jnp.concatenate([own_ids, own_ids], axis=0)
    q_two = two_heads(q_ref[0])
    d_self = d_self_ref[0]
    d_self_two = two_heads(d_self)
    delta = columns_of(head_sum(d_self.astype(f32) * self_ref[...]))
    lse = columns_of(lse_self_ref[...])

    d_cross = d_cross_ref[...]
    d_cross_two = two_heads(d_cross)
    delta_cross = columns_of(head_sum(d_cross.astype(f32) * cross_ref[...]))
    lse_cross = columns_of(lse_cross_ref[...])
    cross_p = jnp.exp(mm(q_two, tk_ref[...], 1, 1) - lse_cross)
    d_cross_p = mm(d_cross_two, tv_ref[...], 1, 1)
    d_cross_s = (cross_p * (d_cross_p - delta_cross)).astype(bf16)
    d_tv_ref[...] = mm(cross_p.astype(bf16), d_cross_two, 0, 0)
    d_tk_ref[...] = mm(d_cross_s, q_two, 0, 0)
    acc_ref[...] = mm(d_cross_s, tk_ref[...], 1, 0)
    for slot, (ref, at) in enumerate(pieces):
        rows = ref.shape[1]

        @pl.when(flag_ref[slot] > 0)
        def _(slot=slot, ref=ref, at=at, rows=rows):
            key = ref[at + 1]
            scores = mm(q_two, key, 1, 1)
            scores = jnp.where(own_two == ids_ref[slot : slot + 1, :rows], scores, MASKED)
            weights = jnp.exp(scores - lse)
            d_weights = mm(d_self_two, ref[at + 2], 1, 1)
            d_scores = (weights * (d_weights - delta)).astype(bf16)
            acc_ref[...] += mm(d_scores, key, 1, 0)

    d_query = one_pair(acc_ref[...]) * (HD**-0.5)
    d_raw, d_gain = norm_rope_back(raw_ref[0], gain_ref[...], cos_ref[...], sin_ref[...], d_query)
    d_raw_ref[...] = d_raw.astype(bf16)
    d_gain_ref[...] = d_gain


def key_back_kernel(counts, tok, flag_ref, k_ref, v_ref, own_ids_ref, ids_ref, raw_ref, gain_ref, cos_ref, sin_ref, *rest):
    n = len(counts)
    q_views = piece_views(rest[:n], counts, 3)
    g_views = piece_views(rest[n : 2 * n], counts, 1)
    g_tables = piece_views(rest[2 * n : 3 * n], counts, 1)
    d_both_ref, d_gain_ref, acc_k_ref, acc_v_ref = rest[3 * n :]
    step = pl.program_id(0)
    own_ids = own_ids_ref[...]
    k_two = two_heads(k_ref[0])
    v_two = two_heads(v_ref[0])
    acc_k_ref[...] = jnp.zeros(acc_k_ref.shape, f32)
    acc_v_ref[...] = jnp.zeros(acc_v_ref.shape, f32)
    for slot in range(PIECES):
        q_ref, q_at = q_views[slot]
        g_ref, at = g_views[slot]
        rows = q_ref.shape[1]
        @pl.when(flag_ref[slot] > 0)
        def _(slot=slot, q_ref=q_ref, q_at=q_at, g_ref=g_ref, at=at, rows=rows):
            query = q_ref[q_at]
            d_self = g_ref[at]
            tables = joined(g_tables[slot][0][at], tok)[:, :rows]
            delta, lse = tables[:TABLE], tables[TABLE:]
            same = own_ids == ids_ref[slot : slot + 1, :rows]
            scores = mm(k_two, query, 1, 1)
            d_weights = mm(v_two, d_self, 1, 1)
            p_low, d_low = [], []
            for head in range(2):
                part = slice(head * tok, (head + 1) * tok)
                masked = jnp.where(same, scores[part], MASKED)
                weights = jnp.exp(masked - take_row(lse, 2 * step + head))
                p_low.append(weights.astype(bf16))
                d_low.append((weights * (d_weights[part] - take_row(delta, 2 * step + head))).astype(bf16))
            acc_v_ref[...] += mm(jnp.concatenate(p_low, axis=0), d_self, 1, 0)
            acc_k_ref[...] += mm(jnp.concatenate(d_low, axis=0), query, 1, 0)

    d_raw, d_gain = norm_rope_back(
        raw_ref[0], gain_ref[...], cos_ref[...], sin_ref[...], one_pair(acc_k_ref[...])
    )
    d_gain_ref[...] = d_gain
    place = pl.multiple_of(step * LANES, LANES)
    d_both_ref[:, pl.ds(place, LANES)] = d_raw.astype(bf16)
    half = pl.num_programs(0) * LANES
    d_both_ref[:, pl.ds(pl.multiple_of(half + place, LANES), LANES)] = one_pair(acc_v_ref[...]).astype(bf16)


def place_rows(lines_ref, start, table, out_ref, top=None):
    rows, columns = table
    per_row = columns // LANES
    for at in range(per_row):
        part = lines_ref[pl.ds(start + at, rows, stride=per_row), :].astype(bf16)
        if top is None:
            out_ref[:, at * LANES : (at + 1) * LANES] = part
        else:
            row, lane = top + at // (WIDE // LANES) * rows, at % (WIDE // LANES) * LANES
            out_ref[row : row + rows, lane : lane + LANES] = part


def own_rows_kernel(tables, starts, packed, apart, lines_ref, *out_refs):
    top = 0
    for which in packed:
        rows, columns = tables[which]
        place_rows(lines_ref, starts[which], tables[which], out_refs[0], top)
        top += columns // WIDE * rows
    for which, ref in zip(apart, out_refs[bool(packed) :]):
        place_rows(lines_ref, starts[which], tables[which], ref)


def flatten_kernel(places, *refs):
    *in_refs, lines_ref = refs
    for (start, column, columns), ref in zip(places, in_refs):
        for at in range(ref.shape[1] // LANES):
            part = ref[:, at * LANES : (at + 1) * LANES].astype(f32)
            lines_ref[pl.ds(start + column // LANES + at, ref.shape[0], stride=columns // LANES), :] = part


def update_kernel(clip_ref, g_ref, one_ref, two_ref, w_ref, avg_ref, one_out, two_out, w_out, avg_out, low_out):
    one, two, weight, moving = adam_update(
        g_ref[...] * clip_ref[0], one_ref[...], two_ref[...], w_ref[...], avg_ref[...], RATE_MATRIX, DECAY_WEIGHT
    )
    one_out[...] = one
    two_out[...] = two
    w_out[...] = weight
    avg_out[...] = moving
    low_out[...] = weight.astype(bf16)


def adam_update(gradient, first_moment, second_moment, weight, moving, rate, decay):
    first_new = BETA_ONE * first_moment + (1.0 - BETA_ONE) * gradient
    second_new = BETA_TWO * second_moment + (1.0 - BETA_TWO) * gradient * gradient
    corr_one = 1.0 - BETA_ONE**STEP
    corr_two = 1.0 - BETA_TWO**STEP
    step_dir = first_new / corr_one / (jnp.sqrt(second_new / corr_two) + ADAM_EPS)
    weight_new = weight - rate * (step_dir + decay * weight)
    moving_new = EMA_DECAY * moving + (1.0 - EMA_DECAY) * weight_new
    return (first_new, second_new, weight_new, moving_new)


def call(kernel, grid, in_specs, out_specs, out_shape, args, scratch=(), prefetch=0, flops=0, moved=0, vmem=58):
    return pl.pallas_call(
        kernel,
        grid_spec=pltpu.PrefetchScalarGridSpec(
            num_scalar_prefetch=prefetch, grid=grid, in_specs=in_specs, out_specs=out_specs, scratch_shapes=scratch
        ),
        out_shape=out_shape,
        compiler_params=pltpu.CompilerParams(dimension_semantics=("arbitrary",) * len(grid), vmem_limit_bytes=vmem * MIB),
        cost_estimate=pl.CostEstimate(flops=flops, bytes_accessed=moved, transcendentals=0),
    )(*args)


def whole(shape):
    return pl.BlockSpec(shape, lambda *_: (0,) * len(shape))


def pair(rows, first=0):
    return pl.BlockSpec((rows, LANES), lambda j, *_: (0, first + j))


def pairs(count, rows, at=0):
    return pl.BlockSpec((count, rows, LANES), lambda j, *_: (at, 0, j))


def shape_of(shape, dtype):
    return jax.ShapeDtypeStruct(shape, dtype)


def shifted(x, by):
    count = lax.axis_size("img")
    return lax.ppermute(x, "img", [(i + by, i) for i in range(count) if 0 <= i + by < count])


def crossed(x, bit):
    count = lax.axis_size("img")
    return lax.ppermute(x, "img", [(i, i ^ bit) for i in range(count)])


def other_txt(x):
    return lax.ppermute(x, "txt", [(0, 1), (1, 0)])


def index_bits(count):
    bits = count.bit_length() - 1
    assert count == 1 << bits
    return bits


def sum_over_img(x):
    for bit in range(index_bits(lax.axis_size("img"))):
        x = x + crossed(x, 1 << bit)
    return x


def few_over_img(x):
    bits = index_bits(lax.axis_size("img"))
    for bit in range(0, bits - 1, 2):
        low, high = 1 << bit, 2 << bit
        x = (x + crossed(x, low)) + (crossed(x, high) + crossed(x, low | high))
    if bits % 2:
        x = x + crossed(x, 1 << (bits - 1))
    return x


def own_and_other(x, bit, below=1):
    mine = (lax.axis_index("img") >> bit) & 1
    split = x.reshape(x.shape[0] // (2 * below), 2, below, *x.shape[1:])
    own = lax.dynamic_index_in_dim(split, mine, 1, keepdims=False)
    other = lax.dynamic_index_in_dim(split, 1 - mine, 1, keepdims=False)
    return own.reshape(-1, *x.shape[1:]), other.reshape(-1, *x.shape[1:])


class TermSum:
    def __init__(self, clock, terms, order, sent_as):
        count = lax.axis_size("img")
        self.sent_as = sent_as
        self.clock, self.order, self.level = clock, order, 0
        self.keep = clock.stage(terms).reshape(count, terms.shape[0] // count, terms.shape[1])
        self.send()

    def send(self):
        bit = self.order[self.level]
        below = 1 << sum(other < bit for other in self.order[self.level :])
        self.keep, sent = own_and_other(self.keep, bit, below)
        self.sent = sent.astype(self.sent_as)
        self.clock.mark(self.sent)

    def receive(self):
        self.got = self.clock.stage(crossed(self.sent, 1 << self.order[self.level]))
        self.clock.mark(self.got)

    def advance(self, received=False):
        if not received:
            self.receive()
        self.keep = self.keep + self.clock.stage(self.got).astype(f32)
        self.level += 1
        if self.level == len(self.order):
            self.clock.mark(self.keep)
            return self.keep[0]
        self.send()

    def finish(self):
        while True:
            result = self.advance()
            if result is not None:
                return result


def gather_doubling(x):
    x = x[None]
    for bit in reversed(range(index_bits(lax.axis_size("img")))):
        x = doubled(x, bit)
    return x.reshape(-1, x.shape[-1])


def doubled(x, bit):
    mine = (lax.axis_index("img") >> bit) & 1
    got = crossed(x, 1 << bit)
    both = jnp.where(mine == 0, jnp.stack([x, got], 1), jnp.stack([got, x], 1))
    return both.reshape(-1, *x.shape[1:])


def tie(x, *others):
    return lax.optimization_barrier((x, others))[0]


def tall(left):
    count = lax.axis_size("img")
    return left.T.reshape(count, left.shape[1] // count, left.shape[0])


class Clock:
    def __init__(self):
        self.token = ()
        self.kept = []

    def stage(self, *arrays):
        arrays, passed = lax.optimization_barrier((arrays, self.token))
        self.kept += passed
        return arrays if len(arrays) > 1 else arrays[0]

    def mark(self, *arrays):
        self.token = arrays


class SmallSum:
    def __init__(self, clock, x, row):
        self.x, self.row = clock.stage(x, row)
        self.clock, self.level = clock, 0
        self.levels = index_bits(lax.axis_size("img"))
        self.send()

    def send(self):
        high = lax.reduce_precision(self.row, 8, 7)
        low = lax.reduce_precision(self.row - high, 8, 7)
        self.row = high + low
        self.sent = jnp.concatenate([self.x, high, low], axis=0).astype(bf16)
        self.clock.mark(self.sent)

    def advance(self):
        got = self.clock.stage(crossed(self.sent, 1 << self.level)).astype(f32)
        count = self.x.shape[0]
        self.x = self.x + got[:count]
        self.row = self.row + (got[count : count + 1] + got[count + 1 :])
        self.level += 1
        if self.level < self.levels:
            self.send()
        else:
            self.clock.mark(self.x)


class SmallGather:
    def __init__(self, clock, x):
        x = clock.stage(x)
        self.clock, self.x, self.bit = clock, x[None], index_bits(lax.axis_size("img"))
        clock.mark(x)

    def advance(self):
        self.bit -= 1
        mine = (lax.axis_index("img") >> self.bit) & 1
        got = self.clock.stage(crossed(self.x, 1 << self.bit))
        both = jnp.where(mine == 0, jnp.stack([self.x, got], 1), jnp.stack([got, self.x], 1))
        self.x = both.reshape(-1, *got.shape[1:])
        self.clock.mark(self.x)

    def result(self):
        return self.x.reshape(-1, self.x.shape[-1])


class GradientSum:
    def __init__(self, clock, left, right):
        bits = index_bits(left.shape[0])
        self.order = list(range(bits))
        self.level = 0
        self.clock = clock
        left, self.right = clock.stage(left, right)
        self.own, other = own_and_other(left, 0)
        self.sent = self.terms(other).astype(bf16)
        self.result = None
        clock.mark(self.sent)

    def terms(self, chunks):
        product = mm(chunks.reshape(-1, chunks.shape[2]), self.right, 1, 0)
        return product.reshape(chunks.shape[0], chunks.shape[1], self.right.shape[1])

    def receive(self):
        self.got = self.clock.stage(crossed(self.sent, 1 << self.order[self.level]))
        self.clock.mark(self.got)
        self.level += 1

    def advance(self, received=False, beside=None):
        if beside is not None:
            self.got, *beside = self.clock.stage(crossed(self.sent, 1 << self.order[self.level]), *beside)
            self.clock.mark(self.got)
            self.level += 1
        elif not received:
            self.receive()
        got = self.clock.stage(self.got)
        if self.level == len(self.order):
            self.result = (self.keep + got.astype(f32))[0]
            return self.result
        bit = self.order[self.level]
        if self.level == 1:
            own, other = own_and_other(self.own, bit)
            got_own, got_other = own_and_other(got, bit)
            self.sent = (self.terms(other) + got_other.astype(f32)).astype(bf16)
            self.keep = self.terms(own) + got_own.astype(f32)
        else:
            own, other = own_and_other(self.keep + got.astype(f32), bit)
            self.sent, self.keep = other.astype(bf16), own
        self.clock.mark(self.sent)
        return beside


class Neighbourhood:
    def __init__(self, clock, x, end, beginning):
        count = lax.axis_size("img")
        self.clock = clock
        self.x = x
        self.across = crossed(x, 2)
        self.above, self.below = shifted(x, 4), shifted(x, -4)
        edge = jnp.where(lax.axis_index("img") % 4 == 3, end, beginning)
        pairs_low = [(i - 5, i) for i in range(0, count, 4) if i >= 5]
        pairs_high = [(i + 5, i) for i in range(3, count, 4) if i + 5 < count]
        self.edge = lax.ppermute(edge, "img", pairs_low + pairs_high)

    def second(self):
        across, above, below, self.edge = self.clock.stage(self.across, self.above, self.below, self.edge)
        self.across, self.above, self.below = across, above, below
        self.four_sent = jnp.concatenate([self.x, across, above, below], axis=0)
        self.above_across, self.below_across = shifted(across, 4), shifted(across, -4)
        self.clock.mark(self.four_sent)

    def third(self):
        four = crossed(self.four_sent, 1)
        self.above_across, self.below_across, self.four = self.clock.stage(self.above_across, self.below_across, four)
        self.two_sent = jnp.concatenate([self.above_across, self.below_across], axis=0)
        self.clock.mark(self.two_sent)

    def collect(self):
        two = self.clock.stage(crossed(self.two_sent, 1))
        self.clock.mark(two)
        return [self.x, self.across, self.above, self.below, self.four, self.above_across, self.below_across, two, self.edge]


PIECE_COUNTS = (1, 1, 1, 1, 4, 1, 1, 2, 1)


def neighbour_indices(i):
    b = i ^ 1
    edge = jnp.where(i % 4 == 0, i - 5, i + 5)
    return [i, i ^ 2, i + 4, i - 4, b, b ^ 2, b + 4, b - 4, (i ^ 2) + 4, (i ^ 2) - 4, (b ^ 2) + 4, (b ^ 2) - 4, edge]


def token_places(row_index, image_sides):
    heights = image_sides[:, 0]
    widths = image_sides[:, 1]
    lengths = heights * (widths + 1)
    sample_ends = jnp.cumsum(lengths, dtype=jnp.int32)
    starts = sample_ends - lengths
    sample_ids = ids_of(row_index, sample_ends)
    matched = jnp.arange(image_sides.shape[0], dtype=jnp.int32)[None, :] == sample_ids[:, None]
    first_row = jnp.sum(jnp.where(matched, starts[None, :], 0), axis=1, dtype=jnp.int32)
    row_width = jnp.sum(jnp.where(matched, widths[None, :] + 1, 0), axis=1, dtype=jnp.int32)
    row_width = jnp.maximum(row_width, 1)
    offset = row_index - first_row
    return (sample_ids, offset // row_width, offset % row_width, sample_ends)


def ids_of(rows, sample_ends):
    return jnp.sum((sample_ends <= rows[..., None]).astype(jnp.int32), axis=-1, dtype=jnp.int32)


def turn_tables(row_pos, col_pos):
    quarter = HD // 4
    frequency = 10000.0 ** (-jnp.arange(quarter, dtype=f32) / quarter)
    angles = jnp.concatenate(
        [row_pos.astype(f32)[:, None] * frequency[None, :], col_pos.astype(f32)[:, None] * frequency[None, :]], axis=1
    )
    cosine, sine = jnp.cos(angles), jnp.sin(angles)
    return jnp.concatenate([cosine] * 4, axis=1), jnp.concatenate([-sine, sine, -sine, sine], axis=1)


def rms_norm(values):
    return values * lax.rsqrt(jnp.mean(values * values, axis=-1, keepdims=True) + EPS_NORM)


def rms_back(values, d_normed):
    inverse = lax.rsqrt(jnp.mean(values * values, axis=-1, keepdims=True) + EPS_NORM)
    normed = values * inverse
    return inverse * (d_normed - normed * jnp.mean(d_normed * normed, axis=-1, keepdims=True))


def on_device(
    tokens, cotangent, text_states, conditions, image_sides, master, moment_one, moment_two, average,
    small_master, small_one, small_two, small_average,
):
    n_img = lax.axis_size("img")
    n_txt = lax.axis_size("txt")
    img_index = lax.axis_index("img")
    txt_index = lax.axis_index("txt")
    tok = tokens.shape[0]
    samples = image_sides.shape[0]
    half_d = D // n_txt
    half_ff = FF // n_txt
    local_heads = half_d // HD
    n_pairs = half_d // LANES

    tables = [
        (D // n_img, 2 * half_ff),
        (half_ff // n_img, D),
        (D // n_img, 3 * half_d),
        (TXT_D // n_img, 2 * half_d),
        (half_d // n_img, D),
        (COND // n_img, 6 * half_d),
    ]
    master_lines = master.reshape(-1, LANES)
    lines = master_lines.shape[0]
    starts = [0]
    for rows, columns in tables:
        starts.append(starts[-1] + rows * columns // LANES)

    def scatter(terms):
        return lax.psum_scatter(terms, "img", scatter_dimension=0, tiled=True)

    def gather(rows):
        return lax.all_gather(rows, "img", axis=0, tiled=True)

    together = [0, 1, 4, 2]
    shapes = [tables[w] for w in together]
    heights = [rows * columns // WIDE for rows, columns in shapes]
    in_blocks = all(rows % 16 == 0 for rows, _ in shapes)
    packed = together if in_blocks else []
    apart = [5, 3] if in_blocks else [5, 3] + together
    own = pl.pallas_call(
        functools.partial(own_rows_kernel, tables, starts, packed, apart),
        out_shape=[shape_of((sum(heights), WIDE), bf16)] * in_blocks + [shape_of(tables[w], bf16) for w in apart],
        compiler_params=pltpu.CompilerParams(vmem_limit_bytes=58 * MIB),
    )(master_lines)
    own_modulate, own_text = own[in_blocks : in_blocks + 2]
    if in_blocks:
        blocks = gather(own[0][None])
    else:
        blocks = None
        natural = dict(zip(together, (gather(rows) for rows in own[2:])))

    def weight(which):
        if blocks is None:
            array = natural[which]
            return array, lambda at, group=1: pl.BlockSpec((array.shape[0], group * WIDE), lambda j, *_: (0, at(j)))
        place = together.index(which)
        rows = shapes[place][0]
        first = sum(heights[:place]) // rows
        assert first * rows == sum(heights[:place])

        def spec(at, group=1):
            assert first % group == 0
            return pl.BlockSpec((n_img, group * rows, WIDE), lambda j, *_: (0, first // group + at(j), 0))

        return blocks, spec


    gain_attn = small_master[:D]
    gain_ffn = small_master[D : 2 * D]
    gain_query = small_master[2 * D : 2 * D + HD]
    gain_key = small_master[2 * D + HD : 2 * D + 2 * HD]
    gain_text = small_master[2 * D + 2 * HD : 2 * D + 3 * HD]
    gate_heads = small_master[2 * D + 3 * HD :]
    gate_local = lax.dynamic_slice_in_dim(gate_heads, txt_index * local_heads, local_heads)
    tanh_gate = jnp.tanh(gate_local)
    gate_lanes = jnp.repeat(tanh_gate, HD)[None, :]
    gain_query_pair = jnp.tile(gain_query, 2)[None, :]
    gain_key_pair = jnp.tile(gain_key, 2)[None, :]

    cond_rows = COND // n_img
    cond_own = lax.dynamic_slice_in_dim(conditions, img_index * cond_rows, cond_rows, 1)
    silu_own = jax.nn.silu(cond_own.astype(f32)).astype(bf16)
    mod_sum = sum_over_img(jnp.dot(silu_own, own_modulate, preferred_element_type=f32))
    mod_half = mod_sum.astype(bf16)
    mod_other = other_txt(mod_half)
    mods = jnp.where(
        txt_index == 0, jnp.stack([mod_half, mod_other], 0), jnp.stack([mod_other, mod_half], 0)
    ).reshape(n_txt, samples, 6, half_d).transpose(1, 2, 0, 3)

    row_index = img_index * tok + jnp.arange(tok, dtype=jnp.int32)
    sample_ids, row_pos, col_pos, sample_ends = token_places(row_index, image_sides)
    cosine, sine = turn_tables(row_pos, col_pos)
    one_hot = sample_ids[:, None] == jnp.arange(samples, dtype=jnp.int32)[None, :]
    per_token = jnp.dot(one_hot.astype(bf16), mods.reshape(samples, 6 * D), preferred_element_type=f32).astype(bf16)
    shift_one, scale_one, gate_one, shift_two, scale_two, gate_two = (
        per_token[:, c * D : (c + 1) * D].astype(f32) for c in range(6)
    )

    pieces = jnp.stack([jnp.asarray(p, jnp.int32) for p in neighbour_indices(img_index)])
    place = img_index % 4
    inside = (pieces >= 0) & (pieces < n_img)
    slots = jnp.arange(PIECES)
    inside &= (slots != PIECES - 1) | (place == 0) | (place == 3)
    column = jnp.arange(tok, dtype=jnp.int32)[None, :]
    edge_start = jnp.where((slots == PIECES - 1) & (place == 0), tok - EDGE, 0)
    piece_rows = pieces[:, None] * tok + column + edge_start[:, None]
    there = inside[:, None] & ((slots[:, None] < PIECES - 1) | (column < EDGE))
    piece_ids = jnp.where(there, ids_of(piece_rows, sample_ends), -1)
    flags = jnp.any((piece_ids >= sample_ids[0]) & (piece_ids <= sample_ids[-1]), axis=1).astype(jnp.int32)
    piece_ids = jnp.concatenate([piece_ids, jnp.full((16 - PIECES, tok), -1, jnp.int32)], axis=0)
    own_ids = sample_ids[:, None]

    text_rows = text_states.shape[0]
    text_len = text_rows * n_img
    text_columns = lax.all_to_all(text_states, "img", split_axis=1, concat_axis=0, tiled=True)
    z_first = [0] + list(range(2, index_bits(n_img))) + [1]
    text_proj = TermSum(Clock(), jnp.dot(text_columns, own_text, preferred_element_type=f32), z_first, bf16).finish()
    text_shape = (text_rows, local_heads, HD)
    text_raw = text_proj[:, :half_d].reshape(text_shape)
    text_normed = rms_norm(text_raw)
    text_key_low = (text_normed * gain_text).reshape(text_rows, half_d).astype(bf16)
    text_low = jnp.concatenate([text_key_low, text_proj[:, half_d:].astype(bf16)], axis=1)
    all_text = gather_doubling(text_low)

    if blocks is not None:
        blocks = tie(blocks, all_text, per_token, cosine, sine, flags, piece_ids)
    x_float = tokens.astype(f32)
    x_normed = rms_norm(x_float)
    normed_one = x_normed * gain_attn
    attn_in = (normed_one * (1.0 + scale_one) + shift_one).astype(bf16)
    def wide(rows, group=1):
        return pl.BlockSpec((rows, group * WIDE), lambda j, *_: (0, j))

    thirds = half_d // WIDE
    w_project, project_spec = weight(2)
    own_qkv, raw_qk = call(
        project_kernel,
        (thirds,),
        [whole((tok, D))]
        + [project_spec(lambda j, c=c: c * thirds + j) for c in range(3)]
        + [whole((1, LANES))] * 2
        + [whole((tok, LANES))] * 2,
        [pl.BlockSpec((n, tok, WIDE), lambda j: (0, 0, j)) for n in (3, 2)],
        [shape_of((3, tok, half_d), bf16), shape_of((2, tok, half_d), f32)],
        (attn_in, w_project, w_project, w_project, gain_query_pair, gain_key_pair, cosine, sine),
        flops=2 * tok * D * 3 * half_d,
        moved=2 * D * 3 * half_d,
    )
    clock = Clock()
    clock.mark(own_qkv)
    qkv_near = Neighbourhood(clock, own_qkv, own_qkv[:, tok - EDGE :], own_qkv[:, :EDGE])
    w_updown, updown_spec = weight(0)
    w_down, down_spec = weight(1)
    w_output, output_spec = weight(4)
    def step(j):
        return j

    qkv_near.second()
    qkv_near.third()
    qkv_pieces = qkv_near.collect()

    qkv_specs = [pairs(3 * c, a.shape[1]) for c, a in zip(PIECE_COUNTS, qkv_pieces)]
    id_specs = [whole((tok, 1)), whole((16, tok))]
    text_specs = [pair(text_len), pair(text_len, n_pairs)]
    mixed_low, self_out, cross_out, lse_self, lse_cross, lse_split = call(
        functools.partial(attend_kernel, PIECE_COUNTS, tok),
        (n_pairs,),
        [pairs(1, tok)] + id_specs + text_specs + [pair(1)] + qkv_specs,
        [pair(tok)] * 5 + [whole((TABLE, 3 * tok))],
        [shape_of((tok, half_d), bf16)]
        + [shape_of((tok, half_d), f32)] * 4
        + [shape_of((TABLE, 3 * tok), bf16)],
        (flags, clock.stage(own_qkv), own_ids, piece_ids, all_text, all_text, gate_lanes, *qkv_pieces),
        scratch=[
            pltpu.VMEM((PIECES, 2 * tok, tok), f32),
            pltpu.VMEM((2 * tok, LANES), f32),
            pltpu.VMEM((2 * tok, LANES), f32),
            pltpu.VMEM((2 * tok, LANES), f32),
            pltpu.VMEM((TABLE, tok), f32),
        ],
        prefetch=1,
    )

    def pack_edges(pack):
        table = pack[:, tok:]
        ending = jnp.concatenate(
            [table[:, :, part * tok + tok - EDGE : (part + 1) * tok] for part in range(3) for _ in range(tok // EDGE)],
            axis=2,
        )
        return (
            jnp.concatenate([pack[:, tok - EDGE : tok], ending], axis=1),
            jnp.concatenate([pack[:, :EDGE], table], axis=1),
        )

    clock.mark(mixed_low)
    attn_part = call(
        times_kernel,
        (D // WIDE,),
        [whole((tok, half_d)), output_spec(step)],
        [wide(tok)],
        [shape_of((tok, D), bf16)],
        (clock.stage(mixed_low), w_output),
        flops=2 * tok * half_d * D,
        moved=2 * half_d * D,
    )[0]
    clock.mark(attn_part)
    attn_other = clock.stage(other_txt(attn_part))
    attn_out = attn_part.astype(f32) + attn_other.astype(f32)
    hidden = x_float + gate_one * attn_out
    h_normed = rms_norm(hidden)
    normed_two = h_normed * gain_ffn
    ffn_in = (normed_two * (1.0 + scale_two) + shift_two).astype(bf16)
    clock.mark(ffn_in)
    gate, up, hidden_units, hidden_turned = call(
        hidden_kernel,
        (half_ff // WIDE,),
        [whole((tok, D)), updown_spec(step), updown_spec(lambda j: half_ff // WIDE + j)],
        [wide(tok)] * 3 + [pl.BlockSpec((WIDE, tok), lambda j: (j, 0))],
        [shape_of((tok, half_ff), f32)] * 2 + [shape_of((tok, half_ff), bf16), shape_of((half_ff, tok), bf16)],
        (clock.stage(ffn_in), w_updown, w_updown),
        flops=4 * tok * D * half_ff,
        moved=4 * D * half_ff,
    )
    clock.mark(hidden_turned)
    d_out = cotangent.astype(f32)
    d_branch = (d_out * gate_two).astype(bf16)
    down_terms = mm(clock.stage(hidden_turned), d_branch, 1, 0).astype(bf16)
    clock.mark(down_terms)
    grad_down = scatter(down_terms)
    d_gate_up = call(
        hidden_back_kernel,
        (D // WIDE // 3,),
        [wide(tok, 3), down_spec(step, 3), whole((tok, half_ff)), whole((tok, half_ff))],
        [whole((tok, 2 * half_ff))],
        [shape_of((tok, 2 * half_ff), bf16)],
        (clock.stage(d_branch), w_down, gate, up),
        scratch=[pltpu.VMEM((tok, half_ff), f32)],
        flops=2 * tok * D * half_ff,
        moved=2 * D * half_ff,
    )[0]
    clock.mark(d_gate_up)
    d_gate_up = clock.stage(d_gate_up)
    d_ffn_part = call(
        times_transposed_kernel,
        (2 * half_ff // WIDE // 4,),
        [wide(tok, 4), updown_spec(step, 4)],
        [whole((tok, D))],
        [shape_of((tok, D), bf16)],
        (d_gate_up, w_updown),
        scratch=[pltpu.VMEM((tok, D), f32)],
        flops=4 * tok * D * half_ff,
        moved=4 * D * half_ff,
    )[0]
    clock.mark(d_ffn_part)
    d_ffn_other = other_txt(d_ffn_part)
    updown_terms = mm(clock.stage(ffn_in), d_gate_up, 0, 0).astype(bf16)
    clock.mark(updown_terms)
    grad_updown = scatter(updown_terms)
    d_ffn_part, d_ffn_other = clock.stage(d_ffn_part, d_ffn_other)
    d_ffn_in = d_ffn_part.astype(f32) + d_ffn_other.astype(f32)
    d_scale_two = d_ffn_in * normed_two
    d_normed_two = d_ffn_in * (1.0 + scale_two)
    d_gain_ffn = jnp.sum(d_normed_two * h_normed, axis=0)
    d_hidden = d_out + rms_back(hidden, d_normed_two * gain_ffn)
    d_attn = (d_hidden * gate_one).astype(bf16)
    clock.mark(d_attn)
    grad_pack, d_cross_low, d_gate_lanes = call(
        functools.partial(mixed_back_kernel, tok),
        (D // WIDE // 3,),
        [wide(tok, 3), output_spec(step, 3), whole((tok, half_d)), whole((tok, half_d)), whole((1, half_d)), whole((TABLE, 3 * tok))],
        [whole((1, tok + PACK, half_d)), whole((tok, half_d)), whole((1, half_d))],
        [
            shape_of((1, tok + PACK, half_d), bf16),
            shape_of((tok, half_d), bf16),
            shape_of((1, half_d), f32),
        ],
        (clock.stage(d_attn), w_output, self_out, cross_out, gate_lanes, lse_split),
        scratch=[pltpu.VMEM((tok, half_d), f32)],
        flops=2 * tok * D * half_d,
        moved=2 * D * half_d,
    )
    clock.mark(grad_pack)
    grad_near = Neighbourhood(clock, grad_pack, *pack_edges(grad_pack))
    branch_part = call(
        times_kernel,
        (D // WIDE,),
        [whole((tok, half_ff)), down_spec(step)],
        [wide(tok)],
        [shape_of((tok, D), f32)],
        (clock.stage(hidden_units), w_down),
        flops=2 * tok * D * half_ff,
        moved=2 * D * half_ff,
    )[0]
    clock.mark(branch_part)
    branch_other = other_txt(branch_part)
    grad_near.second()
    turn_specs = [whole((1, LANES)), whole((tok, LANES)), whole((tok, LANES))]

    def query_back(first, count, d_cross):
        def at(rows, also=0):
            return pair(rows, first + also)

        def some(arrays, rows, index=0):
            return pl.BlockSpec((arrays, rows, LANES), lambda j, *_: (index, 0, first + j))

        return call(
            functools.partial(query_back_kernel, PIECE_COUNTS, tok),
            (count,),
            [some(1, tok)]
            + id_specs
            + [at(text_len), at(text_len, n_pairs)]
            + [some(1, tok), at(tok)]
            + [at(tok)] * 4
            + [some(1, tok)]
            + turn_specs
            + [some(3 * c, a.shape[1]) for c, a in zip(PIECE_COUNTS, qkv_pieces)],
            [pair(tok), pair(1), pair(text_len), pair(text_len)],
            [
                shape_of((tok, count * LANES), bf16),
                shape_of((1, count * LANES), f32),
                shape_of((text_len, count * LANES), f32),
                shape_of((text_len, count * LANES), f32),
            ],
            (
                flags, own_qkv, own_ids, piece_ids, all_text, all_text, grad_pack, d_cross,
                self_out, cross_out, lse_self, lse_cross, raw_qk, gain_query_pair, cosine, sine, *qkv_pieces,
            ),
            scratch=[pltpu.VMEM((2 * tok, LANES), f32)],
            prefetch=1,
        )

    head_half = n_pairs // 2
    first_half = query_back(0, head_half, clock.stage(d_cross_low))
    clock.mark(first_half[0])
    grad_near.third()
    output_sum = GradientSum(clock, tall(mixed_low), d_attn)
    grad_pieces = grad_near.collect()
    output_sum.advance()
    second_half = query_back(head_half, n_pairs - head_half, clock.stage(d_cross_low))
    clock.mark(second_half[0])
    grad_down, branch_other = clock.stage(grad_down, branch_other)
    clock.mark(grad_down, branch_other)
    d_query_raw, d_gain_query, d_text_key, d_text_value = (
        jnp.concatenate(halves, axis=1) for halves in zip(first_half, second_half)
    )
    attn_tall = tall(attn_in)
    text_sum = TermSum(clock, jnp.concatenate([d_text_key, d_text_value], axis=1), z_first, bf16)
    query_sum = GradientSum(clock, attn_tall, d_query_raw)
    text_sum.advance()
    query_sum.advance()

    pack_specs = [pairs(c, a.shape[1] - PACK) for c, a in zip(PIECE_COUNTS, grad_pieces)] + [
        pl.BlockSpec((c, PACK, half_d), lambda j, *_, at=(a.shape[1] - PACK) // PACK: (0, at, 0))
        for c, a in zip(PIECE_COUNTS, grad_pieces)
    ]

    d_key_value, d_gain_key = call(
        functools.partial(key_back_kernel, PIECE_COUNTS, tok),
        (n_pairs,),
        [pairs(1, tok, 1), pairs(1, tok, 2)]
        + id_specs
        + [pairs(1, tok, 1)]
        + turn_specs
        + qkv_specs
        + pack_specs,
        [whole((tok, 2 * half_d)), pair(1)],
        [shape_of((tok, 2 * half_d), bf16), shape_of((1, half_d), f32)],
        (
            flags, clock.stage(own_qkv), own_qkv, own_ids, piece_ids, raw_qk, gain_key_pair,
            cosine, sine, *qkv_pieces, *grad_pieces, *grad_pieces,
        ),
        scratch=[pltpu.VMEM((2 * tok, LANES), f32)] * 2,
        prefetch=1,
    )
    clock.mark(d_key_value)
    key_value_sum = GradientSum(clock, attn_tall, d_key_value)
    d_key_value = clock.stage(d_key_value)
    d_attn_part = call(
        input_back_kernel,
        (3,),
        [whole((tok, half_d)), whole((tok, 2 * half_d)), project_spec(step, thirds)],
        [whole((tok, D))],
        [shape_of((tok, D), bf16)],
        (d_query_raw, d_key_value, w_project),
        scratch=[pltpu.VMEM((tok, D), f32)],
        flops=6 * tok * D * half_d,
        moved=6 * D * half_d,
    )[0]
    clock.mark(d_attn_part)
    d_attn_other = other_txt(d_attn_part)
    key_value_sum.advance()
    text_sum.advance()
    output_sum.advance()

    one_hot_wide = one_hot.astype(f32)

    def by_sample(values):
        summed = lax.dot_general(one_hot_wide, values, (((0,), (0,)), ((), ())), precision=HIGH)
        return lax.dynamic_slice_in_dim(summed, txt_index * half_d, half_d, 1)

    d_hidden_late, d_ffn_late = clock.stage(d_hidden, d_ffn_in)
    branch = branch_part + branch_other
    block_out = hidden + gate_two * branch
    d_mod_early = jnp.concatenate(
        [
            by_sample(v)
            for v in (d_hidden_late * attn_out, d_ffn_late, d_ffn_late * normed_two, d_out * branch)
        ],
        axis=1,
    )
    clock.mark(d_mod_early)
    text_own = text_sum.finish()
    d_text_scaled = text_own[:, :half_d].reshape(text_shape)
    d_gain_text = jnp.sum(d_text_scaled * text_normed, axis=(0, 1))
    d_text_raw = rms_back(text_raw, d_text_scaled * gain_text).reshape(text_rows, half_d)
    text_gather = SmallGather(clock, jnp.concatenate([d_text_raw, text_own[:, half_d:]], axis=1).astype(bf16))
    d_attn_other = clock.stage(d_attn_other)
    d_attn_in = d_attn_part.astype(f32) + d_attn_other.astype(f32)
    d_scale_one = d_attn_in * normed_one
    d_normed_one = d_attn_in * (1.0 + scale_one)
    d_gain_attn = jnp.sum(d_normed_one * x_normed, axis=0)
    d_tokens = d_hidden + rms_back(x_float, d_normed_one * gain_attn)
    d_mod = jnp.concatenate([by_sample(d_attn_in), by_sample(d_scale_one), d_mod_early], axis=1)

    replica = (txt_index == 0).astype(f32)
    d_gate_local = jnp.sum(d_gate_lanes.reshape(local_heads, HD), axis=1) * (1.0 - tanh_gate**2)
    gate_full = lax.dynamic_update_slice(jnp.zeros((HEADS,), f32), d_gate_local, (txt_index * local_heads,))
    small_terms = jnp.concatenate(
        [
            d_gain_attn * replica,
            d_gain_ffn * replica,
            jnp.sum(d_gain_query.reshape(local_heads, HD), axis=0),
            jnp.sum(d_gain_key.reshape(local_heads, HD), axis=0),
            jnp.zeros((HD,), f32),
            gate_full,
        ]
    )
    small_count = small_terms.shape[0]
    small_row = jnp.pad(small_terms, (0, d_mod.shape[1] - small_count))[None]
    small_sum = SmallSum(clock, d_mod, small_row)
    output_sum.advance()
    query_sum.advance()
    text_gather.advance()
    (grad_updown,) = key_value_sum.advance(beside=(grad_updown,))
    small_sum.advance()
    small_sum.advance()
    query_sum.advance()
    key_value_sum.advance()
    small_sum.advance()
    text_gather.advance()
    output_sum.advance()
    text_gather.advance()
    query_sum.advance()
    small_sum.advance()
    key_value_sum.advance()
    while text_gather.bit:
        text_gather.advance()
    grad_text = mm(text_columns, text_gather.result(), 0, 0)
    pending = [one for one in (output_sum, query_sum, key_value_sum) if one.result is None]
    while pending or small_sum.level < small_sum.levels:
        if small_sum.level < small_sum.levels:
            small_sum.advance()
        for one in list(pending):
            if one.result is None:
                one.advance()
            if one.result is not None:
                pending.remove(one)
    d_mod, small_row = small_sum.x, small_sum.row
    small_grad = (small_row + other_txt(small_row))[0, :small_count]
    grad_modulate = lax.dot_general(silu_own.astype(f32), d_mod, (((0,), (0,)), ((), ())), precision=HIGH)

    grads = [grad_updown, grad_down, query_sum.result, grad_text, output_sum.result, grad_modulate, key_value_sum.result]
    places = [(start, 0, columns) for start, (_, columns) in zip(starts, tables)]
    places.append((starts[2], half_d, 3 * half_d))
    square = sum(jnp.sum(jnp.square(g.astype(f32))) for g in grads)
    squares = jnp.pad(square.reshape(1, 1), ((0, 0), (0, LANES - 1)))
    reduced = pl.pallas_call(
        functools.partial(flatten_kernel, places),
        out_shape=shape_of((lines, LANES), f32),
        in_specs=[pl.BlockSpec(memory_space=pltpu.VMEM)] * len(grads)
        + [pl.BlockSpec(memory_space=pl.ANY)] * len(clock.kept),
        compiler_params=pltpu.CompilerParams(vmem_limit_bytes=58 * MIB),
    )(*grads, *clock.kept)

    last = few_over_img(jnp.concatenate([squares, jnp.pad(d_gain_text, (0, LANES - HD))[None]], axis=0))
    last, reduced = lax.optimization_barrier((last, reduced))
    last = last + other_txt(last)
    small_grad = lax.dynamic_update_slice(small_grad, last[1, :HD], (2 * D + 2 * HD,))
    grad_square = jnp.sum(last[0]) + jnp.sum(small_grad * small_grad)
    clip_factor = MAX_NORM / jnp.maximum(jnp.sqrt(grad_square), MAX_NORM)

    block = math.gcd(lines, 2048)
    line_spec = pl.BlockSpec((block, LANES), lambda i: (i, 0))
    as_lines = (lines, LANES)
    updated = call(
        update_kernel,
        (lines // block,),
        [pl.BlockSpec(memory_space=pltpu.SMEM)] + [line_spec] * 5,
        [line_spec] * 5,
        [shape_of(as_lines, f32)] * 4 + [shape_of(as_lines, bf16)],
        (clip_factor.reshape(1), reduced, *(a.reshape(as_lines) for a in (moment_one, moment_two, master, average))),
        flops=20 * lines * LANES,
        moved=38 * lines * LANES,
    )
    one_new, two_new, master_new, average_new, master_low = (a.reshape(master.shape) for a in updated)
    small_one_new, small_two_new, small_new, small_average_new = adam_update(
        small_grad * clip_factor, small_one, small_two, small_master, small_average, RATE_SMALL, 0.0
    )
    return (
        block_out,
        d_tokens,
        grad_square,
        one_new,
        two_new,
        master_new,
        average_new,
        master_low,
        small_one_new,
        small_two_new,
        small_new,
        small_average_new,
    )


def solution(mesh):
    rows = P("img", None)
    shards = P("img", "txt", None)
    in_specs = (rows, rows, rows, P(), P(), shards, shards, shards, shards, P(), P(), P(), P())
    out_specs = (rows, rows, P(), shards, shards, shards, shards, shards, P(), P(), P(), P())
    return jax.shard_map(on_device, mesh=mesh, in_specs=in_specs, out_specs=out_specs, check_vma=False)
```

```python
import functools
import math

import jax
import jax.numpy as jnp
from jax import lax
from jax.experimental import pallas as pl
from jax.experimental.pallas import tpu as pltpu
from jax.sharding import PartitionSpec as P

D = 1536
HEADS = 24
HD = 64
FF = 4096
TXT_D = 4096
COND = 1024
SIDE_MAX = 32
STEP = 10

HIGH = lax.Precision.HIGHEST
EPS_NORM = 1e-06
MAX_NORM = 1.0
BETA_ONE = 0.5
BETA_TWO = 0.5
RATE_MATRIX = 0.01
RATE_SMALL = 0.1
DECAY_WEIGHT = 0.01
ADAM_EPS = 1e-08
EMA_DECAY = 0.8

LANES = 128
EDGE = 128
TABLE = 16
PACK = 2 * TABLE
WIDE = 256
PIECES = 13
MASKED = -1e30
MIB = 1024 * 1024

bf16 = jnp.bfloat16
f32 = jnp.float32


def mm(a, b, on_a, on_b):
    return lax.dot_general(a, b, (((on_a,), (on_b,)), ((), ())), preferred_element_type=f32)


def lane_index(rows):
    return lax.broadcasted_iota(jnp.int32, (rows, LANES), 1)


def head_sum(values):
    low = lane_index(values.shape[0]) < HD
    first = jnp.sum(jnp.where(low, values, 0.0), axis=1, keepdims=True)
    second = jnp.sum(jnp.where(low, 0.0, values), axis=1, keepdims=True)
    return jnp.where(low, first, second)


def swap_halves(values):
    first = lane_index(values.shape[0]) % HD < HD // 2
    return jnp.where(
        first, pltpu.roll(values, LANES - HD // 2, 1), pltpu.roll(values, HD // 2, 1)
    )


def two_heads(pair):
    low = lane_index(pair.shape[0]) < HD
    zero = jnp.zeros_like(pair)
    return jnp.concatenate([jnp.where(low, pair, zero), jnp.where(low, zero, pair)], axis=0)


def one_pair(stacked):
    rows = stacked.shape[0] // 2
    low = lane_index(rows) < HD
    return jnp.where(low, stacked[:rows], stacked[rows:])


def columns_of(spread):
    return jnp.concatenate([spread[:, :1], spread[:, HD : HD + 1]], axis=0)


def norm_rope(raw, gain, cosine, sine):
    inverse = lax.rsqrt(head_sum(raw * raw) * (1.0 / HD) + EPS_NORM)
    scaled = raw * inverse * gain
    return scaled * cosine + swap_halves(scaled) * sine


def norm_rope_back(raw, gain, cosine, sine, d_out):
    inverse = lax.rsqrt(head_sum(raw * raw) * (1.0 / HD) + EPS_NORM)
    normed = raw * inverse
    d_scaled = d_out * cosine - swap_halves(d_out) * sine
    d_gain = jnp.sum(d_scaled * normed, axis=0, keepdims=True)
    d_normed = d_scaled * gain
    d_raw = inverse * (d_normed - normed * (head_sum(d_normed * normed) * (1.0 / HD)))
    return d_raw, d_gain


def split_three(values):
    high = values.astype(bf16)
    rest = values - high.astype(f32)
    middle = rest.astype(bf16)
    last = (rest - middle.astype(f32)).astype(bf16)
    return jnp.concatenate([high, middle, last], axis=1)


def joined(packed, rows):
    wide = packed.astype(f32)
    return wide[:, :rows] + wide[:, rows : 2 * rows] + wide[:, 2 * rows : 3 * rows]


def put_row(table, index, row):
    at = lax.broadcasted_iota(jnp.int32, table.shape, 0) == index
    return jnp.where(at, row, table)


def take_row(table, index):
    at = lax.broadcasted_iota(jnp.int32, table.shape, 0) == index
    return jnp.sum(jnp.where(at, table, 0.0), axis=0, keepdims=True)


def as_row(column):
    return jnp.broadcast_to(column, (column.shape[0], LANES)).T[:1]


def tile(ref):
    return ref[...].reshape(-1, WIDE)


def tiles(ref, count):
    if len(ref.shape) == 2:
        return [ref[:, at * WIDE : (at + 1) * WIDE] for at in range(count)]
    rows = ref.shape[1] // count
    return [ref[:, at * rows : (at + 1) * rows, :].reshape(-1, WIDE) for at in range(count)]


def add_transposed(acc_ref, a_ref, w_ref):
    count = a_ref.shape[1] // WIDE
    blocks = tiles(w_ref, count)
    for row in range(0, acc_ref.shape[1], WIDE):
        part = slice(row, row + WIDE)
        total = mm(a_ref[:, :WIDE], blocks[0][part], 1, 1)
        for at in range(1, count):
            total = total + mm(a_ref[:, at * WIDE : (at + 1) * WIDE], blocks[at][part], 1, 1)
        acc_ref[:, part] += total


def project_kernel(a_ref, wq_ref, wk_ref, wv_ref, gq_ref, gk_ref, cos_ref, sin_ref, qkv_ref, raw_ref):
    a = a_ref[...]
    cosine, sine = cos_ref[...], sin_ref[...]
    raw_q = mm(a, tile(wq_ref), 1, 0)
    raw_k = mm(a, tile(wk_ref), 1, 0)
    raw_ref[0] = raw_q
    raw_ref[1] = raw_k
    for at in range(0, WIDE, LANES):
        part = slice(at, at + LANES)
        query = norm_rope(raw_q[:, part], gq_ref[...], cosine, sine).astype(bf16)
        qkv_ref[0, :, part] = query * jnp.asarray(HD**-0.5, bf16)
        qkv_ref[1, :, part] = norm_rope(raw_k[:, part], gk_ref[...], cosine, sine).astype(bf16)
    qkv_ref[2] = mm(a, tile(wv_ref), 1, 0).astype(bf16)


def times_kernel(a_ref, w_ref, out_ref):
    out_ref[...] = mm(a_ref[...], tile(w_ref), 1, 0).astype(out_ref.dtype)


def times_transposed_kernel(a_ref, w_ref, out_ref, acc_ref):
    step = pl.program_id(0)

    @pl.when(step == 0)
    def _():
        acc_ref[...] = jnp.zeros(acc_ref.shape, f32)

    add_transposed(acc_ref, a_ref, w_ref)

    @pl.when(step == pl.num_programs(0) - 1)
    def _():
        out_ref[...] = acc_ref[...].astype(out_ref.dtype)


def input_back_kernel(d_query_ref, d_key_value_ref, w_ref, out_ref, acc_ref):
    step = pl.program_id(0)
    half = d_query_ref.shape[1]

    @pl.when(step == 0)
    def _():
        acc_ref[...] = jnp.zeros(acc_ref.shape, f32)
        add_transposed(acc_ref, d_query_ref, w_ref)

    for at in range(2):

        @pl.when(step == at + 1)
        def _(at=at):
            add_transposed(acc_ref, d_key_value_ref.at[:, at * half : (at + 1) * half], w_ref)

    @pl.when(step == 2)
    def _():
        out_ref[...] = acc_ref[...].astype(out_ref.dtype)


def hidden_kernel(b_ref, w_gate_ref, w_up_ref, gate_ref, up_ref, hidden_ref, turned_ref):
    gate = mm(b_ref[...], tile(w_gate_ref), 1, 0)
    up = mm(b_ref[...], tile(w_up_ref), 1, 0)
    hidden = (gate * jax.nn.sigmoid(gate) * up).astype(bf16)
    gate_ref[...] = gate
    up_ref[...] = up
    hidden_ref[...] = hidden
    turned_ref[...] = hidden.T


def hidden_back_kernel(d_branch_ref, w_ref, gate_ref, up_ref, d_ref, acc_ref):
    step = pl.program_id(0)

    @pl.when(step == 0)
    def _():
        acc_ref[...] = jnp.zeros(acc_ref.shape, f32)

    add_transposed(acc_ref, d_branch_ref, w_ref)

    @pl.when(step == pl.num_programs(0) - 1)
    def _():
        for at in range(0, acc_ref.shape[1], WIDE):
            part = slice(at, at + WIDE)
            d_units, gate = acc_ref[:, part], gate_ref[:, part]
            sigmoid = jax.nn.sigmoid(gate)
            d_gate = d_units * up_ref[:, part] * sigmoid * (1.0 + gate * (1.0 - sigmoid))
            d_ref[:, part] = d_gate.astype(bf16)
            d_ref[:, acc_ref.shape[1] + at : acc_ref.shape[1] + at + WIDE] = (d_units * (gate * sigmoid)).astype(bf16)


def piece_views(piece_refs, counts, per):
    views = []
    for ref, count in zip(piece_refs, counts):
        for at in range(count):
            views.append((ref, at * per))
    return views


def attend_kernel(counts, tok, flag_ref, q_ref, own_ids_ref, ids_ref, tk_ref, tv_ref, gate_ref, *rest):
    pieces = piece_views(rest[: len(counts)], counts, 3)
    mixed_ref, self_ref, cross_ref, lse_self_ref, lse_cross_ref, split_ref = rest[len(counts) : len(counts) + 6]
    scores_ref, most_ref, total_ref, acc_ref, table_ref = rest[len(counts) + 6 :]
    step = pl.program_id(0)
    own_ids = own_ids_ref[...]
    q_two = two_heads(q_ref[0])
    own_two = jnp.concatenate([own_ids, own_ids], axis=0)
    most_ref[...] = jnp.full(most_ref.shape, MASKED, f32)
    total_ref[...] = jnp.zeros(total_ref.shape, f32)
    acc_ref[...] = jnp.zeros(acc_ref.shape, f32)
    for slot, (ref, at) in enumerate(pieces):
        rows = ref.shape[1]

        @pl.when(flag_ref[slot] > 0)
        def _(slot=slot, ref=ref, at=at, rows=rows):
            scores = mm(q_two, ref[at + 1], 1, 1)
            scores = jnp.where(own_two == ids_ref[slot : slot + 1, :rows], scores, MASKED)
            scores_ref[slot, :, :rows] = scores
            most = most_ref[...]
            for part in range(rows // LANES):
                most = jnp.maximum(most, scores[:, part * LANES : (part + 1) * LANES])
            most_ref[...] = most

    row_most = jnp.max(most_ref[...], axis=1, keepdims=True)
    for slot, (ref, at) in enumerate(pieces):
        rows = ref.shape[1]

        @pl.when(flag_ref[slot] > 0)
        def _(slot=slot, ref=ref, at=at, rows=rows):
            weights = jnp.exp(scores_ref[slot, :, :rows] - row_most)
            total = total_ref[...]
            for part in range(rows // LANES):
                total = total + weights[:, part * LANES : (part + 1) * LANES]
            total_ref[...] = total
            acc_ref[...] += mm(weights.astype(bf16), ref[at + 2], 1, 0)

    row_total = jnp.sum(total_ref[...], axis=1, keepdims=True)
    self_out = one_pair(acc_ref[...] / row_total)
    lse_self = row_most + jnp.log(row_total)

    cross_scores = mm(q_two, tk_ref[...], 1, 1)
    cross_most = jnp.max(cross_scores, axis=1, keepdims=True)
    cross_weights = jnp.exp(cross_scores - cross_most)
    cross_total = jnp.sum(cross_weights, axis=1, keepdims=True)
    cross_out = one_pair(mm(cross_weights.astype(bf16), tv_ref[...], 1, 0) / cross_total)
    lse_cross = cross_most + jnp.log(cross_total)

    self_ref[...] = self_out
    cross_ref[...] = cross_out
    mixed_ref[...] = (self_out + gate_ref[...] * cross_out).astype(bf16)
    spread = (tok, LANES)
    low = lane_index(tok) < HD
    lse_self_ref[...] = jnp.where(
        low, jnp.broadcast_to(lse_self[:tok], spread), jnp.broadcast_to(lse_self[tok:], spread)
    )
    lse_cross_ref[...] = jnp.where(
        low, jnp.broadcast_to(lse_cross[:tok], spread), jnp.broadcast_to(lse_cross[tok:], spread)
    )

    @pl.when(step == 0)
    def _():
        table_ref[...] = jnp.zeros(table_ref.shape, f32)

    table = put_row(table_ref[...], 2 * step, as_row(lse_self[:tok]))
    table = put_row(table, 2 * step + 1, as_row(lse_self[tok:]))
    table_ref[...] = table

    @pl.when(step == pl.num_programs(0) - 1)
    def _():
        split_ref[...] = split_three(table_ref[...])


def mixed_back_kernel(tok, d_attn_ref, w_ref, self_ref, cross_ref, gate_ref, lse_ref, pack_ref, d_cross_ref, d_gate_ref, acc_ref):
    step = pl.program_id(0)

    @pl.when(step == 0)
    def _():
        acc_ref[...] = jnp.zeros(acc_ref.shape, f32)

    add_transposed(acc_ref, d_attn_ref, w_ref)

    @pl.when(step == pl.num_programs(0) - 1)
    def _():
        rows = []
        for at in range(0, acc_ref.shape[1], LANES):
            part = slice(at, at + LANES)
            d_mixed = acc_ref[:, part]
            d_self = d_mixed.astype(bf16)
            d_cross_ref[:, part] = (gate_ref[:, part] * d_mixed).astype(bf16)
            d_gate_ref[:, part] = jnp.sum(d_mixed * cross_ref[:, part], axis=0, keepdims=True)
            delta = head_sum(d_self.astype(f32) * self_ref[:, part])
            rows += [as_row(delta[:, :1]), as_row(delta[:, HD : HD + 1])]
            pack_ref[0, :tok, part] = d_self
        rows += [jnp.zeros_like(rows[0])] * (TABLE - len(rows))
        pack_ref[0, tok : tok + TABLE, :] = split_three(jnp.concatenate(rows, axis=0))
        pack_ref[0, tok + TABLE :, :] = lse_ref[...]


def query_back_kernel(
    counts, tok, flag_ref, q_ref, own_ids_ref, ids_ref, tk_ref, tv_ref, d_self_ref, d_cross_ref,
    self_ref, cross_ref, lse_self_ref, lse_cross_ref, raw_ref, gain_ref, cos_ref, sin_ref, *rest
):
    pieces = piece_views(rest[: len(counts)], counts, 3)
    d_raw_ref, d_gain_ref, d_tk_ref, d_tv_ref, acc_ref = rest[len(counts) :]
    own_ids = own_ids_ref[...]
    own_two = jnp.concatenate([own_ids, own_ids], axis=0)
    q_two = two_heads(q_ref[0])
    d_self = d_self_ref[0]
    d_self_two = two_heads(d_self)
    delta = columns_of(head_sum(d_self.astype(f32) * self_ref[...]))
    lse = columns_of(lse_self_ref[...])

    d_cross = d_cross_ref[...]
    d_cross_two = two_heads(d_cross)
    delta_cross = columns_of(head_sum(d_cross.astype(f32) * cross_ref[...]))
    lse_cross = columns_of(lse_cross_ref[...])
    cross_p = jnp.exp(mm(q_two, tk_ref[...], 1, 1) - lse_cross)
    d_cross_p = mm(d_cross_two, tv_ref[...], 1, 1)
    d_cross_s = (cross_p * (d_cross_p - delta_cross)).astype(bf16)
    d_tv_ref[...] = mm(cross_p.astype(bf16), d_cross_two, 0, 0)
    d_tk_ref[...] = mm(d_cross_s, q_two, 0, 0)
    acc_ref[...] = mm(d_cross_s, tk_ref[...], 1, 0)
    for slot, (ref, at) in enumerate(pieces):
        rows = ref.shape[1]

        @pl.when(flag_ref[slot] > 0)
        def _(slot=slot, ref=ref, at=at, rows=rows):
            key = ref[at + 1]
            scores = mm(q_two, key, 1, 1)
            scores = jnp.where(own_two == ids_ref[slot : slot + 1, :rows], scores, MASKED)
            weights = jnp.exp(scores - lse)
            d_weights = mm(d_self_two, ref[at + 2], 1, 1)
            d_scores = (weights * (d_weights - delta)).astype(bf16)
            acc_ref[...] += mm(d_scores, key, 1, 0)

    d_query = one_pair(acc_ref[...]) * (HD**-0.5)
    d_raw, d_gain = norm_rope_back(raw_ref[0], gain_ref[...], cos_ref[...], sin_ref[...], d_query)
    d_raw_ref[...] = d_raw.astype(bf16)
    d_gain_ref[...] = d_gain


def key_back_kernel(counts, tok, flag_ref, k_ref, v_ref, own_ids_ref, ids_ref, raw_ref, gain_ref, cos_ref, sin_ref, *rest):
    n = len(counts)
    q_views = piece_views(rest[:n], counts, 3)
    g_views = piece_views(rest[n : 2 * n], counts, 1)
    g_tables = piece_views(rest[2 * n : 3 * n], counts, 1)
    d_both_ref, d_gain_ref, acc_k_ref, acc_v_ref = rest[3 * n :]
    step = pl.program_id(0)
    own_ids = own_ids_ref[...]
    k_two = two_heads(k_ref[0])
    v_two = two_heads(v_ref[0])
    acc_k_ref[...] = jnp.zeros(acc_k_ref.shape, f32)
    acc_v_ref[...] = jnp.zeros(acc_v_ref.shape, f32)
    for slot in range(PIECES):
        q_ref, q_at = q_views[slot]
        g_ref, at = g_views[slot]
        rows = q_ref.shape[1]
        @pl.when(flag_ref[slot] > 0)
        def _(slot=slot, q_ref=q_ref, q_at=q_at, g_ref=g_ref, at=at, rows=rows):
            query = q_ref[q_at]
            d_self = g_ref[at]
            tables = joined(g_tables[slot][0][at], tok)[:, :rows]
            delta, lse = tables[:TABLE], tables[TABLE:]
            same = own_ids == ids_ref[slot : slot + 1, :rows]
            scores = mm(k_two, query, 1, 1)
            d_weights = mm(v_two, d_self, 1, 1)
            p_low, d_low = [], []
            for head in range(2):
                part = slice(head * tok, (head + 1) * tok)
                masked = jnp.where(same, scores[part], MASKED)
                weights = jnp.exp(masked - take_row(lse, 2 * step + head))
                p_low.append(weights.astype(bf16))
                d_low.append((weights * (d_weights[part] - take_row(delta, 2 * step + head))).astype(bf16))
            acc_v_ref[...] += mm(jnp.concatenate(p_low, axis=0), d_self, 1, 0)
            acc_k_ref[...] += mm(jnp.concatenate(d_low, axis=0), query, 1, 0)

    d_raw, d_gain = norm_rope_back(
        raw_ref[0], gain_ref[...], cos_ref[...], sin_ref[...], one_pair(acc_k_ref[...])
    )
    d_gain_ref[...] = d_gain
    place = pl.multiple_of(step * LANES, LANES)
    d_both_ref[:, pl.ds(place, LANES)] = d_raw.astype(bf16)
    half = pl.num_programs(0) * LANES
    d_both_ref[:, pl.ds(pl.multiple_of(half + place, LANES), LANES)] = one_pair(acc_v_ref[...]).astype(bf16)


def place_rows(lines_ref, start, table, out_ref, top=None):
    rows, columns = table
    per_row = columns // LANES
    for at in range(per_row):
        part = lines_ref[pl.ds(start + at, rows, stride=per_row), :].astype(bf16)
        if top is None:
            out_ref[:, at * LANES : (at + 1) * LANES] = part
        else:
            row, lane = top + at // (WIDE // LANES) * rows, at % (WIDE // LANES) * LANES
            out_ref[row : row + rows, lane : lane + LANES] = part


def own_rows_kernel(tables, starts, packed, apart, lines_ref, *out_refs):
    top = 0
    for which in packed:
        rows, columns = tables[which]
        place_rows(lines_ref, starts[which], tables[which], out_refs[0], top)
        top += columns // WIDE * rows
    for which, ref in zip(apart, out_refs[bool(packed) :]):
        place_rows(lines_ref, starts[which], tables[which], ref)


def flatten_kernel(places, *refs):
    *in_refs, lines_ref = refs
    for (start, column, columns), ref in zip(places, in_refs):
        for at in range(ref.shape[1] // LANES):
            part = ref[:, at * LANES : (at + 1) * LANES].astype(f32)
            lines_ref[pl.ds(start + column // LANES + at, ref.shape[0], stride=columns // LANES), :] = part


def update_kernel(clip_ref, g_ref, one_ref, two_ref, w_ref, avg_ref, one_out, two_out, w_out, avg_out, low_out):
    one, two, weight, moving = adam_update(
        g_ref[...] * clip_ref[0], one_ref[...], two_ref[...], w_ref[...], avg_ref[...], RATE_MATRIX, DECAY_WEIGHT
    )
    one_out[...] = one
    two_out[...] = two
    w_out[...] = weight
    avg_out[...] = moving
    low_out[...] = weight.astype(bf16)


def adam_update(gradient, first_moment, second_moment, weight, moving, rate, decay):
    first_new = BETA_ONE * first_moment + (1.0 - BETA_ONE) * gradient
    second_new = BETA_TWO * second_moment + (1.0 - BETA_TWO) * gradient * gradient
    corr_one = 1.0 - BETA_ONE**STEP
    corr_two = 1.0 - BETA_TWO**STEP
    step_dir = first_new / corr_one / (jnp.sqrt(second_new / corr_two) + ADAM_EPS)
    weight_new = weight - rate * (step_dir + decay * weight)
    moving_new = EMA_DECAY * moving + (1.0 - EMA_DECAY) * weight_new
    return (first_new, second_new, weight_new, moving_new)


def call(kernel, grid, in_specs, out_specs, out_shape, args, scratch=(), prefetch=0, flops=0, moved=0, vmem=58):
    return pl.pallas_call(
        kernel,
        grid_spec=pltpu.PrefetchScalarGridSpec(
            num_scalar_prefetch=prefetch, grid=grid, in_specs=in_specs, out_specs=out_specs, scratch_shapes=scratch
        ),
        out_shape=out_shape,
        compiler_params=pltpu.CompilerParams(dimension_semantics=("arbitrary",) * len(grid), vmem_limit_bytes=vmem * MIB),
        cost_estimate=pl.CostEstimate(flops=flops, bytes_accessed=moved, transcendentals=0),
    )(*args)


def whole(shape):
    return pl.BlockSpec(shape, lambda *_: (0,) * len(shape))


def pair(rows, first=0):
    return pl.BlockSpec((rows, LANES), lambda j, *_: (0, first + j))


def pairs(count, rows, at=0):
    return pl.BlockSpec((count, rows, LANES), lambda j, *_: (at, 0, j))


def shape_of(shape, dtype):
    return jax.ShapeDtypeStruct(shape, dtype)


def shifted(x, by):
    count = lax.axis_size("img")
    return lax.ppermute(x, "img", [(i + by, i) for i in range(count) if 0 <= i + by < count])


def crossed(x, bit):
    count = lax.axis_size("img")
    return lax.ppermute(x, "img", [(i, i ^ bit) for i in range(count)])


def other_txt(x):
    return lax.ppermute(x, "txt", [(0, 1), (1, 0)])


def index_bits(count):
    bits = count.bit_length() - 1
    assert count == 1 << bits
    return bits


def sum_over_img(x):
    for bit in range(index_bits(lax.axis_size("img"))):
        x = x + crossed(x, 1 << bit)
    return x


def few_over_img(x):
    bits = index_bits(lax.axis_size("img"))
    for bit in range(0, bits - 1, 2):
        low, high = 1 << bit, 2 << bit
        x = (x + crossed(x, low)) + (crossed(x, high) + crossed(x, low | high))
    if bits % 2:
        x = x + crossed(x, 1 << (bits - 1))
    return x


def own_and_other(x, bit, below=1):
    mine = (lax.axis_index("img") >> bit) & 1
    split = x.reshape(x.shape[0] // (2 * below), 2, below, *x.shape[1:])
    own = lax.dynamic_index_in_dim(split, mine, 1, keepdims=False)
    other = lax.dynamic_index_in_dim(split, 1 - mine, 1, keepdims=False)
    return own.reshape(-1, *x.shape[1:]), other.reshape(-1, *x.shape[1:])


class TermSum:
    def __init__(self, clock, terms, order, sent_as):
        count = lax.axis_size("img")
        self.sent_as = sent_as
        self.clock, self.order, self.level = clock, order, 0
        self.keep = clock.stage(terms).reshape(count, terms.shape[0] // count, terms.shape[1])
        self.send()

    def send(self):
        bit = self.order[self.level]
        below = 1 << sum(other < bit for other in self.order[self.level :])
        self.keep, sent = own_and_other(self.keep, bit, below)
        self.sent = sent.astype(self.sent_as)
        self.clock.mark(self.sent)

    def receive(self):
        self.got = self.clock.stage(crossed(self.sent, 1 << self.order[self.level]))
        self.clock.mark(self.got)

    def advance(self, received=False):
        if not received:
            self.receive()
        self.keep = self.keep + self.clock.stage(self.got).astype(f32)
        self.level += 1
        if self.level == len(self.order):
            self.clock.mark(self.keep)
            return self.keep[0]
        self.send()

    def finish(self):
        while True:
            result = self.advance()
            if result is not None:
                return result


def gather_doubling(x):
    x = x[None]
    for bit in reversed(range(index_bits(lax.axis_size("img")))):
        x = doubled(x, bit)
    return x.reshape(-1, x.shape[-1])


def doubled(x, bit):
    mine = (lax.axis_index("img") >> bit) & 1
    got = crossed(x, 1 << bit)
    both = jnp.where(mine == 0, jnp.stack([x, got], 1), jnp.stack([got, x], 1))
    return both.reshape(-1, *x.shape[1:])


def tie(x, *others):
    return lax.optimization_barrier((x, others))[0]


def tall(left):
    count = lax.axis_size("img")
    return left.T.reshape(count, left.shape[1] // count, left.shape[0])


class Clock:
    def __init__(self):
        self.token = ()
        self.kept = []

    def stage(self, *arrays):
        arrays, passed = lax.optimization_barrier((arrays, self.token))
        self.kept += passed
        return arrays if len(arrays) > 1 else arrays[0]

    def mark(self, *arrays):
        self.token = arrays


class SmallSum:
    def __init__(self, clock, x, row):
        self.x, self.row = clock.stage(x, row)
        self.clock, self.level = clock, 0
        self.levels = index_bits(lax.axis_size("img"))
        self.send()

    def send(self):
        high = lax.reduce_precision(self.row, 8, 7)
        low = lax.reduce_precision(self.row - high, 8, 7)
        self.row = high + low
        self.sent = jnp.concatenate([self.x, high, low], axis=0).astype(bf16)
        self.clock.mark(self.sent)

    def advance(self):
        got = self.clock.stage(crossed(self.sent, 1 << self.level)).astype(f32)
        count = self.x.shape[0]
        self.x = self.x + got[:count]
        self.row = self.row + (got[count : count + 1] + got[count + 1 :])
        self.level += 1
        if self.level < self.levels:
            self.send()
        else:
            self.clock.mark(self.x)


class SmallGather:
    def __init__(self, clock, x):
        x = clock.stage(x)
        self.clock, self.x, self.bit = clock, x[None], index_bits(lax.axis_size("img"))
        clock.mark(x)

    def advance(self):
        self.bit -= 1
        mine = (lax.axis_index("img") >> self.bit) & 1
        got = self.clock.stage(crossed(self.x, 1 << self.bit))
        both = jnp.where(mine == 0, jnp.stack([self.x, got], 1), jnp.stack([got, self.x], 1))
        self.x = both.reshape(-1, *got.shape[1:])
        self.clock.mark(self.x)

    def result(self):
        return self.x.reshape(-1, self.x.shape[-1])


class GradientSum:
    def __init__(self, clock, left, right):
        bits = index_bits(left.shape[0])
        self.order = list(range(bits))
        self.level = 0
        self.clock = clock
        left, self.right = clock.stage(left, right)
        self.own, other = own_and_other(left, 0)
        self.sent = self.terms(other).astype(bf16)
        self.result = None
        clock.mark(self.sent)

    def terms(self, chunks):
        product = mm(chunks.reshape(-1, chunks.shape[2]), self.right, 1, 0)
        return product.reshape(chunks.shape[0], chunks.shape[1], self.right.shape[1])

    def receive(self):
        self.got = self.clock.stage(crossed(self.sent, 1 << self.order[self.level]))
        self.clock.mark(self.got)
        self.level += 1

    def advance(self, received=False, beside=None):
        if beside is not None:
            self.got, *beside = self.clock.stage(crossed(self.sent, 1 << self.order[self.level]), *beside)
            self.clock.mark(self.got)
            self.level += 1
        elif not received:
            self.receive()
        got = self.clock.stage(self.got)
        if self.level == len(self.order):
            self.result = (self.keep + got.astype(f32))[0]
            return self.result
        bit = self.order[self.level]
        if self.level == 1:
            own, other = own_and_other(self.own, bit)
            got_own, got_other = own_and_other(got, bit)
            self.sent = (self.terms(other) + got_other.astype(f32)).astype(bf16)
            self.keep = self.terms(own) + got_own.astype(f32)
        else:
            own, other = own_and_other(self.keep + got.astype(f32), bit)
            self.sent, self.keep = other.astype(bf16), own
        self.clock.mark(self.sent)
        return beside


class Neighbourhood:
    def __init__(self, clock, x, end, beginning):
        count = lax.axis_size("img")
        self.clock = clock
        self.x = x
        self.across = crossed(x, 2)
        self.above, self.below = shifted(x, 4), shifted(x, -4)
        edge = jnp.where(lax.axis_index("img") % 4 == 3, end, beginning)
        pairs_low = [(i - 5, i) for i in range(0, count, 4) if i >= 5]
        pairs_high = [(i + 5, i) for i in range(3, count, 4) if i + 5 < count]
        self.edge = lax.ppermute(edge, "img", pairs_low + pairs_high)

    def second(self):
        across, above, below, self.edge = self.clock.stage(self.across, self.above, self.below, self.edge)
        self.across, self.above, self.below = across, above, below
        self.four_sent = jnp.concatenate([self.x, across, above, below], axis=0)
        self.above_across, self.below_across = shifted(across, 4), shifted(across, -4)
        self.clock.mark(self.four_sent)

    def third(self):
        four = crossed(self.four_sent, 1)
        self.above_across, self.below_across, self.four = self.clock.stage(self.above_across, self.below_across, four)
        self.two_sent = jnp.concatenate([self.above_across, self.below_across], axis=0)
        self.clock.mark(self.two_sent)

    def collect(self):
        two = self.clock.stage(crossed(self.two_sent, 1))
        self.clock.mark(two)
        return [self.x, self.across, self.above, self.below, self.four, self.above_across, self.below_across, two, self.edge]


PIECE_COUNTS = (1, 1, 1, 1, 4, 1, 1, 2, 1)


def neighbour_indices(i):
    b = i ^ 1
    edge = jnp.where(i % 4 == 0, i - 5, i + 5)
    return [i, i ^ 2, i + 4, i - 4, b, b ^ 2, b + 4, b - 4, (i ^ 2) + 4, (i ^ 2) - 4, (b ^ 2) + 4, (b ^ 2) - 4, edge]


def token_places(row_index, image_sides):
    heights = image_sides[:, 0]
    widths = image_sides[:, 1]
    lengths = heights * (widths + 1)
    sample_ends = jnp.cumsum(lengths, dtype=jnp.int32)
    starts = sample_ends - lengths
    sample_ids = ids_of(row_index, sample_ends)
    matched = jnp.arange(image_sides.shape[0], dtype=jnp.int32)[None, :] == sample_ids[:, None]
    first_row = jnp.sum(jnp.where(matched, starts[None, :], 0), axis=1, dtype=jnp.int32)
    row_width = jnp.sum(jnp.where(matched, widths[None, :] + 1, 0), axis=1, dtype=jnp.int32)
    row_width = jnp.maximum(row_width, 1)
    offset = row_index - first_row
    return (sample_ids, offset // row_width, offset % row_width, sample_ends)


def ids_of(rows, sample_ends):
    return jnp.sum((sample_ends <= rows[..., None]).astype(jnp.int32), axis=-1, dtype=jnp.int32)


def turn_tables(row_pos, col_pos):
    quarter = HD // 4
    frequency = 10000.0 ** (-jnp.arange(quarter, dtype=f32) / quarter)
    angles = jnp.concatenate(
        [row_pos.astype(f32)[:, None] * frequency[None, :], col_pos.astype(f32)[:, None] * frequency[None, :]], axis=1
    )
    cosine, sine = jnp.cos(angles), jnp.sin(angles)
    return jnp.concatenate([cosine] * 4, axis=1), jnp.concatenate([-sine, sine, -sine, sine], axis=1)


def rms_norm(values):
    return values * lax.rsqrt(jnp.mean(values * values, axis=-1, keepdims=True) + EPS_NORM)


def rms_back(values, d_normed):
    inverse = lax.rsqrt(jnp.mean(values * values, axis=-1, keepdims=True) + EPS_NORM)
    normed = values * inverse
    return inverse * (d_normed - normed * jnp.mean(d_normed * normed, axis=-1, keepdims=True))


def on_device(
    tokens, cotangent, text_states, conditions, image_sides, master, moment_one, moment_two, average,
    small_master, small_one, small_two, small_average,
):
    n_img = lax.axis_size("img")
    n_txt = lax.axis_size("txt")
    img_index = lax.axis_index("img")
    txt_index = lax.axis_index("txt")
    tok = tokens.shape[0]
    samples = image_sides.shape[0]
    half_d = D // n_txt
    half_ff = FF // n_txt
    local_heads = half_d // HD
    n_pairs = half_d // LANES

    tables = [
        (D // n_img, 2 * half_ff),
        (half_ff // n_img, D),
        (D // n_img, 3 * half_d),
        (TXT_D // n_img, 2 * half_d),
        (half_d // n_img, D),
        (COND // n_img, 6 * half_d),
    ]
    master_lines = master.reshape(-1, LANES)
    lines = master_lines.shape[0]
    starts = [0]
    for rows, columns in tables:
        starts.append(starts[-1] + rows * columns // LANES)

    def scatter(terms):
        return lax.psum_scatter(terms, "img", scatter_dimension=0, tiled=True)

    def gather(rows):
        return lax.all_gather(rows, "img", axis=0, tiled=True)

    together = [0, 1, 4, 2]
    shapes = [tables[w] for w in together]
    heights = [rows * columns // WIDE for rows, columns in shapes]
    in_blocks = all(rows % 16 == 0 for rows, _ in shapes)
    packed = together if in_blocks else []
    apart = [5, 3] if in_blocks else [5, 3] + together
    own = pl.pallas_call(
        functools.partial(own_rows_kernel, tables, starts, packed, apart),
        out_shape=[shape_of((sum(heights), WIDE), bf16)] * in_blocks + [shape_of(tables[w], bf16) for w in apart],
        compiler_params=pltpu.CompilerParams(vmem_limit_bytes=58 * MIB),
    )(master_lines)
    own_modulate, own_text = own[in_blocks : in_blocks + 2]
    if in_blocks:
        blocks = gather(own[0][None])
    else:
        blocks = None
        natural = dict(zip(together, (gather(rows) for rows in own[2:])))

    def weight(which):
        if blocks is None:
            array = natural[which]
            return array, lambda at, group=1: pl.BlockSpec((array.shape[0], group * WIDE), lambda j, *_: (0, at(j)))
        place = together.index(which)
        rows = shapes[place][0]
        first = sum(heights[:place]) // rows
        assert first * rows == sum(heights[:place])

        def spec(at, group=1):
            assert first % group == 0
            return pl.BlockSpec((n_img, group * rows, WIDE), lambda j, *_: (0, first // group + at(j), 0))

        return blocks, spec


    gain_attn = small_master[:D]
    gain_ffn = small_master[D : 2 * D]
    gain_query = small_master[2 * D : 2 * D + HD]
    gain_key = small_master[2 * D + HD : 2 * D + 2 * HD]
    gain_text = small_master[2 * D + 2 * HD : 2 * D + 3 * HD]
    gate_heads = small_master[2 * D + 3 * HD :]
    gate_local = lax.dynamic_slice_in_dim(gate_heads, txt_index * local_heads, local_heads)
    tanh_gate = jnp.tanh(gate_local)
    gate_lanes = jnp.repeat(tanh_gate, HD)[None, :]
    gain_query_pair = jnp.tile(gain_query, 2)[None, :]
    gain_key_pair = jnp.tile(gain_key, 2)[None, :]

    cond_rows = COND // n_img
    cond_own = lax.dynamic_slice_in_dim(conditions, img_index * cond_rows, cond_rows, 1)
    silu_own = jax.nn.silu(cond_own.astype(f32)).astype(bf16)
    z_first = [0] + list(range(2, index_bits(n_img))) + [1]
    mod_width = 6 * half_d // n_img
    mod_terms = jnp.dot(silu_own, own_modulate, preferred_element_type=f32)
    mod_terms = mod_terms.reshape(samples, n_img, mod_width).transpose(1, 0, 2).reshape(-1, mod_width)
    mod_own = TermSum(Clock(), mod_terms, z_first, f32).finish().astype(bf16)
    mod_half = gather_doubling(mod_own).reshape(n_img, samples, mod_width).transpose(1, 0, 2)
    mod_half = mod_half.reshape(samples, 6 * half_d)
    mod_other = other_txt(mod_half)
    mods = jnp.where(
        txt_index == 0, jnp.stack([mod_half, mod_other], 0), jnp.stack([mod_other, mod_half], 0)
    ).reshape(n_txt, samples, 6, half_d).transpose(1, 2, 0, 3)

    row_index = img_index * tok + jnp.arange(tok, dtype=jnp.int32)
    sample_ids, row_pos, col_pos, sample_ends = token_places(row_index, image_sides)
    cosine, sine = turn_tables(row_pos, col_pos)
    one_hot = sample_ids[:, None] == jnp.arange(samples, dtype=jnp.int32)[None, :]
    per_token = jnp.dot(one_hot.astype(bf16), mods.reshape(samples, 6 * D), preferred_element_type=f32).astype(bf16)
    shift_one, scale_one, gate_one, shift_two, scale_two, gate_two = (
        per_token[:, c * D : (c + 1) * D].astype(f32) for c in range(6)
    )

    pieces = jnp.stack([jnp.asarray(p, jnp.int32) for p in neighbour_indices(img_index)])
    place = img_index % 4
    inside = (pieces >= 0) & (pieces < n_img)
    slots = jnp.arange(PIECES)
    inside &= (slots != PIECES - 1) | (place == 0) | (place == 3)
    column = jnp.arange(tok, dtype=jnp.int32)[None, :]
    edge_start = jnp.where((slots == PIECES - 1) & (place == 0), tok - EDGE, 0)
    piece_rows = pieces[:, None] * tok + column + edge_start[:, None]
    there = inside[:, None] & ((slots[:, None] < PIECES - 1) | (column < EDGE))
    piece_ids = jnp.where(there, ids_of(piece_rows, sample_ends), -1)
    flags = jnp.any((piece_ids >= sample_ids[0]) & (piece_ids <= sample_ids[-1]), axis=1).astype(jnp.int32)
    piece_ids = jnp.concatenate([piece_ids, jnp.full((16 - PIECES, tok), -1, jnp.int32)], axis=0)
    own_ids = sample_ids[:, None]

    text_rows = text_states.shape[0]
    text_len = text_rows * n_img
    text_columns = lax.all_to_all(text_states, "img", split_axis=1, concat_axis=0, tiled=True)
    text_proj = TermSum(Clock(), jnp.dot(text_columns, own_text, preferred_element_type=f32), z_first, bf16).finish()
    text_shape = (text_rows, local_heads, HD)
    text_raw = text_proj[:, :half_d].reshape(text_shape)
    text_normed = rms_norm(text_raw)
    text_key_low = (text_normed * gain_text).reshape(text_rows, half_d).astype(bf16)
    text_low = jnp.concatenate([text_key_low, text_proj[:, half_d:].astype(bf16)], axis=1)
    all_text = gather_doubling(text_low)

    if blocks is not None:
        blocks = tie(blocks, all_text, per_token, cosine, sine, flags, piece_ids)
    x_float = tokens.astype(f32)
    x_normed = rms_norm(x_float)
    normed_one = x_normed * gain_attn
    attn_in = (normed_one * (1.0 + scale_one) + shift_one).astype(bf16)
    def wide(rows, group=1):
        return pl.BlockSpec((rows, group * WIDE), lambda j, *_: (0, j))

    thirds = half_d // WIDE
    w_project, project_spec = weight(2)
    own_qkv, raw_qk = call(
        project_kernel,
        (thirds,),
        [whole((tok, D))]
        + [project_spec(lambda j, c=c: c * thirds + j) for c in range(3)]
        + [whole((1, LANES))] * 2
        + [whole((tok, LANES))] * 2,
        [pl.BlockSpec((n, tok, WIDE), lambda j: (0, 0, j)) for n in (3, 2)],
        [shape_of((3, tok, half_d), bf16), shape_of((2, tok, half_d), f32)],
        (attn_in, w_project, w_project, w_project, gain_query_pair, gain_key_pair, cosine, sine),
        flops=2 * tok * D * 3 * half_d,
        moved=2 * D * 3 * half_d,
    )
    clock = Clock()
    clock.mark(own_qkv)
    qkv_near = Neighbourhood(clock, own_qkv, own_qkv[:, tok - EDGE :], own_qkv[:, :EDGE])
    w_updown, updown_spec = weight(0)
    w_down, down_spec = weight(1)
    w_output, output_spec = weight(4)
    def step(j):
        return j

    qkv_near.second()
    qkv_near.third()
    qkv_pieces = qkv_near.collect()

    qkv_specs = [pairs(3 * c, a.shape[1]) for c, a in zip(PIECE_COUNTS, qkv_pieces)]
    id_specs = [whole((tok, 1)), whole((16, tok))]
    text_specs = [pair(text_len), pair(text_len, n_pairs)]
    mixed_low, self_out, cross_out, lse_self, lse_cross, lse_split = call(
        functools.partial(attend_kernel, PIECE_COUNTS, tok),
        (n_pairs,),
        [pairs(1, tok)] + id_specs + text_specs + [pair(1)] + qkv_specs,
        [pair(tok)] * 5 + [whole((TABLE, 3 * tok))],
        [shape_of((tok, half_d), bf16)]
        + [shape_of((tok, half_d), f32)] * 4
        + [shape_of((TABLE, 3 * tok), bf16)],
        (flags, clock.stage(own_qkv), own_ids, piece_ids, all_text, all_text, gate_lanes, *qkv_pieces),
        scratch=[
            pltpu.VMEM((PIECES, 2 * tok, tok), f32),
            pltpu.VMEM((2 * tok, LANES), f32),
            pltpu.VMEM((2 * tok, LANES), f32),
            pltpu.VMEM((2 * tok, LANES), f32),
            pltpu.VMEM((TABLE, tok), f32),
        ],
        prefetch=1,
    )

    def pack_edges(pack):
        table = pack[:, tok:]
        ending = jnp.concatenate(
            [table[:, :, part * tok + tok - EDGE : (part + 1) * tok] for part in range(3) for _ in range(tok // EDGE)],
            axis=2,
        )
        return (
            jnp.concatenate([pack[:, tok - EDGE : tok], ending], axis=1),
            jnp.concatenate([pack[:, :EDGE], table], axis=1),
        )

    clock.mark(mixed_low)
    attn_part = call(
        times_kernel,
        (D // WIDE,),
        [whole((tok, half_d)), output_spec(step)],
        [wide(tok)],
        [shape_of((tok, D), bf16)],
        (clock.stage(mixed_low), w_output),
        flops=2 * tok * half_d * D,
        moved=2 * half_d * D,
    )[0]
    clock.mark(attn_part)
    attn_other = clock.stage(other_txt(attn_part))
    attn_out = attn_part.astype(f32) + attn_other.astype(f32)
    hidden = x_float + gate_one * attn_out
    h_normed = rms_norm(hidden)
    normed_two = h_normed * gain_ffn
    ffn_in = (normed_two * (1.0 + scale_two) + shift_two).astype(bf16)
    clock.mark(ffn_in)
    gate, up, hidden_units, hidden_turned = call(
        hidden_kernel,
        (half_ff // WIDE,),
        [whole((tok, D)), updown_spec(step), updown_spec(lambda j: half_ff // WIDE + j)],
        [wide(tok)] * 3 + [pl.BlockSpec((WIDE, tok), lambda j: (j, 0))],
        [shape_of((tok, half_ff), f32)] * 2 + [shape_of((tok, half_ff), bf16), shape_of((half_ff, tok), bf16)],
        (clock.stage(ffn_in), w_updown, w_updown),
        flops=4 * tok * D * half_ff,
        moved=4 * D * half_ff,
    )
    clock.mark(hidden_turned)
    d_out = cotangent.astype(f32)
    d_branch = (d_out * gate_two).astype(bf16)
    down_terms = mm(clock.stage(hidden_turned), d_branch, 1, 0).astype(bf16)
    clock.mark(down_terms)
    grad_down = scatter(down_terms)
    d_gate_up = call(
        hidden_back_kernel,
        (D // WIDE // 3,),
        [wide(tok, 3), down_spec(step, 3), whole((tok, half_ff)), whole((tok, half_ff))],
        [whole((tok, 2 * half_ff))],
        [shape_of((tok, 2 * half_ff), bf16)],
        (clock.stage(d_branch), w_down, gate, up),
        scratch=[pltpu.VMEM((tok, half_ff), f32)],
        flops=2 * tok * D * half_ff,
        moved=2 * D * half_ff,
    )[0]
    clock.mark(d_gate_up)
    d_gate_up = clock.stage(d_gate_up)
    d_ffn_part = call(
        times_transposed_kernel,
        (2 * half_ff // WIDE // 4,),
        [wide(tok, 4), updown_spec(step, 4)],
        [whole((tok, D))],
        [shape_of((tok, D), bf16)],
        (d_gate_up, w_updown),
        scratch=[pltpu.VMEM((tok, D), f32)],
        flops=4 * tok * D * half_ff,
        moved=4 * D * half_ff,
    )[0]
    clock.mark(d_ffn_part)
    d_ffn_other = other_txt(d_ffn_part)
    updown_terms = mm(clock.stage(ffn_in), d_gate_up, 0, 0).astype(bf16)
    clock.mark(updown_terms)
    grad_updown = scatter(updown_terms)
    d_ffn_part, d_ffn_other = clock.stage(d_ffn_part, d_ffn_other)
    d_ffn_in = d_ffn_part.astype(f32) + d_ffn_other.astype(f32)
    d_scale_two = d_ffn_in * normed_two
    d_normed_two = d_ffn_in * (1.0 + scale_two)
    d_gain_ffn = jnp.sum(d_normed_two * h_normed, axis=0)
    d_hidden = d_out + rms_back(hidden, d_normed_two * gain_ffn)
    d_attn = (d_hidden * gate_one).astype(bf16)
    clock.mark(d_attn)
    grad_pack, d_cross_low, d_gate_lanes = call(
        functools.partial(mixed_back_kernel, tok),
        (D // WIDE // 3,),
        [wide(tok, 3), output_spec(step, 3), whole((tok, half_d)), whole((tok, half_d)), whole((1, half_d)), whole((TABLE, 3 * tok))],
        [whole((1, tok + PACK, half_d)), whole((tok, half_d)), whole((1, half_d))],
        [
            shape_of((1, tok + PACK, half_d), bf16),
            shape_of((tok, half_d), bf16),
            shape_of((1, half_d), f32),
        ],
        (clock.stage(d_attn), w_output, self_out, cross_out, gate_lanes, lse_split),
        scratch=[pltpu.VMEM((tok, half_d), f32)],
        flops=2 * tok * D * half_d,
        moved=2 * D * half_d,
    )
    clock.mark(grad_pack)
    grad_near = Neighbourhood(clock, grad_pack, *pack_edges(grad_pack))
    branch_part = call(
        times_kernel,
        (D // WIDE,),
        [whole((tok, half_ff)), down_spec(step)],
        [wide(tok)],
        [shape_of((tok, D), f32)],
        (clock.stage(hidden_units), w_down),
        flops=2 * tok * D * half_ff,
        moved=2 * D * half_ff,
    )[0]
    clock.mark(branch_part)
    branch_other = other_txt(branch_part)
    grad_near.second()
    turn_specs = [whole((1, LANES)), whole((tok, LANES)), whole((tok, LANES))]

    def query_back(first, count, d_cross):
        def at(rows, also=0):
            return pair(rows, first + also)

        def some(arrays, rows, index=0):
            return pl.BlockSpec((arrays, rows, LANES), lambda j, *_: (index, 0, first + j))

        return call(
            functools.partial(query_back_kernel, PIECE_COUNTS, tok),
            (count,),
            [some(1, tok)]
            + id_specs
            + [at(text_len), at(text_len, n_pairs)]
            + [some(1, tok), at(tok)]
            + [at(tok)] * 4
            + [some(1, tok)]
            + turn_specs
            + [some(3 * c, a.shape[1]) for c, a in zip(PIECE_COUNTS, qkv_pieces)],
            [pair(tok), pair(1), pair(text_len), pair(text_len)],
            [
                shape_of((tok, count * LANES), bf16),
                shape_of((1, count * LANES), f32),
                shape_of((text_len, count * LANES), f32),
                shape_of((text_len, count * LANES), f32),
            ],
            (
                flags, own_qkv, own_ids, piece_ids, all_text, all_text, grad_pack, d_cross,
                self_out, cross_out, lse_self, lse_cross, raw_qk, gain_query_pair, cosine, sine, *qkv_pieces,
            ),
            scratch=[pltpu.VMEM((2 * tok, LANES), f32)],
            prefetch=1,
        )

    head_half = n_pairs // 2
    first_half = query_back(0, head_half, clock.stage(d_cross_low))
    clock.mark(first_half[0])
    grad_near.third()
    output_sum = GradientSum(clock, tall(mixed_low), d_attn)
    grad_pieces = grad_near.collect()
    output_sum.advance()
    second_half = query_back(head_half, n_pairs - head_half, clock.stage(d_cross_low))
    clock.mark(second_half[0])
    grad_down, branch_other = clock.stage(grad_down, branch_other)
    clock.mark(grad_down, branch_other)
    d_query_raw, d_gain_query, d_text_key, d_text_value = (
        jnp.concatenate(halves, axis=1) for halves in zip(first_half, second_half)
    )
    attn_tall = tall(attn_in)
    text_sum = TermSum(clock, jnp.concatenate([d_text_key, d_text_value], axis=1), z_first, bf16)
    query_sum = GradientSum(clock, attn_tall, d_query_raw)
    text_sum.advance()
    query_sum.advance()

    pack_specs = [pairs(c, a.shape[1] - PACK) for c, a in zip(PIECE_COUNTS, grad_pieces)] + [
        pl.BlockSpec((c, PACK, half_d), lambda j, *_, at=(a.shape[1] - PACK) // PACK: (0, at, 0))
        for c, a in zip(PIECE_COUNTS, grad_pieces)
    ]

    d_key_value, d_gain_key = call(
        functools.partial(key_back_kernel, PIECE_COUNTS, tok),
        (n_pairs,),
        [pairs(1, tok, 1), pairs(1, tok, 2)]
        + id_specs
        + [pairs(1, tok, 1)]
        + turn_specs
        + qkv_specs
        + pack_specs,
        [whole((tok, 2 * half_d)), pair(1)],
        [shape_of((tok, 2 * half_d), bf16), shape_of((1, half_d), f32)],
        (
            flags, clock.stage(own_qkv), own_qkv, own_ids, piece_ids, raw_qk, gain_key_pair,
            cosine, sine, *qkv_pieces, *grad_pieces, *grad_pieces,
        ),
        scratch=[pltpu.VMEM((2 * tok, LANES), f32)] * 2,
        prefetch=1,
    )
    clock.mark(d_key_value)
    key_value_sum = GradientSum(clock, attn_tall, d_key_value)
    d_key_value = clock.stage(d_key_value)
    d_attn_part = call(
        input_back_kernel,
        (3,),
        [whole((tok, half_d)), whole((tok, 2 * half_d)), project_spec(step, thirds)],
        [whole((tok, D))],
        [shape_of((tok, D), bf16)],
        (d_query_raw, d_key_value, w_project),
        scratch=[pltpu.VMEM((tok, D), f32)],
        flops=6 * tok * D * half_d,
        moved=6 * D * half_d,
    )[0]
    clock.mark(d_attn_part)
    d_attn_other = other_txt(d_attn_part)
    key_value_sum.advance()
    text_sum.advance()
    output_sum.advance()

    one_hot_wide = one_hot.astype(f32)

    def by_sample(values):
        summed = lax.dot_general(one_hot_wide, values, (((0,), (0,)), ((), ())), precision=HIGH)
        return lax.dynamic_slice_in_dim(summed, txt_index * half_d, half_d, 1)

    d_hidden_late, d_ffn_late = clock.stage(d_hidden, d_ffn_in)
    branch = branch_part + branch_other
    block_out = hidden + gate_two * branch
    d_mod_early = jnp.concatenate(
        [
            by_sample(v)
            for v in (d_hidden_late * attn_out, d_ffn_late, d_ffn_late * normed_two, d_out * branch)
        ],
        axis=1,
    )
    clock.mark(d_mod_early)
    text_own = text_sum.finish()
    d_text_scaled = text_own[:, :half_d].reshape(text_shape)
    d_gain_text = jnp.sum(d_text_scaled * text_normed, axis=(0, 1))
    d_text_raw = rms_back(text_raw, d_text_scaled * gain_text).reshape(text_rows, half_d)
    text_gather = SmallGather(clock, jnp.concatenate([d_text_raw, text_own[:, half_d:]], axis=1).astype(bf16))
    d_attn_other = clock.stage(d_attn_other)
    d_attn_in = d_attn_part.astype(f32) + d_attn_other.astype(f32)
    d_scale_one = d_attn_in * normed_one
    d_normed_one = d_attn_in * (1.0 + scale_one)
    d_gain_attn = jnp.sum(d_normed_one * x_normed, axis=0)
    d_tokens = d_hidden + rms_back(x_float, d_normed_one * gain_attn)
    d_mod = jnp.concatenate([by_sample(d_attn_in), by_sample(d_scale_one), d_mod_early], axis=1)

    replica = (txt_index == 0).astype(f32)
    d_gate_local = jnp.sum(d_gate_lanes.reshape(local_heads, HD), axis=1) * (1.0 - tanh_gate**2)
    gate_full = lax.dynamic_update_slice(jnp.zeros((HEADS,), f32), d_gate_local, (txt_index * local_heads,))
    small_terms = jnp.concatenate(
        [
            d_gain_attn * replica,
            d_gain_ffn * replica,
            jnp.sum(d_gain_query.reshape(local_heads, HD), axis=0),
            jnp.sum(d_gain_key.reshape(local_heads, HD), axis=0),
            jnp.zeros((HD,), f32),
            gate_full,
        ]
    )
    small_count = small_terms.shape[0]
    small_row = jnp.pad(small_terms, (0, d_mod.shape[1] - small_count))[None]
    small_sum = SmallSum(clock, d_mod, small_row)
    output_sum.advance()
    query_sum.advance()
    text_gather.advance()
    (grad_updown,) = key_value_sum.advance(beside=(grad_updown,))
    small_sum.advance()
    small_sum.advance()
    query_sum.advance()
    key_value_sum.advance()
    small_sum.advance()
    text_gather.advance()
    output_sum.advance()
    text_gather.advance()
    query_sum.advance()
    small_sum.advance()
    key_value_sum.advance()
    while text_gather.bit:
        text_gather.advance()
    grad_text = mm(text_columns, text_gather.result(), 0, 0)
    pending = [one for one in (output_sum, query_sum, key_value_sum) if one.result is None]
    while pending or small_sum.level < small_sum.levels:
        if small_sum.level < small_sum.levels:
            small_sum.advance()
        for one in list(pending):
            if one.result is None:
                one.advance()
            if one.result is not None:
                pending.remove(one)
    d_mod, small_row = small_sum.x, small_sum.row
    small_grad = (small_row + other_txt(small_row))[0, :small_count]
    grad_modulate = lax.dot_general(silu_own.astype(f32), d_mod, (((0,), (0,)), ((), ())), precision=HIGH)

    grads = [grad_updown, grad_down, query_sum.result, grad_text, output_sum.result, grad_modulate, key_value_sum.result]
    places = [(start, 0, columns) for start, (_, columns) in zip(starts, tables)]
    places.append((starts[2], half_d, 3 * half_d))
    square = sum(jnp.sum(jnp.square(g.astype(f32))) for g in grads)
    squares = jnp.pad(square.reshape(1, 1), ((0, 0), (0, LANES - 1)))
    reduced = pl.pallas_call(
        functools.partial(flatten_kernel, places),
        out_shape=shape_of((lines, LANES), f32),
        in_specs=[pl.BlockSpec(memory_space=pltpu.VMEM)] * len(grads)
        + [pl.BlockSpec(memory_space=pl.ANY)] * len(clock.kept),
        compiler_params=pltpu.CompilerParams(vmem_limit_bytes=58 * MIB),
    )(*grads, *clock.kept)

    last = few_over_img(jnp.concatenate([squares, jnp.pad(d_gain_text, (0, LANES - HD))[None]], axis=0))
    last, reduced = lax.optimization_barrier((last, reduced))
    last = last + other_txt(last)
    small_grad = lax.dynamic_update_slice(small_grad, last[1, :HD], (2 * D + 2 * HD,))
    grad_square = jnp.sum(last[0]) + jnp.sum(small_grad * small_grad)
    clip_factor = MAX_NORM / jnp.maximum(jnp.sqrt(grad_square), MAX_NORM)

    block = math.gcd(lines, 2048)
    line_spec = pl.BlockSpec((block, LANES), lambda i: (i, 0))
    as_lines = (lines, LANES)
    updated = call(
        update_kernel,
        (lines // block,),
        [pl.BlockSpec(memory_space=pltpu.SMEM)] + [line_spec] * 5,
        [line_spec] * 5,
        [shape_of(as_lines, f32)] * 4 + [shape_of(as_lines, bf16)],
        (clip_factor.reshape(1), reduced, *(a.reshape(as_lines) for a in (moment_one, moment_two, master, average))),
        flops=20 * lines * LANES,
        moved=38 * lines * LANES,
    )
    one_new, two_new, master_new, average_new, master_low = (a.reshape(master.shape) for a in updated)
    small_one_new, small_two_new, small_new, small_average_new = adam_update(
        small_grad * clip_factor, small_one, small_two, small_master, small_average, RATE_SMALL, 0.0
    )
    return (
        block_out,
        d_tokens,
        grad_square,
        one_new,
        two_new,
        master_new,
        average_new,
        master_low,
        small_one_new,
        small_two_new,
        small_new,
        small_average_new,
    )


def solution(mesh):
    rows = P("img", None)
    shards = P("img", "txt", None)
    in_specs = (rows, rows, rows, P(), P(), shards, shards, shards, shards, P(), P(), P(), P())
    out_specs = (rows, rows, P(), shards, shards, shards, shards, shards, P(), P(), P(), P())
    return jax.shard_map(on_device, mesh=mesh, in_specs=in_specs, out_specs=out_specs, check_vma=False)
```
